256 devices in a mesh: dp: 32 (over y, z), tensor: 8 (over x, core).
Axes of the slice: x: 4, y: 4, z: 8, core: 2. Of those that a mesh axis runs over, the one named last changes fastest.
Arguments:
- queries: bfloat16 [16384, 8192], P('dp', 'tensor'), may hold values from -70 to 70
- features: bfloat16 [64, 128, 8192], P('dp'), may hold values from -6 to 6
- k_weight: bfloat16 [8192, 1024], P('dp', 'tensor'), may hold values from -0.0625 to 0.0625
- v_weight: bfloat16 [8192, 1024], P('dp', 'tensor'), may hold values from -0.0625 to 0.0625
- k_gain: float32 [128], replicated, may hold values from 0.1 to 1.9
- block_image: int32 [1024], replicated, may hold values from 0 to 63, as said below
- image_slot: int32 [64], replicated, may hold values from 0 to 63, as said below
- image_tiles: int32 [64], replicated, may hold values from 1 to 4, as said below
- cotangent: bfloat16 [16384, 8192], P('dp', 'tensor'), may hold values from -6 to 6
Outputs:
- attended: bfloat16 [16384, 8192], P('dp', 'tensor')
- grad_queries: bfloat16 [16384, 8192], P('dp', 'tensor')
- grad_features: bfloat16 [64, 128, 8192], P('dp', 'tensor')
- grad_k_weight: float32 [8192, 1024], P('dp', 'tensor')
- grad_v_weight: float32 [8192, 1024], P('dp', 'tensor')
The draws below stay inside these ranges and needn't reach their ends.
Inputs may be any that keep to these rules, and one draw needn't show every extreme that they name: `block_image`: the blocks of one index of dp cite exactly 16 distinct images, whose slots lie on 16 distinct owners (at most one cited slot of each owner); each cited image is cited by one run of consecutive blocks. A permutation: image i lives in slot image_slot[i], that is on index image_slot[i] // 2 of dp, at position image_slot[i] % 2 of its features. `image_tiles`: both ends are taken in every draw.
All inputs are finite; a program needn't handle non-finite values.
Results may differ from the reference program's by a relative error of at most 0.03.
The reference program's roundings to bfloat16 on the way count: a program that leaves them out, or rounds other values in their place, can miss the bound.
Values may be sent and summed in bfloat16 or wider, within the bound.
No kernel may reach another device: no remote copies, remote signals or barrier semaphores. Data moves between devices by JAX's collectives and lax.ppermute only.
A program may use at most 128 MiB of HBM per device.

```python
import jax
import jax.numpy as jnp
from jax import lax

D = 8192
H = 64
KVH = 8
HD = 128
VD = 8192
TILES = 4
TILE_TOK = 32
IMG_DEV = 2
BLK = 16
VTOK = 128
IMAGES = 64
TEXT = 16384
BLK_DEV = 32
CITE = 16
N_DP = 32


def citation_plan(key):
    order_key, perm_key = jax.random.split(key, 2)

    def one_device(dev_key):
        key_one, key_two, key_three = jax.random.split(dev_key, 3)
        owners = jax.random.permutation(key_one, N_DP)[:CITE].astype(jnp.int32)
        positions = jax.random.randint(key_two, (CITE,), 0, IMG_DEV).astype(jnp.int32)
        extras = jax.random.randint(key_three, (BLK_DEV - CITE,), 0, CITE).astype(jnp.int32)
        run_index = jnp.sort(jnp.concatenate([jnp.arange(CITE, dtype=jnp.int32), extras]))
        cited_slots = owners * IMG_DEV + positions
        return cited_slots[run_index]
    block_slots = jax.vmap(one_device)(jax.random.split(order_key, N_DP)).reshape(-1)
    image_slot = jax.random.permutation(perm_key, IMAGES).astype(jnp.int32)
    slot_image = jnp.zeros((IMAGES,), jnp.int32).at[image_slot].set(jnp.arange(IMAGES, dtype=jnp.int32))
    return (slot_image[block_slots].astype(jnp.int32), image_slot)


def draw_block_image(key, part):
    planned = citation_plan(key)
    return planned[0]


def draw_image_slot(key, part):
    planned = citation_plan(key)
    return planned[1]


def draw_image_tiles(key, part):
    key = jax.random.fold_in(key, 3)
    key_one, key_two, key_three = jax.random.split(key, 3)
    tile_counts = jax.random.randint(key_one, (IMAGES,), 1, TILES + 1).astype(jnp.int32)
    fullest = jax.random.randint(key_two, (), 0, IMAGES)
    emptiest = (fullest + 1 + jax.random.randint(key_three, (), 0, IMAGES - 1)) % IMAGES
    tile_counts = tile_counts.at[fullest].set(TILES)
    tile_counts = tile_counts.at[emptiest].set(1)
    return tile_counts.astype(jnp.int32)


def draw_queries(key, part):
    key = jax.random.fold_in(key, 5)
    key_one = jax.random.fold_in(key, 0)
    base_values = jax.random.normal(key_one, (TEXT, D), jnp.float32) * 2.0
    return jnp.clip(base_values, -8.0, 8.0).astype(jnp.bfloat16)


def shard_levels(stream_key, extent, cuts, smallest, largest):
    level = 1.0
    for axis_at, shards_of in cuts:
        draws = jax.random.uniform(jax.random.fold_in(jax.random.fold_in(stream_key, 6), axis_at), (shards_of,), jnp.float32, smallest / len(cuts), largest / len(cuts))
        level = level * jnp.repeat(jnp.exp(draws), extent[axis_at] // shards_of).reshape((-1,) + (1,) * (len(extent) - 1 - axis_at))
    return level


def normal_values(stream_key, dims, deviation, reach, shards=(), kind=jnp.bfloat16):
    drawn = jax.random.normal(stream_key, dims, jnp.float32) * deviation
    if len(shards) > 0:
        drawn = shard_levels(stream_key, dims, shards, -0.22, 0.18) * drawn
    return jnp.clip(drawn, min=-reach, max=reach).astype(kind)


def setup_inputs(seed: int = 0) -> dict:
    key_list = jax.random.split(jax.random.key(seed), 10)
    return {
        "queries": draw_queries(jax.random.fold_in(key_list[9], 71), 0),
        "features": normal_values(key_list[1], (IMAGES, VTOK, VD), 1.0, 6.0, ((0, 32),)),
        "k_weight": normal_values(key_list[2], (VD, KVH * HD), VD ** -0.5, 0.0625, ((0, 32), (1, 8))),
        "v_weight": normal_values(key_list[3], (VD, KVH * HD), VD ** -0.5, 0.0625, ((0, 32), (1, 8))),
        "k_gain": jnp.clip(1.0 + 0.18 * jax.random.normal(key_list[4], (HD,), jnp.float32), 0.1, 1.9),
        "block_image": draw_block_image(jax.random.fold_in(key_list[9], 71), 0),
        "image_slot": draw_image_slot(jax.random.fold_in(key_list[9], 71), 0),
        "image_tiles": draw_image_tiles(jax.random.fold_in(key_list[9], 71), 0),
        "cotangent": normal_values(key_list[8], (TEXT, D), 1.0, 6.0, ((0, 32), (1, 8))),
    }


EPS = 1e-05
MASKED_SCORE = -1e+30

def key_norm(raw_keys, gain):
    mean_square = lax.optimization_barrier(jnp.mean(raw_keys * raw_keys, axis=-1, keepdims=True))
    return raw_keys * lax.rsqrt(mean_square + EPS) * gain

def round_kept(values_full):
    return lax.optimization_barrier(values_full.astype(jnp.bfloat16)).astype(jnp.float32)

def reference(queries, features, k_weight, v_weight, k_gain, block_image, image_slot, image_tiles, cotangent):
    group_size = H // KVH
    score_scale = HD ** (-0.5)
    flat_rows = features.reshape(IMAGES * VTOK, VD)
    keys_raw = jnp.dot(flat_rows, k_weight, preferred_element_type=jnp.float32).reshape(IMAGES * VTOK, KVH, HD)
    values_raw = jnp.dot(flat_rows, v_weight, preferred_element_type=jnp.float32)
    keys_all = key_norm(keys_raw, k_gain).astype(jnp.bfloat16).reshape(IMAGES, VTOK, KVH, HD)
    values_all = values_raw.astype(jnp.bfloat16).reshape(IMAGES, VTOK, KVH, HD)
    block_slots = image_slot[block_image].astype(jnp.int32).reshape(N_DP, BLK_DEV)
    block_tiles = image_tiles[block_image].astype(jnp.int32).reshape(N_DP, BLK_DEV)
    query_blocks = queries.reshape(N_DP, BLK_DEV, BLK, KVH, group_size, HD)
    grad_blocks = cotangent.reshape(N_DP, BLK_DEV, BLK, KVH, group_size, HD)
    token_index = jnp.arange(VTOK, dtype=jnp.int32)

    def one_device(running, inputs):
        query_here, grad_here, slots_here, tiles_here = inputs
        block_keys = keys_all[slots_here].astype(jnp.float32)
        block_values = values_all[slots_here].astype(jnp.float32)
        query_full = query_here.astype(jnp.float32)
        grad_full = grad_here.astype(jnp.float32)
        valid_keys = token_index[None, :] < (tiles_here * TILE_TOK)[:, None]
        scores = jnp.einsum('brkgd,bjkd->bkgrj', query_full, block_keys) * score_scale
        scores = jnp.where(valid_keys[:, None, None, None, :], scores, MASKED_SCORE)
        row_max = lax.optimization_barrier(jnp.max(scores, axis=-1, keepdims=True))
        exp_scores = jnp.exp(scores - row_max)
        attn_probs = exp_scores / lax.optimization_barrier(jnp.sum(exp_scores, axis=-1, keepdims=True))
        probs_half = round_kept(attn_probs)
        attended = jnp.einsum('bkgrj,bjkd->brkgd', probs_half, block_values).astype(jnp.bfloat16)
        grad_probs = jnp.einsum('brkgd,bjkd->bkgrj', grad_full, block_values)
        row_delta = lax.optimization_barrier(jnp.sum(attn_probs * grad_probs, axis=-1, keepdims=True))
        grad_scores = round_kept(attn_probs * (grad_probs - row_delta) * score_scale)
        grad_query = jnp.einsum('bkgrj,bjkd->brkgd', grad_scores, block_keys).astype(jnp.bfloat16)
        key_blocks = jnp.einsum('bkgrj,brkgd->bjkd', grad_scores, query_full)
        value_blocks = jnp.einsum('bkgrj,brkgd->bjkd', probs_half, grad_full)
        empty_slots = jnp.zeros((IMAGES, VTOK, KVH, HD), jnp.float32)
        key_part = round_kept(empty_slots.at[slots_here].add(key_blocks))
        value_part = round_kept(empty_slots.at[slots_here].add(value_blocks))
        return ((running[0] + key_part, running[1] + value_part), (attended, grad_query))
    initial = (jnp.zeros((IMAGES, VTOK, KVH, HD), jnp.float32), jnp.zeros((IMAGES, VTOK, KVH, HD), jnp.float32))
    sums, outputs = lax.scan(one_device, initial, (query_blocks, grad_blocks, block_slots, block_tiles))
    grad_keys, grad_values = sums
    attended = outputs[0].reshape(TEXT, D)
    grad_queries = outputs[1].reshape(TEXT, D)
    _, pull_back = jax.vjp(lambda raw_keys: key_norm(raw_keys, k_gain), keys_raw)
    grad_keys_raw = pull_back(grad_keys.reshape(IMAGES * VTOK, KVH, HD))[0]
    grad_keys_raw = grad_keys_raw.reshape(IMAGES * VTOK, KVH * HD).astype(jnp.bfloat16)
    grad_values_half = grad_values.reshape(IMAGES * VTOK, KVH * HD).astype(jnp.bfloat16)
    grad_k_weight = jnp.dot(flat_rows.T, grad_keys_raw, preferred_element_type=jnp.float32)
    grad_v_weight = jnp.dot(flat_rows.T, grad_values_half, preferred_element_type=jnp.float32)
    feature_sum = jnp.dot(grad_keys_raw, k_weight.T, preferred_element_type=jnp.float32)
    feature_sum = feature_sum + jnp.dot(grad_values_half, v_weight.T, preferred_element_type=jnp.float32)
    grad_features = feature_sum.astype(jnp.bfloat16).reshape(IMAGES, VTOK, VD)
    return (attended, grad_queries, grad_features, grad_k_weight, grad_v_weight)
```

```python
import functools

import jax
import jax.numpy as jnp
from jax import lax
from jax.experimental import pallas as pl
from jax.experimental.pallas import tpu as pltpu
from jax.sharding import PartitionSpec as P

TILES = 4
EPS = 1e-05
MASKED_SCORE = -1e30
NY, NZ = 4, 8
Y_GROUPS = [[y * NZ + z for y in range(NY)] for z in range(NZ)]
Z_GROUPS = [[y * NZ + z for z in range(NZ)] for y in range(NY)]
BF16, F32 = jnp.bfloat16, jnp.float32
VMEM_BYTES = 48 * 1024 * 1024


def dot_dims(a, b, a_dim, b_dim):
    return lax.dot_general(
        a, b, (((a_dim,), (b_dim,)), ((), ())), preferred_element_type=F32
    )


def project_kernel(pos_ref, f_ref, w_ref, gain_ref, send_ref, raw_ref, acc, kv):
    step = pl.program_id(0)
    part = jnp.dot(f_ref[...], w_ref[...], preferred_element_type=F32)

    @pl.when(step == 0)
    def _():
        acc[...] = part

    @pl.when(step > 0)
    def _():
        acc[...] += part

    @pl.when(step == pl.num_programs(0) - 1)
    def _():
        head_dim = gain_ref.shape[1]
        tokens = send_ref.shape[1]
        raw = acc[:, :head_dim]
        raw_ref[...] = raw
        scale = lax.rsqrt(jnp.mean(raw * raw, axis=-1, keepdims=True) + EPS)
        keys = (raw * scale * gain_ref[...]).astype(BF16)
        values = acc[:, head_dim:].astype(BF16)
        for i in range(kv.shape[0]):
            kv[i, :, :head_dim] = keys[i * tokens : (i + 1) * tokens]
            kv[i, :, head_dim:] = values[i * tokens : (i + 1) * tokens]

        def put(d, carry):
            send_ref[d] = kv[jnp.maximum(pos_ref[d], 0)]
            return carry

        lax.fori_loop(0, send_ref.shape[0], put, 0)


def project(pos, rows, weights, gain, images, tokens):
    depth = rows.shape[1]
    cols = weights.shape[1]
    dp = pos.shape[0]
    tile = 1024
    return pl.pallas_call(
        project_kernel,
        grid_spec=pltpu.PrefetchScalarGridSpec(
            num_scalar_prefetch=1,
            grid=(depth // tile,),
            in_specs=[
                pl.BlockSpec((rows.shape[0], tile), lambda i, s: (0, i)),
                pl.BlockSpec((tile, cols), lambda i, s: (i, 0)),
                pl.BlockSpec((1, gain.shape[1]), lambda i, s: (0, 0)),
            ],
            out_specs=[
                pl.BlockSpec((dp, tokens, cols), lambda i, s: (0, 0, 0)),
                pl.BlockSpec((rows.shape[0], cols // 2), lambda i, s: (0, 0)),
            ],
            scratch_shapes=[
                pltpu.VMEM((rows.shape[0], cols), F32),
                pltpu.VMEM((images, tokens, cols), BF16),
            ],
        ),
        out_shape=[
            jax.ShapeDtypeStruct((dp, tokens, cols), BF16),
            jax.ShapeDtypeStruct((rows.shape[0], cols // 2), F32),
        ],
        compiler_params=pltpu.CompilerParams(vmem_limit_bytes=VMEM_BYTES),
        name="project",
    )(pos, rows, weights, gain)


def attend_kernel(
    owner_ref, valid_ref, first_ref, q_ref, ct_ref, kv_ref, out_ref, gq_ref, part_ref, acc
):
    blocks = owner_ref.shape[0]
    rows = q_ref.shape[0] // blocks
    head_dim = kv_ref.shape[2] // 2
    heads = q_ref.shape[1] // head_dim
    tokens = kv_ref.shape[1]
    scale = head_dim**-0.5
    part_ref[...] = jnp.zeros_like(part_ref)

    def one_block(b, carry):
        start = pl.multiple_of(b * rows, rows)
        owner = owner_ref[b]

        def load(ref):
            return jnp.concatenate(
                [
                    ref[pl.ds(start, rows), g * head_dim : (g + 1) * head_dim]
                    for g in range(heads)
                ],
                axis=0,
            )

        def store(ref, full):
            for g in range(heads):
                ref[pl.ds(start, rows), g * head_dim : (g + 1) * head_dim] = full[
                    g * rows : (g + 1) * rows
                ]

        queries, grads = load(q_ref), load(ct_ref)
        keys = kv_ref[owner, :, :head_dim]
        values = kv_ref[owner, :, head_dim:]
        scores = dot_dims(keys, queries, 1, 1) * scale
        token = lax.broadcasted_iota(jnp.int32, (tokens, 1), 0)
        scores = jnp.where(token < valid_ref[b], scores, MASKED_SCORE)
        weights = jnp.exp(scores - jnp.max(scores, axis=0, keepdims=True))
        probs = weights / jnp.sum(weights, axis=0, keepdims=True)
        probs_half = probs.astype(BF16)
        d_probs = dot_dims(values, grads, 1, 1)
        delta = jnp.sum(probs * d_probs, axis=0, keepdims=True)
        d_scores = (probs * (d_probs - delta) * scale).astype(BF16)
        store(out_ref, dot_dims(probs_half, values, 0, 0).astype(BF16))
        store(gq_ref, dot_dims(d_scores, keys, 0, 0).astype(BF16))
        key_part = jnp.dot(d_scores, queries, preferred_element_type=F32)
        value_part = jnp.dot(probs_half, grads, preferred_element_type=F32)
        keep = first_ref[b] == 0
        key_part = key_part + jnp.where(keep, acc[:, :head_dim], 0.0)
        value_part = value_part + jnp.where(keep, acc[:, head_dim:], 0.0)
        acc[:, :head_dim] = key_part
        acc[:, head_dim:] = value_part
        part_ref[owner, :, :head_dim] = key_part.astype(BF16)
        part_ref[owner, :, head_dim:] = value_part.astype(BF16)
        return carry

    acc[...] = jnp.zeros_like(acc)
    lax.fori_loop(0, blocks, one_block, 0, unroll=2)


def attend(owner, valid, first, queries, cotangent, kv):
    smem = pl.BlockSpec(memory_space=pltpu.SMEM)
    vmem = pl.BlockSpec(memory_space=pltpu.VMEM)
    return pl.pallas_call(
        attend_kernel,
        in_specs=[smem] * 3 + [vmem] * 3,
        out_specs=[vmem] * 3,
        out_shape=[
            jax.ShapeDtypeStruct(queries.shape, BF16),
            jax.ShapeDtypeStruct(queries.shape, BF16),
            jax.ShapeDtypeStruct(kv.shape, BF16),
        ],
        scratch_shapes=[pltpu.VMEM(kv.shape[1:], F32)],
        compiler_params=pltpu.CompilerParams(vmem_limit_bytes=VMEM_BYTES),
        name="attend",
    )(owner, valid, first, queries, cotangent, kv)


def owner_kernel(pos_ref, part_ref, raw_ref, gain_ref, grad_ref, acc):
    head_dim = gain_ref.shape[1]
    tokens = part_ref.shape[1]
    acc[...] = jnp.zeros_like(acc)

    def add(d, carry):
        @pl.when(pos_ref[d] >= 0)
        def _():
            acc[pos_ref[d]] += part_ref[d].astype(F32)

        return carry

    lax.fori_loop(0, part_ref.shape[0], add, 0)
    gain = gain_ref[...]
    for i in range(acc.shape[0]):
        here = slice(i * tokens, (i + 1) * tokens)
        raw = raw_ref[here]
        scale = lax.rsqrt(jnp.mean(raw * raw, axis=-1, keepdims=True) + EPS)
        scaled = acc[i, :, :head_dim] * gain
        pull = jnp.mean(raw * scaled, axis=-1, keepdims=True)
        grad = scale * scaled - raw * (scale * scale * scale * pull)
        grad_ref[here, :head_dim] = grad.astype(BF16)
        grad_ref[here, head_dim:] = acc[i, :, head_dim:].astype(BF16)


def owner_grads(pos, parts, raw, gain, images):
    smem = pl.BlockSpec(memory_space=pltpu.SMEM)
    vmem = pl.BlockSpec(memory_space=pltpu.VMEM)
    return pl.pallas_call(
        owner_kernel,
        in_specs=[smem] + [vmem] * 3,
        out_specs=vmem,
        out_shape=jax.ShapeDtypeStruct((raw.shape[0], parts.shape[2]), BF16),
        scratch_shapes=[pltpu.VMEM((images,) + parts.shape[1:], F32)],
        compiler_params=pltpu.CompilerParams(vmem_limit_bytes=VMEM_BYTES),
        name="owner_grads",
    )(pos, parts, raw, gain)


def local(
    queries, features, k_weight, v_weight, k_gain, block_image, image_slot, image_tiles, cotangent
):
    dp_count = lax.axis_size("dp")
    tensor_count = lax.axis_size("tensor")
    me = lax.axis_index("dp")
    images, tokens, width = features.shape
    head_dim = k_gain.shape[0]
    cols = 2 * head_dim
    rows = features.reshape(images * tokens, width)
    gain = k_gain.reshape(1, head_dim)

    image_ids = lax.broadcasted_iota(jnp.int32, (1, image_slot.shape[0]), 1)
    id_match = block_image[:, None] == image_ids
    slots = jnp.sum(jnp.where(id_match, image_slot[None, :], 0), axis=1).reshape(dp_count, -1)
    tiles = jnp.sum(jnp.where(id_match, image_tiles[None, :], 0), axis=1).reshape(dp_count, -1)
    my_slots = lax.dynamic_index_in_dim(slots, me, 0, keepdims=False)
    my_tiles = lax.dynamic_index_in_dim(tiles, me, 0, keepdims=False)
    owner = my_slots // images
    valid = my_tiles * (tokens // TILES)
    first = jnp.concatenate(
        [jnp.ones((1,), jnp.int32), (my_slots[1:] != my_slots[:-1]).astype(jnp.int32)]
    )
    pos = jnp.max(jnp.where(slots // images == me, slots % images, -1), axis=1)

    weights = lax.all_gather(
        jnp.concatenate([k_weight, v_weight], axis=1), "dp", axis=0, tiled=True
    )
    feature_cols = lax.all_to_all(
        rows, "dp", 1, 0, tiled=True, axis_index_groups=Y_GROUPS
    )
    send, raw = project(pos, rows, weights, gain, images, tokens)
    kv = lax.all_to_all(send, "dp", 0, 0, tiled=True)
    attended, grad_queries, parts = attend(owner, valid, first, queries, cotangent, kv)
    parts = lax.all_to_all(parts, "dp", 0, 0, tiled=True)
    grads = owner_grads(pos, parts, raw, gain, images)

    line = lax.all_gather(grads, "dp", axis=0, tiled=True, axis_index_groups=Y_GROUPS)
    shares = dot_dims(feature_cols, line, 0, 0).astype(BF16)
    shares = lax.all_to_all(
        shares.reshape(NZ, -1, cols), "dp", 0, 0, tiled=True, axis_index_groups=Z_GROUPS
    )
    weight_grads = jnp.sum(shares.astype(F32), axis=0)

    by_target = jnp.transpose(
        grads.reshape(images, tensor_count, tokens // tensor_count, cols), (1, 0, 2, 3)
    ).reshape(images * tokens, cols)
    partial = dot_dims(by_target, weights, 1, 1).astype(BF16)
    partial = lax.all_to_all(
        partial.reshape(tensor_count, -1, width), "tensor", 0, 0, tiled=True
    )
    grad_features = jnp.sum(partial.astype(F32), axis=0).astype(BF16)
    grad_features = grad_features.reshape(images, tokens // tensor_count, width)
    return (
        attended,
        grad_queries,
        grad_features,
        weight_grads[:, :head_dim],
        weight_grads[:, head_dim:],
    )


def solution(mesh):
    in_specs = (
        P("dp", "tensor"),
        P("dp", None, None),
        P("dp", "tensor"),
        P("dp", "tensor"),
        P(),
        P(),
        P(),
        P(),
        P("dp", "tensor"),
    )
    out_specs = (
        P("dp", "tensor"),
        P("dp", "tensor"),
        P("dp", "tensor", None),
        P("dp", "tensor"),
        P("dp", "tensor"),
    )
    return jax.shard_map(local, mesh=mesh, in_specs=in_specs, out_specs=out_specs, check_vma=False)
```

```python
import functools

import jax
import jax.numpy as jnp
from jax import lax
from jax.experimental import pallas as pl
from jax.experimental.pallas import tpu as pltpu
from jax.sharding import PartitionSpec as P

TILES = 4
EPS = 1e-05
MASKED_SCORE = -1e30
NY, NZ = 4, 8
Y_GROUPS = [[y * NZ + z for y in range(NY)] for z in range(NZ)]
Z_GROUPS = [[y * NZ + z for z in range(NZ)] for y in range(NY)]
BF16, F32 = jnp.bfloat16, jnp.float32
VMEM_BYTES = 32 * 1024 * 1024
GROUP = 4


def dot_dims(a, b, a_dim, b_dim):
    return lax.dot_general(
        a, b, (((a_dim,), (b_dim,)), ((), ())), preferred_element_type=F32
    )


def project_kernel(
    pos_ref, place_ref, f_ref, kw_ref, *refs, zones
):
    vw_refs, (gain_ref, send_ref, raw_ref, kv) = refs[: len(zones)], refs[len(zones) :]
    head_dim = gain_ref.shape[1]
    tokens = send_ref.shape[1]
    total = jnp.zeros((f_ref.shape[0], 2 * head_dim), F32)
    for cols, w in weight_blocks(place_ref, kw_ref, vw_refs, zones):
        total = total + jnp.dot(f_ref[:, cols], w, preferred_element_type=F32)
    raw = total[:, :head_dim]
    raw_ref[...] = raw
    scale = lax.rsqrt(jnp.mean(raw * raw, axis=-1, keepdims=True) + EPS)
    keys = (raw * scale * gain_ref[...]).astype(BF16)
    values = total[:, head_dim:].astype(BF16)
    for i in range(kv.shape[0]):
        kv[i, :, :head_dim] = keys[i * tokens : (i + 1) * tokens]
        kv[i, :, head_dim:] = values[i * tokens : (i + 1) * tokens]

    def put(d, carry):
        send_ref[d] = kv[jnp.maximum(pos_ref[d], 0)]
        return carry

    lax.fori_loop(0, send_ref.shape[0], put, 0)


def weight_blocks(place_ref, kw_ref, vw_refs, zones):
    for ref, (offset, y_from, y_count) in zip(vw_refs, zones):
        z = lax.rem(place_ref[1] + offset + NZ, NZ)
        block = ref.shape[0] // y_count
        for i in range(y_count):
            y = lax.rem(place_ref[0] + y_from + i, NY)
            at = pl.multiple_of((y * NZ + z) * block, block)
            here = pl.ds(at, block)
            yield here, jnp.concatenate(
                [kw_ref[here, :], ref[i * block : (i + 1) * block, :]], axis=1
            )


def project(pos, place, rows, k_full, v_pieces, zones, gain, images, tokens):
    smem = pl.BlockSpec(memory_space=pltpu.SMEM)
    vmem = pl.BlockSpec(memory_space=pltpu.VMEM)
    dp, cols = pos.shape[0], 2 * k_full.shape[1]
    return pl.pallas_call(
        functools.partial(project_kernel, zones=zones),
        in_specs=[smem] * 2 + [vmem] * (3 + len(v_pieces)),
        out_specs=[vmem] * 2,
        out_shape=[
            jax.ShapeDtypeStruct((dp, tokens, cols), BF16),
            jax.ShapeDtypeStruct((rows.shape[0], cols // 2), F32),
        ],
        scratch_shapes=[pltpu.VMEM((images, tokens, cols), BF16)],
        compiler_params=pltpu.CompilerParams(vmem_limit_bytes=VMEM_BYTES),
        cost_estimate=pl.CostEstimate(
            flops=2 * rows.size * cols, bytes_accessed=12 * 2**20, transcendentals=0
        ),
        name="project",
    )(pos, place, rows, k_full, *v_pieces, gain)


def feature_kernel(place_ref, grad_ref, kw_ref, *refs, zones, targets):
    vw_refs, (own_ref, other_ref, lhs) = refs[: len(zones)], refs[len(zones) :]
    half = own_ref.shape[0]
    chips = targets // 2
    tokens = grad_ref.shape[0] // 2
    share = tokens // targets
    for core in range(2):
        for chip in range(chips):
            x = lax.rem(place_ref[2] + chip, chips)
            target = x * 2 + lax.rem(place_ref[3] + core, 2)
            for i in range(2):
                at = pl.multiple_of(i * tokens + target * share, share)
                to = ((core * chips + chip) * 2 + i) * share
                lhs[to : to + share, :] = grad_ref[pl.ds(at, share), :]
    for cols, w in weight_blocks(place_ref, kw_ref, vw_refs, zones):
        part = dot_dims(lhs[...], w, 1, 1).astype(BF16)
        own_ref[:, cols] = part[:half]
        other_ref[:, cols] = part[half:]


def feature_terms(place, grads, k_full, v_pieces, zones, targets):
    smem = pl.BlockSpec(memory_space=pltpu.SMEM)
    vmem = pl.BlockSpec(memory_space=pltpu.VMEM)
    half = jax.ShapeDtypeStruct((grads.shape[0] // 2, k_full.shape[0]), BF16)
    return pl.pallas_call(
        functools.partial(feature_kernel, zones=zones, targets=targets),
        in_specs=[smem] + [vmem] * (2 + len(v_pieces)),
        out_specs=[vmem] * 2,
        out_shape=[half, half],
        scratch_shapes=[pltpu.VMEM(grads.shape, BF16)],
        compiler_params=pltpu.CompilerParams(vmem_limit_bytes=VMEM_BYTES),
        cost_estimate=pl.CostEstimate(
            flops=4 * half.size * grads.shape[1], bytes_accessed=8 * 2**20, transcendentals=0
        ),
        name="feature_terms",
    )(place, grads, k_full, *v_pieces)


def load_heads(ref, start, rows, head_dim):
    heads = ref.shape[1] // head_dim
    return jnp.concatenate(
        [ref[pl.ds(start, rows), g * head_dim : (g + 1) * head_dim] for g in range(heads)],
        axis=0,
    )


def store_heads(ref, start, rows, head_dim, full):
    for g in range(ref.shape[1] // head_dim):
        ref[pl.ds(start, rows), g * head_dim : (g + 1) * head_dim] = full[
            g * rows : (g + 1) * rows
        ]


def attend_kernel(
    owner_ref, valid_ref, first_ref, q_ref, ct_ref, kv_ref, part_ref, probs_ref, ds_ref, acc
):
    blocks = owner_ref.shape[0]
    rows = q_ref.shape[0] // blocks
    head_dim = kv_ref.shape[2] // 2
    tokens = kv_ref.shape[1]
    scale = head_dim**-0.5
    part_ref[...] = jnp.zeros_like(part_ref)
    acc[...] = jnp.zeros_like(acc)

    def some_blocks(step, carry):
        at = [step * GROUP + i for i in range(GROUP)]
        owners = [owner_ref[b] for b in at]
        starts = [pl.multiple_of(b * rows, rows) for b in at]
        queries = [load_heads(q_ref, s, rows, head_dim) for s in starts]
        grads = [load_heads(ct_ref, s, rows, head_dim) for s in starts]
        scores = [
            dot_dims(kv_ref[o, :, :head_dim], q, 1, 1) * scale for o, q in zip(owners, queries)
        ]
        d_probs = [dot_dims(kv_ref[o, :, head_dim:], g, 1, 1) for o, g in zip(owners, grads)]
        token = lax.broadcasted_iota(jnp.int32, (tokens, 1), 0)
        scores = [
            jnp.where(token < valid_ref[b], s, MASKED_SCORE) for b, s in zip(at, scores)
        ]
        weights = [jnp.exp(s - jnp.max(s, axis=0, keepdims=True)) for s in scores]
        probs = [w * (1.0 / jnp.sum(w, axis=0, keepdims=True)) for w in weights]
        halves = [p.astype(BF16) for p in probs]
        deltas = [jnp.sum(p * d, axis=0, keepdims=True) for p, d in zip(probs, d_probs)]
        d_scores = [
            (p * (d - x) * scale).astype(BF16) for p, d, x in zip(probs, d_probs, deltas)
        ]
        key_parts = [
            jnp.dot(d, q, preferred_element_type=F32) for d, q in zip(d_scores, queries)
        ]
        value_parts = [
            jnp.dot(p, g, preferred_element_type=F32) for p, g in zip(halves, grads)
        ]
        key_run, value_run = acc[:, :head_dim], acc[:, head_dim:]
        for i, b in enumerate(at):
            keep = first_ref[b] == 0
            key_run = key_parts[i] + jnp.where(keep, key_run, 0.0)
            value_run = value_parts[i] + jnp.where(keep, value_run, 0.0)
            part_ref[owners[i], :, :head_dim] = key_run.astype(BF16)
            part_ref[owners[i], :, head_dim:] = value_run.astype(BF16)
            probs_ref[b] = halves[i]
            ds_ref[b] = d_scores[i]
        acc[:, :head_dim] = key_run
        acc[:, head_dim:] = value_run
        return carry

    lax.fori_loop(0, blocks // GROUP, some_blocks, 0)


def attend(owner, valid, first, queries, cotangent, kv):
    smem = pl.BlockSpec(memory_space=pltpu.SMEM)
    vmem = pl.BlockSpec(memory_space=pltpu.VMEM)
    blocks, (_, tokens, cols) = owner.shape[0], kv.shape
    rows = queries.size * 2 // (blocks * cols)
    stash = jax.ShapeDtypeStruct((blocks, tokens, rows), BF16)
    return pl.pallas_call(
        attend_kernel,
        in_specs=[smem] * 3 + [vmem] * 3,
        out_specs=[vmem] * 3,
        out_shape=[jax.ShapeDtypeStruct(kv.shape, BF16), stash, stash],
        scratch_shapes=[pltpu.VMEM(kv.shape[1:], F32)],
        compiler_params=pltpu.CompilerParams(vmem_limit_bytes=VMEM_BYTES),
        cost_estimate=pl.CostEstimate(
            flops=8 * queries.size * tokens, bytes_accessed=8 * 2**20, transcendentals=0
        ),
        name="attend",
    )(owner, valid, first, queries, cotangent, kv)


def apply_kernel(owner_ref, kv_ref, probs_ref, ds_ref, out_ref, gq_ref):
    blocks = owner_ref.shape[0]
    rows = out_ref.shape[0] // blocks
    head_dim = kv_ref.shape[2] // 2

    def some_blocks(step, carry):
        at = [step * GROUP + i for i in range(GROUP)]
        owners = [owner_ref[b] for b in at]
        outs = [
            dot_dims(probs_ref[b], kv_ref[o, :, head_dim:], 0, 0) for b, o in zip(at, owners)
        ]
        gqs = [dot_dims(ds_ref[b], kv_ref[o, :, :head_dim], 0, 0) for b, o in zip(at, owners)]
        for i, b in enumerate(at):
            start = pl.multiple_of(b * rows, rows)
            store_heads(out_ref, start, rows, head_dim, outs[i].astype(BF16))
            store_heads(gq_ref, start, rows, head_dim, gqs[i].astype(BF16))
        return carry

    lax.fori_loop(0, blocks // GROUP, some_blocks, 0)


def apply(owner, kv, probs, d_scores, shape):
    smem = pl.BlockSpec(memory_space=pltpu.SMEM)
    vmem = pl.BlockSpec(memory_space=pltpu.VMEM)
    out = jax.ShapeDtypeStruct(shape, BF16)
    return pl.pallas_call(
        apply_kernel,
        in_specs=[smem] + [vmem] * 3,
        out_specs=[vmem] * 2,
        out_shape=[out, out],
        compiler_params=pltpu.CompilerParams(vmem_limit_bytes=VMEM_BYTES),
        cost_estimate=pl.CostEstimate(
            flops=4 * out.size * kv.shape[1], bytes_accessed=6 * 2**20, transcendentals=0
        ),
        name="apply",
    )(owner, kv, probs, d_scores)


def owner_kernel(
    pos_ref, place_ref, part_ref, raw_ref, gain_ref, grad_ref, by_core_ref, acc
):
    head_dim = gain_ref.shape[1]
    tokens = part_ref.shape[1]
    acc[...] = jnp.zeros_like(acc)

    def add(d, carry):
        @pl.when(pos_ref[d] >= 0)
        def _():
            acc[pos_ref[d]] += part_ref[d].astype(F32)

        return carry

    lax.fori_loop(0, part_ref.shape[0], add, 0)
    gain = gain_ref[...]
    for i in range(acc.shape[0]):
        here = slice(i * tokens, (i + 1) * tokens)
        raw = raw_ref[here]
        scale = lax.rsqrt(jnp.mean(raw * raw, axis=-1, keepdims=True) + EPS)
        scaled = acc[i, :, :head_dim] * gain
        pull = jnp.mean(raw * scaled, axis=-1, keepdims=True)
        grad = scale * scaled - raw * (scale * scale * scale * pull)
        grad_ref[here, :head_dim] = grad.astype(BF16)
        grad_ref[here, head_dim:] = acc[i, :, head_dim:].astype(BF16)
    for i in range(2):
        at = pl.multiple_of(lax.rem(place_ref[3] + i, 2) * tokens, tokens)
        by_core_ref[i * tokens : (i + 1) * tokens, :] = grad_ref[pl.ds(at, tokens), :]


def owner_grads(pos, place, parts, raw, gain, images):
    smem = pl.BlockSpec(memory_space=pltpu.SMEM)
    vmem = pl.BlockSpec(memory_space=pltpu.VMEM)
    return pl.pallas_call(
        owner_kernel,
        in_specs=[smem] * 2 + [vmem] * 3,
        out_specs=[vmem] * 2,
        out_shape=[jax.ShapeDtypeStruct((raw.shape[0], parts.shape[2]), BF16)] * 2,
        scratch_shapes=[pltpu.VMEM((images,) + parts.shape[1:], F32)],
        compiler_params=pltpu.CompilerParams(vmem_limit_bytes=VMEM_BYTES),
        name="owner_grads",
    )(pos, place, parts, raw, gain)


def transpose_kernel(*refs):
    pieces, out_ref = refs[:-1], refs[-1]
    tokens = pieces[0].shape[0]
    for i, ref in enumerate(pieces):
        out_ref[:, i * tokens : (i + 1) * tokens] = ref[...].T


def transpose_pieces(pieces):
    vmem = pl.BlockSpec(memory_space=pltpu.VMEM)
    tokens, width = pieces[0].shape
    return pl.pallas_call(
        transpose_kernel,
        in_specs=[vmem] * len(pieces),
        out_specs=vmem,
        out_shape=jax.ShapeDtypeStruct((width, tokens * len(pieces)), BF16),
        compiler_params=pltpu.CompilerParams(vmem_limit_bytes=VMEM_BYTES),
        cost_estimate=pl.CostEstimate(
            flops=0, bytes_accessed=8 * tokens * width * len(pieces), transcendentals=0
        ),
        name="transpose_pieces",
    )(*pieces)


def weight_kernel(own_ref, other_ref, *refs):
    lines, out_ref = refs[:-1], refs[-1]
    half = lines[0].shape[0] // 2
    first = jnp.concatenate([ref[:half, :] for ref in lines], axis=0)
    second = jnp.concatenate([ref[half:, :] for ref in lines], axis=0)
    block = out_ref.shape[1]
    for i in range(out_ref.shape[0]):
        here = slice(i * block, (i + 1) * block)
        total = jnp.dot(own_ref[here, :], first, preferred_element_type=F32)
        total = total + jnp.dot(other_ref[here, :], second, preferred_element_type=F32)
        out_ref[i] = total.astype(BF16)


def weight_terms(own_cols, other_cols, lines):
    vmem = pl.BlockSpec(memory_space=pltpu.VMEM)
    width, cols = own_cols.shape[0], lines[0].shape[1]
    return pl.pallas_call(
        weight_kernel,
        in_specs=[vmem] * (2 + len(lines)),
        out_specs=vmem,
        out_shape=jax.ShapeDtypeStruct((NZ, width // NZ, cols), BF16),
        compiler_params=pltpu.CompilerParams(vmem_limit_bytes=VMEM_BYTES),
        cost_estimate=pl.CostEstimate(
            flops=4 * own_cols.size * cols, bytes_accessed=6 * 2**20, transcendentals=0
        ),
        name="weight_terms",
    )(own_cols, other_cols, *lines)


def shift_y(x, by):
    if by == 0:
        return x
    pairs = [(y * NZ + z, (y + by) % NY * NZ + z) for y in range(NY) for z in range(NZ)]
    return lax.ppermute(x, "dp", pairs)


def shift_z(x, by):
    pairs = [(y * NZ + z, y * NZ + (z + by) % NZ) for y in range(NY) for z in range(NZ)]
    return lax.ppermute(x, "dp", pairs)


def swap_cores(x, count):
    return lax.ppermute(x, "tensor", [(t, t ^ 1) for t in range(count)])


def local(
    queries, features, k_weight, v_weight, k_gain, block_image, image_slot, image_tiles, cotangent
):
    dp_count = lax.axis_size("dp")
    tensor_count = lax.axis_size("tensor")
    me = lax.axis_index("dp")
    images, tokens, width = features.shape
    head_dim = k_gain.shape[0]
    cols = 2 * head_dim
    rows = features.reshape(images * tokens, width)
    gain = k_gain.reshape(1, head_dim)

    image_ids = lax.broadcasted_iota(jnp.int32, (1, image_slot.shape[0]), 1)
    id_match = block_image[:, None] == image_ids
    slots = jnp.sum(jnp.where(id_match, image_slot[None, :], 0), axis=1).reshape(dp_count, -1)
    tiles = jnp.sum(jnp.where(id_match, image_tiles[None, :], 0), axis=1).reshape(dp_count, -1)
    my_slots = lax.dynamic_index_in_dim(slots, me, 0, keepdims=False)
    my_tiles = lax.dynamic_index_in_dim(tiles, me, 0, keepdims=False)
    owner = my_slots // images
    valid = my_tiles * (tokens // TILES)
    first = jnp.concatenate(
        [jnp.ones((1,), jnp.int32), (my_slots[1:] != my_slots[:-1]).astype(jnp.int32)]
    )
    pos = jnp.max(jnp.where(slots // images == me, slots % images, -1), axis=1)

    pos, owner, valid, first = lax.optimization_barrier((pos, owner, valid, first))
    my_y, my_z = me // NZ, lax.rem(me, NZ)
    tensor = lax.axis_index("tensor")
    place = jnp.stack([my_y, my_z, tensor // 2, lax.rem(tensor, 2)])

    block = k_weight.shape[0]
    k_line = lax.all_to_all(
        jnp.broadcast_to(k_weight, (NZ,) + k_weight.shape),
        "dp", 0, 0, tiled=True, axis_index_groups=Z_GROUPS,
    )
    v_line = jnp.concatenate([shift_y(v_weight, (NY - i) % NY) for i in range(NY)])
    below, above = shift_z(v_line, 1), shift_z(v_line, -1)
    k_line, below, above = lax.optimization_barrier((k_line, below, above))
    k_full = lax.all_to_all(
        jnp.broadcast_to(k_line, (NY,) + k_line.shape),
        "dp", 0, 0, tiled=True, axis_index_groups=Y_GROUPS,
    ).reshape(width, head_dim)
    v_pieces, zones = [v_line], [(0, 0, NY)]
    for hop in range(1, NZ // 2):
        if hop > 1:
            below, above = shift_z(below, 1), shift_z(above, -1)
        v_pieces += [below, above]
        zones += [(-hop, 0, NY), (hop, 0, NY)]
    half = NY // 2 * block
    v_pieces += [shift_z(below[:half], 1), shift_z(above[half:], -1)]
    zones += [(NZ // 2, 0, NY // 2), (NZ // 2, NY // 2, NY // 2)]

    send, raw = project(pos, place, rows, k_full, v_pieces, zones, gain, images, tokens)
    kv = lax.all_to_all(send, "dp", 0, 0, tiled=True)

    rows_later, _ = lax.optimization_barrier((features, raw))
    core = place[3]
    span = width // NY
    col_pieces = [
        shift_y(
            lax.dynamic_slice(
                rows_later, (core, 0, (my_y + s) % NY * span), (1, tokens, span)
            )[0],
            s,
        )
        for s in range(NY)
    ]

    parts, probs, d_scores = attend(owner, valid, first, queries, cotangent, kv)
    parts, col_pieces = lax.optimization_barrier((parts, col_pieces))
    parts = lax.all_to_all(parts, "dp", 0, 0, tiled=True)
    own_cols = transpose_pieces(col_pieces)
    other_cols = swap_cores(own_cols, tensor_count)
    attended, grad_queries = apply(owner, kv, probs, d_scores, queries.shape)
    parts, other_cols, attended, grad_queries = lax.optimization_barrier(
        (parts, other_cols, attended, grad_queries)
    )
    grads, by_core = owner_grads(pos, place, parts, raw, gain, images)

    lines = [shift_y(by_core, s) for s in range(NY)]
    shares = weight_terms(own_cols, other_cols, lines)
    shares = lax.all_to_all(
        shares, "dp", 0, 0, tiled=True, axis_index_groups=Z_GROUPS
    )
    weight_grads = jnp.sum(shares.astype(F32), axis=0)

    own, other = feature_terms(place, grads, k_full, v_pieces, zones, tensor_count)
    other = swap_cores(other, tensor_count)
    share = own.shape[0] * 2 // tensor_count
    pairs = [
        own[s * share : (s + 1) * share].astype(F32)
        + other[s * share : (s + 1) * share].astype(F32)
        for s in range(tensor_count // 2)
    ]
    grad_features = pairs[0]
    for s in range(1, tensor_count // 2):
        grad_features = grad_features + lax.ppermute(
            pairs[s].astype(BF16),
            "tensor",
            [(t, (t + 2 * s) % tensor_count) for t in range(tensor_count)],
        ).astype(F32)
    grad_features = grad_features.astype(BF16).reshape(images, tokens // tensor_count, width)
    return (
        attended,
        grad_queries,
        grad_features,
        weight_grads[:, :head_dim],
        weight_grads[:, head_dim:],
    )


def solution(mesh):
    in_specs = (
        P("dp", "tensor"),
        P("dp", None, None),
        P("dp", "tensor"),
        P("dp", "tensor"),
        P(),
        P(),
        P(),
        P(),
        P("dp", "tensor"),
    )
    out_specs = (
        P("dp", "tensor"),
        P("dp", "tensor"),
        P("dp", "tensor", None),
        P("dp", "tensor"),
        P("dp", "tensor"),
    )
    return jax.shard_map(local, mesh=mesh, in_specs=in_specs, out_specs=out_specs, check_vma=False)
```

```python
import functools

import jax
import jax.numpy as jnp
from jax import lax
from jax.experimental import pallas as pl
from jax.experimental.pallas import tpu as pltpu
from jax.sharding import PartitionSpec as P

TILES = 4
EPS = 1e-05
MASKED_SCORE = -1e30
NY, NZ = 4, 8
Y_GROUPS = [[y * NZ + z for y in range(NY)] for z in range(NZ)]
Z_GROUPS = [[y * NZ + z for z in range(NZ)] for y in range(NY)]
BF16, F32 = jnp.bfloat16, jnp.float32
MIB = 1024 * 1024
GROUP = 4
POS, OWNER, VALID, FIRST, PLACE = range(5)


def dot_dims(a, b, a_dim, b_dim):
    return lax.dot_general(
        a, b, (((a_dim,), (b_dim,)), ((), ())), preferred_element_type=F32
    )


def limit(mib):
    return pltpu.CompilerParams(vmem_limit_bytes=mib * MIB)


def cost(flops, mib):
    return pl.CostEstimate(flops=flops, bytes_accessed=mib * MIB, transcendentals=0)


def in_vmem():
    return pl.BlockSpec(memory_space=pltpu.VMEM)


def in_hbm():
    return pl.BlockSpec(memory_space=pltpu.HBM)


def park_kernel(x_ref, out_ref, sem):
    copy = pltpu.make_async_copy(x_ref, out_ref, sem)
    copy.start()
    copy.wait()


def park(x):
    return pl.pallas_call(
        park_kernel,
        in_specs=[in_hbm()],
        out_specs=in_vmem(),
        out_shape=pltpu.VMEM(x.shape, x.dtype),
        scratch_shapes=[pltpu.SemaphoreType.DMA],
        compiler_params=limit(6),
        cost_estimate=cost(0, 8),
        name="park",
    )(x)


def weight_blocks(table_ref, w_refs, zones):
    for ref, (offset, y_from, y_count) in zip(w_refs, zones):
        z = lax.rem(table_ref[PLACE, 1] + offset, NZ)
        block = ref.shape[0] // y_count
        for i in range(y_count):
            y = lax.rem(table_ref[PLACE, 0] + y_from + i, NY)
            at = pl.multiple_of((y * NZ + z) * block, block)
            yield pl.ds(at, block), ref[i * block : (i + 1) * block, :]


def project_kernel(table_ref, f_ref, *refs, zones):
    w_refs, (gain_ref, send_ref, raw_ref, kv, sems) = refs[: len(zones)], refs[len(zones) :]
    head_dim = gain_ref.shape[1]
    tokens = send_ref.shape[1]
    total = jnp.zeros((f_ref.shape[0], 2 * head_dim), F32)
    for cols, w in weight_blocks(table_ref, w_refs, zones):
        total = total + jnp.dot(f_ref[:, cols], w[...], preferred_element_type=F32)
    raw = total[:, :head_dim]
    scale = lax.rsqrt(jnp.mean(raw * raw, axis=-1, keepdims=True) + EPS)
    keys = (raw * scale * gain_ref[...]).astype(BF16)
    values = total[:, head_dim:].astype(BF16)
    for i in range(kv.shape[0]):
        kv[i, :, :head_dim] = keys[i * tokens : (i + 1) * tokens]
        kv[i, :, head_dim:] = values[i * tokens : (i + 1) * tokens]
    copies = [
        pltpu.make_async_copy(
            kv.at[jnp.maximum(table_ref[POS, d], 0)], send_ref.at[d], sems.at[d]
        )
        for d in range(send_ref.shape[0])
    ]
    for copy in copies:
        copy.start()
    raw_ref[...] = raw
    for copy in copies:
        copy.wait()


def project(table, rows, pieces, zones, gain, dp, images, tokens):
    cols = 2 * gain.shape[1]
    return pl.pallas_call(
        functools.partial(project_kernel, zones=zones),
        grid_spec=pltpu.PrefetchScalarGridSpec(
            num_scalar_prefetch=1,
            grid=(),
            in_specs=[in_vmem()] * (2 + len(pieces)),
            out_specs=[in_hbm(), in_vmem()],
            scratch_shapes=[
                pltpu.VMEM((images, tokens, cols), BF16),
                pltpu.SemaphoreType.DMA((dp,)),
            ],
        ),
        out_shape=[
            pltpu.HBM((dp, tokens, cols), BF16),
            pltpu.HBM((rows.shape[0], cols // 2), F32),
        ],
        compiler_params=limit(12),
        cost_estimate=cost(2 * rows.size * cols, 10),
        name="project",
    )(table, rows, *pieces, gain)


def load_heads(ref, start, rows, head_dim):
    heads = ref.shape[1] // head_dim
    return jnp.concatenate(
        [ref[start : start + rows, g * head_dim : (g + 1) * head_dim] for g in range(heads)],
        axis=0,
    )


def store_heads(ref, start, rows, head_dim, full):
    for g in range(ref.shape[1] // head_dim):
        ref[start : start + rows, g * head_dim : (g + 1) * head_dim] = full[
            g * rows : (g + 1) * rows
        ]


def attend_kernel(table_ref, q_ref, ct_ref, kv_ref, part_ref, probs_ref, ds_ref, acc):
    step = pl.program_id(0)
    rows = q_ref.shape[0] // GROUP
    head_dim = kv_ref.shape[2] // 2
    tokens = kv_ref.shape[1]
    scale = head_dim**-0.5

    @pl.when(step == 0)
    def _():
        part_ref[...] = jnp.zeros_like(part_ref)
        acc[...] = jnp.zeros_like(acc)

    at = [step * GROUP + i for i in range(GROUP)]
    owners = [table_ref[OWNER, b] for b in at]
    queries = [load_heads(q_ref, i * rows, rows, head_dim) for i in range(GROUP)]
    grads = [load_heads(ct_ref, i * rows, rows, head_dim) for i in range(GROUP)]
    scores = [
        dot_dims(kv_ref[o, :, :head_dim], q, 1, 1) * scale for o, q in zip(owners, queries)
    ]
    d_probs = [dot_dims(kv_ref[o, :, head_dim:], g, 1, 1) for o, g in zip(owners, grads)]
    token = lax.broadcasted_iota(jnp.int32, (tokens, 1), 0)
    scores = [
        jnp.where(token < table_ref[VALID, b], s, MASKED_SCORE) for b, s in zip(at, scores)
    ]
    weights = [jnp.exp(s - jnp.max(s, axis=0, keepdims=True)) for s in scores]
    probs = [w * (1.0 / jnp.sum(w, axis=0, keepdims=True)) for w in weights]
    halves = [p.astype(BF16) for p in probs]
    deltas = [jnp.sum(p * d, axis=0, keepdims=True) for p, d in zip(probs, d_probs)]
    d_scores = [
        (p * (d - x) * scale).astype(BF16) for p, d, x in zip(probs, d_probs, deltas)
    ]
    key_parts = [jnp.dot(d, q, preferred_element_type=F32) for d, q in zip(d_scores, queries)]
    value_parts = [jnp.dot(p, g, preferred_element_type=F32) for p, g in zip(halves, grads)]
    key_run, value_run = acc[:, :head_dim], acc[:, head_dim:]
    for i, b in enumerate(at):
        keep = table_ref[FIRST, b] == 0
        key_run = key_parts[i] + jnp.where(keep, key_run, 0.0)
        value_run = value_parts[i] + jnp.where(keep, value_run, 0.0)
        part_ref[owners[i], :, :head_dim] = key_run.astype(BF16)
        part_ref[owners[i], :, head_dim:] = value_run.astype(BF16)
        probs_ref[i] = halves[i]
        ds_ref[i] = d_scores[i]
    acc[:, :head_dim] = key_run
    acc[:, head_dim:] = value_run


def attend(table, queries, cotangent, kv):
    blocks, (_, tokens, cols) = table.shape[1], kv.shape
    rows = queries.size * 2 // (blocks * cols)
    steps = blocks // GROUP
    text = pl.BlockSpec((queries.shape[0] // steps, queries.shape[1]), lambda i, t: (i, 0))
    whole = pl.BlockSpec(kv.shape, lambda i, t: (0, 0, 0))
    stash = pl.BlockSpec((GROUP, tokens, rows), lambda i, t: (i, 0, 0))
    stash_shape = pltpu.HBM((blocks, tokens, rows), BF16)
    return pl.pallas_call(
        attend_kernel,
        grid_spec=pltpu.PrefetchScalarGridSpec(
            num_scalar_prefetch=1,
            grid=(steps,),
            in_specs=[text, text, whole],
            out_specs=[whole, stash, stash],
            scratch_shapes=[pltpu.VMEM(kv.shape[1:], F32)],
        ),
        out_shape=[pltpu.HBM(kv.shape, BF16), stash_shape, stash_shape],
        compiler_params=limit(14),
        cost_estimate=cost(8 * queries.size * tokens, 8),
        name="attend",
    )(table, *hold(queries, cotangent, kv))


def hold(*arrays):
    return [pltpu.with_memory_space_constraint(x, pltpu.HBM) for x in arrays]


def apply_kernel(table_ref, kv_ref, probs_ref, ds_ref, out_ref, gq_ref):
    step = pl.program_id(0)
    rows = out_ref.shape[0] // GROUP
    head_dim = kv_ref.shape[2] // 2
    owners = [table_ref[OWNER, step * GROUP + i] for i in range(GROUP)]
    outs = [
        dot_dims(probs_ref[i], kv_ref[o, :, head_dim:], 0, 0) for i, o in enumerate(owners)
    ]
    gqs = [dot_dims(ds_ref[i], kv_ref[o, :, :head_dim], 0, 0) for i, o in enumerate(owners)]
    for i in range(GROUP):
        store_heads(out_ref, i * rows, rows, head_dim, outs[i].astype(BF16))
        store_heads(gq_ref, i * rows, rows, head_dim, gqs[i].astype(BF16))


def apply(table, kv, probs, d_scores, shape):
    steps = table.shape[1] // GROUP
    text = pl.BlockSpec((shape[0] // steps, shape[1]), lambda i, t: (i, 0))
    whole = pl.BlockSpec(kv.shape, lambda i, t: (0, 0, 0))
    stash = pl.BlockSpec((GROUP,) + probs.shape[1:], lambda i, t: (i, 0, 0))
    out = pltpu.HBM(shape, BF16)
    return pl.pallas_call(
        apply_kernel,
        grid_spec=pltpu.PrefetchScalarGridSpec(
            num_scalar_prefetch=1,
            grid=(steps,),
            in_specs=[whole, stash, stash],
            out_specs=[text, text],
        ),
        out_shape=[out, out],
        compiler_params=limit(10),
        cost_estimate=cost(4 * shape[0] * shape[1] * kv.shape[1], 6),
        name="apply",
    )(table, *hold(kv, probs, d_scores))


def owner_kernel(table_ref, part_ref, raw_ref, gain_ref, grad_ref, line_ref, acc):
    step = pl.program_id(0)
    head_dim = gain_ref.shape[1]
    count, tokens = part_ref.shape[:2]

    @pl.when(step == 0)
    def _():
        acc[...] = jnp.zeros_like(acc)

    for d in range(count):
        pos = table_ref[POS, step * count + d]

        @pl.when(pos >= 0)
        def _():
            acc[pos] += part_ref[d].astype(F32)

    @pl.when(step == pl.num_programs(0) - 1)
    def _():
        gain = gain_ref[...]
        for i in range(acc.shape[0]):
            here = slice(i * tokens, (i + 1) * tokens)
            raw = raw_ref[here]
            scale = lax.rsqrt(jnp.mean(raw * raw, axis=-1, keepdims=True) + EPS)
            scaled = acc[i, :, :head_dim] * gain
            pull = jnp.mean(raw * scaled, axis=-1, keepdims=True)
            grad = scale * scaled - raw * (scale * scale * scale * pull)
            grad_ref[here, :head_dim] = grad.astype(BF16)
            grad_ref[here, head_dim:] = acc[i, :, head_dim:].astype(BF16)
        for i in range(acc.shape[0]):
            at = pl.multiple_of(lax.rem(table_ref[PLACE, 3] + i, 2) * tokens, tokens)
            half = grad_ref[pl.ds(at, tokens), :]
            for y in range(NY):
                line_ref[y, i * tokens : (i + 1) * tokens, :] = half


def owner_grads(table, parts, raw, gain, images):
    dp, tokens, cols = parts.shape
    count = dp // 4
    return pl.pallas_call(
        owner_kernel,
        grid_spec=pltpu.PrefetchScalarGridSpec(
            num_scalar_prefetch=1,
            grid=(dp // count,),
            in_specs=[
                pl.BlockSpec((count, tokens, cols), lambda i, t: (i, 0, 0)),
                pl.BlockSpec(raw.shape, lambda i, t: (0, 0)),
                pl.BlockSpec(gain.shape, lambda i, t: (0, 0)),
            ],
            out_specs=[
                pl.BlockSpec((images * tokens, cols), lambda i, t: (0, 0)),
                pl.BlockSpec((NY, images * tokens, cols), lambda i, t: (0, 0, 0)),
            ],
            scratch_shapes=[pltpu.VMEM((images, tokens, cols), F32)],
        ),
        out_shape=[
            jax.ShapeDtypeStruct((images * tokens, cols), BF16),
            pltpu.HBM((NY, images * tokens, cols), BF16),
        ],
        compiler_params=limit(6),
        cost_estimate=cost(0, 3),
        name="owner_grads",
    )(table, *hold(parts, raw), gain)


def transpose_kernel(*refs):
    pieces, out_ref = refs[:-1], refs[-1]
    tokens = pieces[0].shape[0]
    for i, ref in enumerate(pieces):
        out_ref[:, i * tokens : (i + 1) * tokens] = ref[...].T


def transpose_pieces(pieces):
    tokens, width = pieces[0].shape
    return pl.pallas_call(
        transpose_kernel,
        in_specs=[in_vmem()] * len(pieces),
        out_specs=in_vmem(),
        out_shape=jax.ShapeDtypeStruct((width, tokens * len(pieces)), BF16),
        compiler_params=limit(7),
        cost_estimate=cost(0, 4),
        name="transpose_pieces",
    )(*pieces)


def weight_kernel(table_ref, own_ref, other_ref, line_ref, out_ref):
    half = line_ref.shape[1] // 2
    lines = [lax.rem(table_ref[PLACE, 0] + NY - s, NY) for s in range(NY)]
    first = jnp.concatenate([line_ref[y, :half, :] for y in lines], axis=0)
    second = jnp.concatenate([line_ref[y, half:, :] for y in lines], axis=0)
    block = out_ref.shape[1]
    for i in range(out_ref.shape[0]):
        here = slice(i * block, (i + 1) * block)
        total = jnp.dot(own_ref[here, :], first, preferred_element_type=F32)
        total = total + jnp.dot(other_ref[here, :], second, preferred_element_type=F32)
        out_ref[i] = total.astype(BF16)


def weight_terms(table, own_cols, other_cols, line):
    width, cols = own_cols.shape[0], line.shape[2]
    return pl.pallas_call(
        weight_kernel,
        grid_spec=pltpu.PrefetchScalarGridSpec(
            num_scalar_prefetch=1,
            grid=(),
            in_specs=[in_vmem()] * 3,
            out_specs=in_vmem(),
        ),
        out_shape=pltpu.HBM((NZ, width // NZ, cols), BF16),
        compiler_params=limit(9),
        cost_estimate=cost(4 * own_cols.size * cols, 6),
        name="weight_terms",
    )(table, own_cols, other_cols, line)


def feature_kernel(table_ref, grad_ref, *refs, zones, targets):
    w_refs, (own_ref, other_ref, lhs) = refs[: len(zones)], refs[len(zones) :]
    half = own_ref.shape[0]
    chips = targets // 2
    tokens = grad_ref.shape[0] // 2
    share = tokens // targets
    for core in range(2):
        for chip in range(chips):
            x = lax.rem(table_ref[PLACE, 2] + chip, chips)
            target = x * 2 + lax.rem(table_ref[PLACE, 3] + core, 2)
            for i in range(2):
                at = pl.multiple_of(i * tokens + target * share, share)
                to = ((core * chips + chip) * 2 + i) * share
                lhs[to : to + share, :] = grad_ref[pl.ds(at, share), :]
    for cols, w in weight_blocks(table_ref, w_refs, zones):
        part = dot_dims(lhs[...], w[...], 1, 1).astype(BF16)
        own_ref[:, cols] = part[:half]
        other_ref[:, cols] = part[half:]


def feature_terms(table, grads, pieces, zones, width, targets):
    half = jax.ShapeDtypeStruct((grads.shape[0] // 2, width), BF16)
    return pl.pallas_call(
        functools.partial(feature_kernel, zones=zones, targets=targets),
        grid_spec=pltpu.PrefetchScalarGridSpec(
            num_scalar_prefetch=1,
            grid=(),
            in_specs=[in_vmem()] * (1 + len(pieces)),
            out_specs=[in_vmem()] * 2,
            scratch_shapes=[pltpu.VMEM(grads.shape, BF16)],
        ),
        out_shape=[half, half],
        compiler_params=limit(13),
        cost_estimate=cost(4 * half.size * grads.shape[1], 8),
        name="feature_terms",
    )(table, grads, *pieces)


def shift_y(x, by):
    if by == 0:
        return x
    pairs = [(y * NZ + z, (y + by) % NY * NZ + z) for y in range(NY) for z in range(NZ)]
    return lax.ppermute(x, "dp", pairs)


def shift_z(x, by):
    pairs = [(y * NZ + z, y * NZ + (z + by) % NZ) for y in range(NY) for z in range(NZ)]
    return lax.ppermute(x, "dp", pairs)


def ring_z(x):
    half = x.shape[0] // 2
    pieces, zones = [x], [(0, 0, NY)]
    below = above = x
    for hop in range(1, NZ // 2):
        below, above = shift_z(below, 1), shift_z(above, -1)
        pieces += [below, above]
        zones += [(NZ - hop, 0, NY), (hop, 0, NY)]
    pieces += [shift_z(below[:half], 1), shift_z(above[half:], -1)]
    zones += [(NZ // 2, 0, NY // 2), (NZ // 2, NY // 2, NY // 2)]
    return pieces, zones


def swap_cores(x, count):
    return lax.ppermute(x, "tensor", [(t, t ^ 1) for t in range(count)])


def local(
    queries, features, k_weight, v_weight, k_gain, block_image, image_slot, image_tiles, cotangent
):
    dp_count = lax.axis_size("dp")
    tensor_count = lax.axis_size("tensor")
    me = lax.axis_index("dp")
    images, tokens, width = features.shape
    head_dim = k_gain.shape[0]
    rows = features.reshape(images * tokens, width)
    gain = k_gain.reshape(1, head_dim)
    my_y, my_z = me // NZ, lax.rem(me, NZ)
    tensor = lax.axis_index("tensor")
    core = lax.rem(tensor, 2)

    image_ids = lax.broadcasted_iota(jnp.int32, (1, image_slot.shape[0]), 1)
    id_match = block_image[:, None] == image_ids
    slots = jnp.sum(jnp.where(id_match, image_slot[None, :], 0), axis=1).reshape(dp_count, -1)
    tiles = jnp.sum(jnp.where(id_match, image_tiles[None, :], 0), axis=1).reshape(dp_count, -1)
    my_slots = lax.dynamic_index_in_dim(slots, me, 0, keepdims=False)
    my_tiles = lax.dynamic_index_in_dim(tiles, me, 0, keepdims=False)
    first = jnp.concatenate(
        [jnp.ones((1,), jnp.int32), (my_slots[1:] != my_slots[:-1]).astype(jnp.int32)]
    )
    pos = jnp.max(jnp.where(slots // images == me, slots % images, -1), axis=1)
    place = jnp.stack([my_y, my_z, tensor // 2, core])
    place = jnp.pad(place, (0, pos.shape[0] - place.shape[0]))
    table = jnp.stack([pos, my_slots // images, my_tiles * (tokens // TILES), first, place])

    block = jnp.concatenate([k_weight, v_weight], axis=1)
    line = jnp.concatenate([shift_y(block, (NY - i) % NY) for i in range(NY)])
    rows_near, line = lax.optimization_barrier((park(rows), line))
    pieces, zones = ring_z(line)

    send, raw = project(table, rows_near, pieces, zones, gain, dp_count, images, tokens)
    kv = lax.all_to_all(send, "dp", 0, 0, tiled=True)

    rows_later, _ = lax.optimization_barrier((features, raw))
    span = width // NY
    col_pieces = [
        shift_y(
            lax.dynamic_slice(
                rows_later, (core, 0, (my_y + s) % NY * span), (1, tokens, span)
            )[0],
            s,
        )
        for s in range(NY)
    ]

    parts, probs, d_scores = attend(table, queries, cotangent, kv)
    parts, col_pieces = lax.optimization_barrier((parts, col_pieces))
    parts = lax.all_to_all(parts, "dp", 0, 0, tiled=True)
    own_cols = transpose_pieces(col_pieces)
    other_cols = swap_cores(own_cols, tensor_count)
    attended, grad_queries = apply(table, kv, probs, d_scores, queries.shape)
    parts, other_cols, attended, grad_queries = lax.optimization_barrier(
        (parts, other_cols, attended, grad_queries)
    )
    grads, line_grads = owner_grads(table, parts, raw, gain, images)

    line_grads = lax.all_to_all(
        line_grads, "dp", 0, 0, tiled=True, axis_index_groups=Y_GROUPS
    )
    shares = weight_terms(table, own_cols, other_cols, line_grads)
    shares = lax.all_to_all(shares, "dp", 0, 0, tiled=True, axis_index_groups=Z_GROUPS)

    own, other = feature_terms(table, grads, pieces, zones, width, tensor_count)
    other = swap_cores(other, tensor_count)
    share = own.shape[0] * 2 // tensor_count
    pairs = [
        own[s * share : (s + 1) * share].astype(F32)
        + other[s * share : (s + 1) * share].astype(F32)
        for s in range(tensor_count // 2)
    ]
    grad_features = pairs[0]
    for s in range(1, tensor_count // 2):
        grad_features = grad_features + lax.ppermute(
            pairs[s].astype(BF16),
            "tensor",
            [(t, (t + 2 * s) % tensor_count) for t in range(tensor_count)],
        ).astype(F32)
    grad_features = grad_features.astype(BF16).reshape(images, tokens // tensor_count, width)
    shares, grad_features = lax.optimization_barrier((shares, grad_features))
    weight_grads = jnp.sum(shares.astype(F32), axis=0)
    return (
        attended,
        grad_queries,
        grad_features,
        weight_grads[:, :head_dim],
        weight_grads[:, head_dim:],
    )


def solution(mesh):
    in_specs = (
        P("dp", "tensor"),
        P("dp", None, None),
        P("dp", "tensor"),
        P("dp", "tensor"),
        P(),
        P(),
        P(),
        P(),
        P("dp", "tensor"),
    )
    out_specs = (
        P("dp", "tensor"),
        P("dp", "tensor"),
        P("dp", "tensor", None),
        P("dp", "tensor"),
        P("dp", "tensor"),
    )
    return jax.shard_map(local, mesh=mesh, in_specs=in_specs, out_specs=out_specs, check_vma=False)
```

```python
import functools

import jax
import jax.numpy as jnp
from jax import lax
from jax.experimental import pallas as pl
from jax.experimental.pallas import tpu as pltpu
from jax.sharding import PartitionSpec as P

TILES = 4
EPS = 1e-05
MASKED_SCORE = -1e30
NY, NZ = 4, 8
Y_GROUPS = [[y * NZ + z for y in range(NY)] for z in range(NZ)]
Z_GROUPS = [[y * NZ + z for z in range(NZ)] for y in range(NY)]
BF16, F32 = jnp.bfloat16, jnp.float32
MIB = 1024 * 1024
GROUP = 4
POS, OWNER, VALID, FIRST, PLACE = range(5)


def dot_dims(a, b, a_dim, b_dim):
    return lax.dot_general(
        a, b, (((a_dim,), (b_dim,)), ((), ())), preferred_element_type=F32
    )


def limit(mib):
    return pltpu.CompilerParams(vmem_limit_bytes=mib * MIB)


def cost(flops, mib):
    return pl.CostEstimate(flops=flops, bytes_accessed=mib * MIB, transcendentals=0)


def in_vmem():
    return pl.BlockSpec(memory_space=pltpu.VMEM)


def in_hbm():
    return pl.BlockSpec(memory_space=pltpu.HBM)


def weight_blocks(table_ref, kw_ref, vw_refs, zones):
    for ref, offset in zip(vw_refs, zones):
        z = lax.rem(table_ref[PLACE, 1] + offset, NZ)
        block = ref.shape[0] // NY
        for i in range(NY):
            y = lax.rem(table_ref[PLACE, 0] + i, NY)
            here = pl.ds(pl.multiple_of((y * NZ + z) * block, block), block)
            v = ref[i * block : (i + 1) * block, :]
            yield here, jnp.concatenate([kw_ref[here, :], v], axis=1)


def project_kernel(table_ref, f_ref, kw_ref, *refs, zones):
    vw_refs, (gain_ref, send_ref, raw_ref, kv) = refs[: len(zones)], refs[len(zones) :]
    head_dim = gain_ref.shape[1]
    tokens = send_ref.shape[1]
    total = jnp.zeros((f_ref.shape[0], 2 * head_dim), F32)
    for cols, w in weight_blocks(table_ref, kw_ref, vw_refs, zones):
        total = total + jnp.dot(f_ref[:, cols], w, preferred_element_type=F32)
    raw = total[:, :head_dim]
    raw_ref[...] = raw
    scale = lax.rsqrt(jnp.mean(raw * raw, axis=-1, keepdims=True) + EPS)
    keys = (raw * scale * gain_ref[...]).astype(BF16)
    values = total[:, head_dim:].astype(BF16)
    for i in range(kv.shape[0]):
        kv[i, :, :head_dim] = keys[i * tokens : (i + 1) * tokens]
        kv[i, :, head_dim:] = values[i * tokens : (i + 1) * tokens]

    def put(d, carry):
        send_ref[d] = kv[jnp.maximum(table_ref[POS, d], 0)]
        return carry

    lax.fori_loop(0, send_ref.shape[0], put, 0, unroll=4)


def project(table, rows, k_full, v_pieces, zones, gain, dp, images, tokens):
    cols = 2 * gain.shape[1]
    return pl.pallas_call(
        functools.partial(project_kernel, zones=zones),
        grid_spec=pltpu.PrefetchScalarGridSpec(
            num_scalar_prefetch=1,
            grid=(),
            in_specs=[in_vmem()] * (3 + len(v_pieces)),
            out_specs=[in_vmem()] * 2,
            scratch_shapes=[pltpu.VMEM((images, tokens, cols), BF16)],
        ),
        out_shape=[
            pltpu.HBM((dp, tokens, cols), BF16),
            pltpu.HBM((rows.shape[0], cols // 2), F32),
        ],
        compiler_params=limit(14),
        cost_estimate=cost(2 * rows.size * cols, 10),
        name="project",
    )(table, *hold(rows), k_full, *v_pieces, gain)


def load_heads(ref, start, rows, head_dim):
    heads = ref.shape[1] // head_dim
    return jnp.concatenate(
        [ref[pl.ds(start, rows), g * head_dim : (g + 1) * head_dim] for g in range(heads)],
        axis=0,
    )


def store_heads(ref, start, rows, head_dim, full):
    for g in range(ref.shape[1] // head_dim):
        ref[pl.ds(start, rows), g * head_dim : (g + 1) * head_dim] = full[
            g * rows : (g + 1) * rows
        ]


def attend_kernel(table_ref, q_ref, ct_ref, kv_ref, part_ref, probs_ref, ds_ref, acc):
    blocks = table_ref.shape[1]
    rows = q_ref.shape[0] // blocks
    head_dim = kv_ref.shape[2] // 2
    tokens = kv_ref.shape[1]
    scale = head_dim**-0.5
    part_ref[...] = jnp.zeros_like(part_ref)
    acc[...] = jnp.zeros_like(acc)

    def some_blocks(step, carry):
        at = [step * GROUP + i for i in range(GROUP)]
        owners = [table_ref[OWNER, b] for b in at]
        starts = [pl.multiple_of(b * rows, rows) for b in at]
        queries = [load_heads(q_ref, s, rows, head_dim) for s in starts]
        grads = [load_heads(ct_ref, s, rows, head_dim) for s in starts]
        scores = [
            dot_dims(kv_ref[o, :, :head_dim], q, 1, 1) * scale for o, q in zip(owners, queries)
        ]
        d_probs = [dot_dims(kv_ref[o, :, head_dim:], g, 1, 1) for o, g in zip(owners, grads)]
        token = lax.broadcasted_iota(jnp.int32, (tokens, 1), 0)
        scores = [
            jnp.where(token < table_ref[VALID, b], s, MASKED_SCORE) for b, s in zip(at, scores)
        ]
        weights = [jnp.exp(s - jnp.max(s, axis=0, keepdims=True)) for s in scores]
        probs = [w * (1.0 / jnp.sum(w, axis=0, keepdims=True)) for w in weights]
        halves = [p.astype(BF16) for p in probs]
        deltas = [jnp.sum(p * d, axis=0, keepdims=True) for p, d in zip(probs, d_probs)]
        d_scores = [
            (p * (d - x) * scale).astype(BF16) for p, d, x in zip(probs, d_probs, deltas)
        ]
        key_parts = [
            jnp.dot(d, q, preferred_element_type=F32) for d, q in zip(d_scores, queries)
        ]
        value_parts = [
            jnp.dot(p, g, preferred_element_type=F32) for p, g in zip(halves, grads)
        ]
        key_run, value_run = acc[:, :head_dim], acc[:, head_dim:]
        for i, b in enumerate(at):
            keep = table_ref[FIRST, b] == 0
            key_run = key_parts[i] + jnp.where(keep, key_run, 0.0)
            value_run = value_parts[i] + jnp.where(keep, value_run, 0.0)
            part_ref[owners[i], :, :head_dim] = key_run.astype(BF16)
            part_ref[owners[i], :, head_dim:] = value_run.astype(BF16)
            probs_ref[b] = halves[i]
            ds_ref[b] = d_scores[i]
        acc[:, :head_dim] = key_run
        acc[:, head_dim:] = value_run
        return carry

    lax.fori_loop(0, blocks // GROUP, some_blocks, 0)


def hold(*arrays):
    return [pltpu.with_memory_space_constraint(x, pltpu.HBM) for x in arrays]


def attend(table, queries, cotangent, kv):
    blocks, (_, tokens, cols) = table.shape[1], kv.shape
    rows = queries.size * 2 // (blocks * cols)
    stash = pltpu.HBM((blocks, tokens, rows), BF16)
    return pl.pallas_call(
        attend_kernel,
        grid_spec=pltpu.PrefetchScalarGridSpec(
            num_scalar_prefetch=1,
            grid=(),
            in_specs=[in_vmem()] * 3,
            out_specs=[in_vmem()] * 3,
            scratch_shapes=[pltpu.VMEM(kv.shape[1:], F32)],
        ),
        out_shape=[pltpu.HBM(kv.shape, BF16), stash, stash],
        compiler_params=limit(13),
        cost_estimate=cost(8 * queries.size * tokens, 8),
        name="attend",
    )(table, *hold(queries, cotangent, kv))


def apply_kernel(table_ref, kv_ref, probs_ref, ds_ref, out_ref, gq_ref):
    blocks = table_ref.shape[1]
    rows = out_ref.shape[0] // blocks
    head_dim = kv_ref.shape[2] // 2

    def some_blocks(step, carry):
        at = [step * GROUP + i for i in range(GROUP)]
        owners = [table_ref[OWNER, b] for b in at]
        outs = [
            dot_dims(probs_ref[b], kv_ref[o, :, head_dim:], 0, 0) for b, o in zip(at, owners)
        ]
        gqs = [dot_dims(ds_ref[b], kv_ref[o, :, :head_dim], 0, 0) for b, o in zip(at, owners)]
        for i, b in enumerate(at):
            start = pl.multiple_of(b * rows, rows)
            store_heads(out_ref, start, rows, head_dim, outs[i].astype(BF16))
            store_heads(gq_ref, start, rows, head_dim, gqs[i].astype(BF16))
        return carry

    lax.fori_loop(0, blocks // GROUP, some_blocks, 0)


def apply(table, kv, probs, d_scores, shape):
    out = pltpu.HBM(shape, BF16)
    return pl.pallas_call(
        apply_kernel,
        grid_spec=pltpu.PrefetchScalarGridSpec(
            num_scalar_prefetch=1,
            grid=(),
            in_specs=[in_vmem()] * 3,
            out_specs=[in_vmem()] * 2,
        ),
        out_shape=[out, out],
        compiler_params=limit(9),
        cost_estimate=cost(4 * shape[0] * shape[1] * kv.shape[1], 6),
        name="apply",
    )(table, *hold(kv, probs, d_scores))


def owner_kernel(table_ref, part_ref, raw_ref, gain_ref, grad_ref, by_core_ref, acc):
    head_dim = gain_ref.shape[1]
    tokens = part_ref.shape[1]
    acc[...] = jnp.zeros_like(acc)

    def add(d, carry):
        @pl.when(table_ref[POS, d] >= 0)
        def _():
            acc[table_ref[POS, d]] += part_ref[d].astype(F32)

        return carry

    lax.fori_loop(0, part_ref.shape[0], add, 0)
    gain = gain_ref[...]
    for i in range(acc.shape[0]):
        here = slice(i * tokens, (i + 1) * tokens)
        raw = raw_ref[here]
        scale = lax.rsqrt(jnp.mean(raw * raw, axis=-1, keepdims=True) + EPS)
        scaled = acc[i, :, :head_dim] * gain
        pull = jnp.mean(raw * scaled, axis=-1, keepdims=True)
        grad = scale * scaled - raw * (scale * scale * scale * pull)
        grad_ref[here, :head_dim] = grad.astype(BF16)
        grad_ref[here, head_dim:] = acc[i, :, head_dim:].astype(BF16)
    for i in range(acc.shape[0]):
        at = pl.multiple_of(lax.rem(table_ref[PLACE, 3] + i, 2) * tokens, tokens)
        by_core_ref[i * tokens : (i + 1) * tokens, :] = grad_ref[pl.ds(at, tokens), :]


def owner_grads(table, parts, raw, gain, images):
    tokens, cols = parts.shape[1:]
    grads = jax.ShapeDtypeStruct((images * tokens, cols), BF16)
    return pl.pallas_call(
        owner_kernel,
        grid_spec=pltpu.PrefetchScalarGridSpec(
            num_scalar_prefetch=1,
            grid=(),
            in_specs=[in_vmem()] * 3,
            out_specs=[in_vmem()] * 2,
            scratch_shapes=[pltpu.VMEM((images, tokens, cols), F32)],
        ),
        out_shape=[grads, grads],
        compiler_params=limit(6),
        cost_estimate=cost(0, 3),
        name="owner_grads",
    )(table, *hold(parts, raw), gain)


def transpose_kernel(*refs):
    pieces, out_ref = refs[:-1], refs[-1]
    tokens = pieces[0].shape[0]
    for i, ref in enumerate(pieces):
        out_ref[:, i * tokens : (i + 1) * tokens] = ref[...].T


def transpose_pieces(pieces):
    tokens, width = pieces[0].shape
    return pl.pallas_call(
        transpose_kernel,
        in_specs=[in_vmem()] * len(pieces),
        out_specs=in_vmem(),
        out_shape=jax.ShapeDtypeStruct((width, tokens * len(pieces)), BF16),
        compiler_params=limit(7),
        cost_estimate=cost(0, 4),
        name="transpose_pieces",
    )(*pieces)


def weight_kernel(own_ref, other_ref, *refs):
    lines, out_ref = refs[:-1], refs[-1]
    half = lines[0].shape[0] // 2
    first = jnp.concatenate([ref[:half, :] for ref in lines], axis=0)
    second = jnp.concatenate([ref[half:, :] for ref in lines], axis=0)
    block = out_ref.shape[1]
    for i in range(out_ref.shape[0]):
        here = slice(i * block, (i + 1) * block)
        total = jnp.dot(own_ref[here, :], first, preferred_element_type=F32)
        total = total + jnp.dot(other_ref[here, :], second, preferred_element_type=F32)
        out_ref[i] = total.astype(BF16)


def weight_terms(own_cols, other_cols, lines):
    width, cols = own_cols.shape[0], lines[0].shape[1]
    return pl.pallas_call(
        weight_kernel,
        in_specs=[in_vmem()] * (2 + len(lines)),
        out_specs=in_vmem(),
        out_shape=pltpu.HBM((NZ, width // NZ, cols), BF16),
        compiler_params=limit(9),
        cost_estimate=cost(4 * own_cols.size * cols, 6),
        name="weight_terms",
    )(own_cols, other_cols, *lines)


def feature_kernel(table_ref, grad_ref, kw_ref, *refs, zones, targets):
    vw_refs, (own_ref, other_ref, lhs) = refs[: len(zones)], refs[len(zones) :]
    half = own_ref.shape[0]
    chips = targets // 2
    tokens = grad_ref.shape[0] // 2
    share = tokens // targets
    for core in range(2):
        for chip in range(chips):
            x = lax.rem(table_ref[PLACE, 2] + chip, chips)
            target = x * 2 + lax.rem(table_ref[PLACE, 3] + core, 2)
            for i in range(2):
                at = pl.multiple_of(i * tokens + target * share, share)
                to = ((core * chips + chip) * 2 + i) * share
                lhs[to : to + share, :] = grad_ref[pl.ds(at, share), :]
    for cols, w in weight_blocks(table_ref, kw_ref, vw_refs, zones):
        part = dot_dims(lhs[...], w, 1, 1).astype(BF16)
        own_ref[:, cols] = part[:half]
        other_ref[:, cols] = part[half:]


def feature_terms(table, grads, k_full, v_pieces, zones, width, targets):
    half = jax.ShapeDtypeStruct((grads.shape[0] // 2, width), BF16)
    return pl.pallas_call(
        functools.partial(feature_kernel, zones=zones, targets=targets),
        grid_spec=pltpu.PrefetchScalarGridSpec(
            num_scalar_prefetch=1,
            grid=(),
            in_specs=[in_vmem()] * (2 + len(v_pieces)),
            out_specs=[in_vmem()] * 2,
            scratch_shapes=[pltpu.VMEM(grads.shape, BF16)],
        ),
        out_shape=[half, half],
        compiler_params=limit(13),
        cost_estimate=cost(4 * half.size * grads.shape[1], 8),
        name="feature_terms",
    )(table, grads, k_full, *v_pieces)


def shift_y(x, by):
    if by == 0:
        return x
    pairs = [(y * NZ + z, (y + by) % NY * NZ + z) for y in range(NY) for z in range(NZ)]
    return lax.ppermute(x, "dp", pairs)


def shift_z(x, by):
    pairs = [(y * NZ + z, y * NZ + (z + by) % NZ) for y in range(NY) for z in range(NZ)]
    return lax.ppermute(x, "dp", pairs)


def swap_cores(x, count):
    return lax.ppermute(x, "tensor", [(t, t ^ 1) for t in range(count)])


def local(
    queries, features, k_weight, v_weight, k_gain, block_image, image_slot, image_tiles, cotangent
):
    dp_count = lax.axis_size("dp")
    tensor_count = lax.axis_size("tensor")
    me = lax.axis_index("dp")
    images, tokens, width = features.shape
    head_dim = k_gain.shape[0]
    rows = features.reshape(images * tokens, width)
    gain = k_gain.reshape(1, head_dim)
    my_y, my_z = me // NZ, lax.rem(me, NZ)
    tensor = lax.axis_index("tensor")
    core = lax.rem(tensor, 2)

    image_ids = lax.broadcasted_iota(jnp.int32, (1, image_slot.shape[0]), 1)
    id_match = block_image[:, None] == image_ids
    slots = jnp.sum(jnp.where(id_match, image_slot[None, :], 0), axis=1).reshape(dp_count, -1)
    tiles = jnp.sum(jnp.where(id_match, image_tiles[None, :], 0), axis=1).reshape(dp_count, -1)
    my_slots = lax.dynamic_index_in_dim(slots, me, 0, keepdims=False)
    my_tiles = lax.dynamic_index_in_dim(tiles, me, 0, keepdims=False)
    first = jnp.concatenate(
        [jnp.ones((1,), jnp.int32), (my_slots[1:] != my_slots[:-1]).astype(jnp.int32)]
    )
    pos = jnp.max(jnp.where(slots // images == me, slots % images, -1), axis=1)
    place = jnp.stack([my_y, my_z, tensor // 2, core])
    place = jnp.pad(place, (0, pos.shape[0] - place.shape[0]))
    table = jnp.stack([pos, my_slots // images, my_tiles * (tokens // TILES), first, place])

    k_line = lax.all_to_all(
        jnp.broadcast_to(k_weight, (NZ,) + k_weight.shape),
        "dp", 0, 0, tiled=True, axis_index_groups=Z_GROUPS,
    )
    v_line = jnp.concatenate([shift_y(v_weight, (NY - i) % NY) for i in range(NY)])
    below, above = shift_z(v_line, 1), shift_z(v_line, -1)
    k_line, below, above, table = lax.optimization_barrier((k_line, below, above, table))
    k_full = lax.all_to_all(
        jnp.broadcast_to(k_line, (NY,) + k_line.shape),
        "dp", 0, 0, tiled=True, axis_index_groups=Y_GROUPS,
    ).reshape(width, head_dim)
    v_pieces, zones = [v_line], [0]
    for hop in range(1, NZ // 2):
        if hop > 1:
            below, above = shift_z(below, 1), shift_z(above, -1)
        v_pieces += [below, above]
        zones += [NZ - hop, hop]
    v_pieces += [shift_z(below, 1)]
    zones += [NZ // 2]

    send, raw = project(
        table, rows, k_full, v_pieces, zones, gain, dp_count, images, tokens
    )
    kv = lax.all_to_all(send, "dp", 0, 0, tiled=True)

    rows_later, _ = lax.optimization_barrier((features, raw))
    span = width // NY
    col_pieces = [
        shift_y(
            lax.dynamic_slice(
                rows_later, (core, 0, (my_y + s) % NY * span), (1, tokens, span)
            )[0],
            s,
        )
        for s in range(NY)
    ]

    parts, probs, d_scores = attend(table, queries, cotangent, kv)
    parts, col_pieces = lax.optimization_barrier((parts, col_pieces))
    parts = lax.all_to_all(parts, "dp", 0, 0, tiled=True)
    own_cols = transpose_pieces(col_pieces)
    other_cols = swap_cores(own_cols, tensor_count)
    attended, grad_queries = apply(table, kv, probs, d_scores, queries.shape)
    parts, other_cols, attended, grad_queries = lax.optimization_barrier(
        (parts, other_cols, attended, grad_queries)
    )
    grads, by_core = owner_grads(table, parts, raw, gain, images)

    lines = [shift_y(by_core, s) for s in range(NY)]
    shares = weight_terms(own_cols, other_cols, lines)
    shares = lax.all_to_all(shares, "dp", 0, 0, tiled=True, axis_index_groups=Z_GROUPS)

    grads, _ = lax.optimization_barrier((grads, lines))
    own, other = feature_terms(table, grads, k_full, v_pieces, zones, width, tensor_count)
    other = swap_cores(other, tensor_count)
    share = own.shape[0] * 2 // tensor_count
    pairs = [
        own[s * share : (s + 1) * share].astype(F32)
        + other[s * share : (s + 1) * share].astype(F32)
        for s in range(tensor_count // 2)
    ]
    grad_features = pairs[0]
    for s in range(1, tensor_count // 2):
        grad_features = grad_features + lax.ppermute(
            pairs[s].astype(BF16),
            "tensor",
            [(t, (t + 2 * s) % tensor_count) for t in range(tensor_count)],
        ).astype(F32)
    grad_features = grad_features.astype(BF16).reshape(images, tokens // tensor_count, width)
    shares, grad_features = lax.optimization_barrier((shares, grad_features))
    weight_grads = jnp.sum(shares.astype(F32), axis=0)
    return (
        attended,
        grad_queries,
        grad_features,
        weight_grads[:, :head_dim],
        weight_grads[:, head_dim:],
    )


def solution(mesh):
    in_specs = (
        P("dp", "tensor"),
        P("dp", None, None),
        P("dp", "tensor"),
        P("dp", "tensor"),
        P(),
        P(),
        P(),
        P(),
        P("dp", "tensor"),
    )
    out_specs = (
        P("dp", "tensor"),
        P("dp", "tensor"),
        P("dp", "tensor", None),
        P("dp", "tensor"),
        P("dp", "tensor"),
    )
    return jax.shard_map(local, mesh=mesh, in_specs=in_specs, out_specs=out_specs, check_vma=False)
```

```python
import functools

import jax
import jax.numpy as jnp
from jax import lax
from jax.experimental import pallas as pl
from jax.experimental.pallas import tpu as pltpu
from jax.sharding import PartitionSpec as P

TILES = 4
EPS = 1e-05
MASKED_SCORE = -1e30
NY, NZ = 4, 8
Y_GROUPS = [[y * NZ + z for y in range(NY)] for z in range(NZ)]
Z_GROUPS = [[y * NZ + z for z in range(NZ)] for y in range(NY)]
BF16, F32 = jnp.bfloat16, jnp.float32
MIB = 1024 * 1024
GROUP = 4
POS, OWNER, VALID, FIRST, PLACE = range(5)


def dot_dims(a, b, a_dim, b_dim):
    return lax.dot_general(
        a, b, (((a_dim,), (b_dim,)), ((), ())), preferred_element_type=F32
    )


def limit(mib):
    return pltpu.CompilerParams(vmem_limit_bytes=mib * MIB)


def cost(flops, mib):
    return pl.CostEstimate(flops=flops, bytes_accessed=mib * MIB, transcendentals=0)


def in_vmem():
    return pl.BlockSpec(memory_space=pltpu.VMEM)


def in_hbm():
    return pl.BlockSpec(memory_space=pltpu.HBM)


def weight_blocks(table_ref, w_refs, zones):
    spots = {}
    for n, blocks in enumerate(zones):
        for i, at in enumerate(blocks):
            size = w_refs[n].shape[0] // len(blocks)
            spots.setdefault(at, []).append((w_refs[n], slice(i * size, (i + 1) * size)))
    found = []
    for (y_off, z_off), spot in spots.items():
        y = lax.rem(table_ref[PLACE, 0] + y_off, NY)
        z = lax.rem(table_ref[PLACE, 1] + z_off, NZ)
        size = spot[0][1].stop - spot[0][1].start
        found.append((pl.ds(pl.multiple_of((y * NZ + z) * size, size), size), spot))
    return found


def side_by_side(spot):
    return jnp.concatenate([ref[rows, :] for ref, rows in spot], axis=1)


def project_kernel(table_ref, f_ref, *refs, zones):
    w_refs, (gain_ref, send_ref, raw_ref, kv, held, sems) = refs[: len(zones)], refs[len(zones) :]
    head_dim = gain_ref.shape[1]
    tokens = send_ref.shape[1]
    blocks = weight_blocks(table_ref, w_refs, zones)
    copies = [
        pltpu.make_async_copy(f_ref.at[:, cols], held.at[i], sems.at[i])
        for i, (cols, _) in enumerate(blocks)
    ]
    for copy in copies:
        copy.start()
    total = jnp.zeros((f_ref.shape[0], 2 * head_dim), F32)
    for i, (_, spot) in enumerate(blocks):
        copies[i].wait()
        total = total + jnp.dot(held[i], side_by_side(spot), preferred_element_type=F32)
    raw = total[:, :head_dim]
    raw_ref[...] = raw
    scale = lax.rsqrt(jnp.mean(raw * raw, axis=-1, keepdims=True) + EPS)
    keys = (raw * scale * gain_ref[...]).astype(BF16)
    values = total[:, head_dim:].astype(BF16)
    for i in range(kv.shape[0]):
        kv[i, :, :head_dim] = keys[i * tokens : (i + 1) * tokens]
        kv[i, :, head_dim:] = values[i * tokens : (i + 1) * tokens]

    def put(d, carry):
        send_ref[d] = kv[jnp.maximum(table_ref[POS, d], 0)]
        return carry

    lax.fori_loop(0, send_ref.shape[0], put, 0, unroll=4)


def project(table, rows, pieces, zones, gain, dp, images, tokens):
    cols = 2 * gain.shape[1]
    depth = rows.shape[1] // dp
    return pl.pallas_call(
        functools.partial(project_kernel, zones=zones),
        grid_spec=pltpu.PrefetchScalarGridSpec(
            num_scalar_prefetch=1,
            grid=(),
            in_specs=[in_hbm()] + [in_vmem()] * (1 + len(pieces)),
            out_specs=[in_vmem()] * 2,
            scratch_shapes=[
                pltpu.VMEM((images, tokens, cols), BF16),
                pltpu.VMEM((dp, rows.shape[0], depth), BF16),
                pltpu.SemaphoreType.DMA((dp,)),
            ],
        ),
        out_shape=[
            pltpu.HBM((dp, tokens, cols), BF16),
            pltpu.HBM((rows.shape[0], cols // 2), F32),
        ],
        compiler_params=limit(14),
        cost_estimate=cost(2 * rows.size * cols, 10),
        name="project",
    )(table, rows, *pieces, gain)


def load_heads(ref, start, rows, head_dim):
    heads = ref.shape[1] // head_dim
    return jnp.concatenate(
        [ref[pl.ds(start, rows), g * head_dim : (g + 1) * head_dim] for g in range(heads)],
        axis=0,
    )


def store_heads(ref, start, rows, head_dim, full):
    for g in range(ref.shape[1] // head_dim):
        ref[pl.ds(start, rows), g * head_dim : (g + 1) * head_dim] = full[
            g * rows : (g + 1) * rows
        ]


def attend_kernel(table_ref, q_ref, ct_ref, kv_ref, part_ref, probs_ref, ds_ref, acc):
    blocks = table_ref.shape[1]
    rows = q_ref.shape[0] // blocks
    head_dim = kv_ref.shape[2] // 2
    tokens = kv_ref.shape[1]
    scale = head_dim**-0.5
    part_ref[...] = jnp.zeros_like(part_ref)
    acc[...] = jnp.zeros_like(acc)

    def some_blocks(step, carry):
        at = [step * GROUP + i for i in range(GROUP)]
        owners = [table_ref[OWNER, b] for b in at]
        starts = [pl.multiple_of(b * rows, rows) for b in at]
        queries = [load_heads(q_ref, s, rows, head_dim) for s in starts]
        grads = [load_heads(ct_ref, s, rows, head_dim) for s in starts]
        scores = [
            dot_dims(kv_ref[o, :, :head_dim], q, 1, 1) * scale for o, q in zip(owners, queries)
        ]
        d_probs = [dot_dims(kv_ref[o, :, head_dim:], g, 1, 1) for o, g in zip(owners, grads)]
        token = lax.broadcasted_iota(jnp.int32, (tokens, 1), 0)
        scores = [
            jnp.where(token < table_ref[VALID, b], s, MASKED_SCORE) for b, s in zip(at, scores)
        ]
        weights = [jnp.exp(s - jnp.max(s, axis=0, keepdims=True)) for s in scores]
        probs = [w * (1.0 / jnp.sum(w, axis=0, keepdims=True)) for w in weights]
        halves = [p.astype(BF16) for p in probs]
        deltas = [jnp.sum(p * d, axis=0, keepdims=True) for p, d in zip(probs, d_probs)]
        d_scores = [
            (p * (d - x) * scale).astype(BF16) for p, d, x in zip(probs, d_probs, deltas)
        ]
        key_parts = [
            jnp.dot(d, q, preferred_element_type=F32) for d, q in zip(d_scores, queries)
        ]
        value_parts = [
            jnp.dot(p, g, preferred_element_type=F32) for p, g in zip(halves, grads)
        ]
        key_run, value_run = acc[:, :head_dim], acc[:, head_dim:]
        for i, b in enumerate(at):
            keep = table_ref[FIRST, b] == 0
            key_run = key_parts[i] + jnp.where(keep, key_run, 0.0)
            value_run = value_parts[i] + jnp.where(keep, value_run, 0.0)
            part_ref[owners[i], :, :head_dim] = key_run.astype(BF16)
            part_ref[owners[i], :, head_dim:] = value_run.astype(BF16)
            probs_ref[b] = halves[i]
            ds_ref[b] = d_scores[i]
        acc[:, :head_dim] = key_run
        acc[:, head_dim:] = value_run
        return carry

    lax.fori_loop(0, blocks // GROUP, some_blocks, 0)


def hold(*arrays):
    return [pltpu.with_memory_space_constraint(x, pltpu.HBM) for x in arrays]


def attend(table, queries, cotangent, kv):
    blocks, (_, tokens, cols) = table.shape[1], kv.shape
    rows = queries.size * 2 // (blocks * cols)
    stash = pltpu.HBM((blocks, tokens, rows), BF16)
    return pl.pallas_call(
        attend_kernel,
        grid_spec=pltpu.PrefetchScalarGridSpec(
            num_scalar_prefetch=1,
            grid=(),
            in_specs=[in_vmem()] * 3,
            out_specs=[in_vmem()] * 3,
            scratch_shapes=[pltpu.VMEM(kv.shape[1:], F32)],
        ),
        out_shape=[pltpu.HBM(kv.shape, BF16), stash, stash],
        compiler_params=limit(13),
        cost_estimate=cost(8 * queries.size * tokens, 8),
        name="attend",
    )(table, *hold(queries, cotangent, kv))


def apply_kernel(table_ref, kv_ref, probs_ref, ds_ref, out_ref, gq_ref):
    blocks = table_ref.shape[1]
    rows = out_ref.shape[0] // blocks
    head_dim = kv_ref.shape[2] // 2

    def some_blocks(step, carry):
        at = [step * GROUP + i for i in range(GROUP)]
        owners = [table_ref[OWNER, b] for b in at]
        outs = [
            dot_dims(probs_ref[b], kv_ref[o, :, head_dim:], 0, 0) for b, o in zip(at, owners)
        ]
        gqs = [dot_dims(ds_ref[b], kv_ref[o, :, :head_dim], 0, 0) for b, o in zip(at, owners)]
        for i, b in enumerate(at):
            start = pl.multiple_of(b * rows, rows)
            store_heads(out_ref, start, rows, head_dim, outs[i].astype(BF16))
            store_heads(gq_ref, start, rows, head_dim, gqs[i].astype(BF16))
        return carry

    lax.fori_loop(0, blocks // GROUP, some_blocks, 0)


def apply(table, kv, probs, d_scores, shape):
    out = pltpu.HBM(shape, BF16)
    return pl.pallas_call(
        apply_kernel,
        grid_spec=pltpu.PrefetchScalarGridSpec(
            num_scalar_prefetch=1,
            grid=(),
            in_specs=[in_vmem()] * 3,
            out_specs=[in_vmem()] * 2,
        ),
        out_shape=[out, out],
        compiler_params=limit(9),
        cost_estimate=cost(4 * shape[0] * shape[1] * kv.shape[1], 6),
        name="apply",
    )(table, *hold(kv, probs, d_scores))


def owner_kernel(table_ref, part_ref, raw_ref, gain_ref, grad_ref, by_core_ref, acc):
    head_dim = gain_ref.shape[1]
    tokens = part_ref.shape[1]
    acc[...] = jnp.zeros_like(acc)

    def add(d, carry):
        @pl.when(table_ref[POS, d] >= 0)
        def _():
            acc[table_ref[POS, d]] += part_ref[d].astype(F32)

        return carry

    lax.fori_loop(0, part_ref.shape[0], add, 0)
    gain = gain_ref[...]
    for i in range(acc.shape[0]):
        here = slice(i * tokens, (i + 1) * tokens)
        raw = raw_ref[here]
        scale = lax.rsqrt(jnp.mean(raw * raw, axis=-1, keepdims=True) + EPS)
        scaled = acc[i, :, :head_dim] * gain
        pull = jnp.mean(raw * scaled, axis=-1, keepdims=True)
        grad = scale * scaled - raw * (scale * scale * scale * pull)
        grad_ref[here, :head_dim] = grad.astype(BF16)
        grad_ref[here, head_dim:] = acc[i, :, head_dim:].astype(BF16)
    for i in range(acc.shape[0]):
        at = pl.multiple_of(lax.rem(table_ref[PLACE, 3] + i, 2) * tokens, tokens)
        by_core_ref[i * tokens : (i + 1) * tokens, :] = grad_ref[pl.ds(at, tokens), :]


def owner_grads(table, parts, raw, gain, images):
    tokens, cols = parts.shape[1:]
    grads = jax.ShapeDtypeStruct((images * tokens, cols), BF16)
    return pl.pallas_call(
        owner_kernel,
        grid_spec=pltpu.PrefetchScalarGridSpec(
            num_scalar_prefetch=1,
            grid=(),
            in_specs=[in_vmem()] * 3,
            out_specs=[in_vmem()] * 2,
            scratch_shapes=[pltpu.VMEM((images, tokens, cols), F32)],
        ),
        out_shape=[grads, grads],
        compiler_params=limit(6),
        cost_estimate=cost(0, 3),
        name="owner_grads",
    )(table, *hold(parts, raw), gain)


def transpose_kernel(*refs):
    pieces, out_ref = refs[:-1], refs[-1]
    tokens = pieces[0].shape[0]
    for i, ref in enumerate(pieces):
        out_ref[:, i * tokens : (i + 1) * tokens] = ref[...].T


def transpose_pieces(pieces):
    tokens, width = pieces[0].shape
    return pl.pallas_call(
        transpose_kernel,
        in_specs=[in_vmem()] * len(pieces),
        out_specs=in_vmem(),
        out_shape=jax.ShapeDtypeStruct((width, tokens * len(pieces)), BF16),
        compiler_params=limit(7),
        cost_estimate=cost(0, 4),
        name="transpose_pieces",
    )(*pieces)


def weight_kernel(own_ref, other_ref, *refs):
    lines, out_ref = refs[:-1], refs[-1]
    half = lines[0].shape[0] // 2
    first = jnp.concatenate([ref[:half, :] for ref in lines], axis=0)
    second = jnp.concatenate([ref[half:, :] for ref in lines], axis=0)
    block = out_ref.shape[1]
    for i in range(out_ref.shape[0]):
        here = slice(i * block, (i + 1) * block)
        total = jnp.dot(own_ref[here, :], first, preferred_element_type=F32)
        total = total + jnp.dot(other_ref[here, :], second, preferred_element_type=F32)
        out_ref[i] = total.astype(BF16)


def weight_terms(own_cols, other_cols, lines):
    width, cols = own_cols.shape[0], lines[0].shape[1]
    return pl.pallas_call(
        weight_kernel,
        in_specs=[in_vmem()] * (2 + len(lines)),
        out_specs=in_vmem(),
        out_shape=pltpu.HBM((NZ, width // NZ, cols), BF16),
        compiler_params=limit(9),
        cost_estimate=cost(4 * own_cols.size * cols, 6),
        name="weight_terms",
    )(own_cols, other_cols, *lines)


def feature_kernel(table_ref, grad_ref, *refs, zones, targets):
    w_refs, (own_ref, other_ref, lhs) = refs[: len(zones)], refs[len(zones) :]
    half = own_ref.shape[0]
    chips = targets // 2
    tokens = grad_ref.shape[0] // 2
    share = tokens // targets
    for core in range(2):
        for chip in range(chips):
            x = lax.rem(table_ref[PLACE, 2] + chip, chips)
            target = x * 2 + lax.rem(table_ref[PLACE, 3] + core, 2)
            for i in range(2):
                at = pl.multiple_of(i * tokens + target * share, share)
                to = ((core * chips + chip) * 2 + i) * share
                lhs[to : to + share, :] = grad_ref[pl.ds(at, share), :]
    for cols, spot in weight_blocks(table_ref, w_refs, zones):
        part = dot_dims(lhs[...], side_by_side(spot), 1, 1).astype(BF16)
        own_ref[:, cols] = part[:half]
        other_ref[:, cols] = part[half:]


def feature_terms(table, grads, pieces, zones, width, targets):
    half = jax.ShapeDtypeStruct((grads.shape[0] // 2, width), BF16)
    return pl.pallas_call(
        functools.partial(feature_kernel, zones=zones, targets=targets),
        grid_spec=pltpu.PrefetchScalarGridSpec(
            num_scalar_prefetch=1,
            grid=(),
            in_specs=[in_vmem()] * (1 + len(pieces)),
            out_specs=[in_vmem()] * 2,
            scratch_shapes=[pltpu.VMEM(grads.shape, BF16)],
        ),
        out_shape=[half, half],
        compiler_params=limit(13),
        cost_estimate=cost(4 * half.size * grads.shape[1], 8),
        name="feature_terms",
    )(table, grads, *pieces)


def shift_y(x, by):
    if by == 0:
        return x
    pairs = [(y * NZ + z, (y + by) % NY * NZ + z) for y in range(NY) for z in range(NZ)]
    return lax.ppermute(x, "dp", pairs)


def shift_z(x, by):
    pairs = [(y * NZ + z, y * NZ + (z + by) % NZ) for y in range(NY) for z in range(NZ)]
    return lax.ppermute(x, "dp", pairs)


def ring_z(x, blocks):
    pieces, zones = [x], [blocks]
    below = above = x
    for hop in range(1, NZ // 2):
        below, above = shift_z(below, 1), shift_z(above, -1)
        pieces += [below, above]
        zones += [[(y, off) for y, _ in blocks] for off in (NZ - hop, hop)]
    pieces += [shift_z(below, 1)]
    zones += [[(y, NZ // 2) for y, _ in blocks]]
    return pieces, zones


def swap_cores(x, count):
    return lax.ppermute(x, "tensor", [(t, t ^ 1) for t in range(count)])


def local(
    queries, features, k_weight, v_weight, k_gain, block_image, image_slot, image_tiles, cotangent
):
    dp_count = lax.axis_size("dp")
    tensor_count = lax.axis_size("tensor")
    me = lax.axis_index("dp")
    images, tokens, width = features.shape
    head_dim = k_gain.shape[0]
    rows = features.reshape(images * tokens, width)
    gain = k_gain.reshape(1, head_dim)
    my_y, my_z = me // NZ, lax.rem(me, NZ)
    tensor = lax.axis_index("tensor")
    core = lax.rem(tensor, 2)

    image_ids = lax.broadcasted_iota(jnp.int32, (1, image_slot.shape[0]), 1)
    id_match = block_image[:, None] == image_ids
    slots = jnp.sum(jnp.where(id_match, image_slot[None, :], 0), axis=1).reshape(dp_count, -1)
    tiles = jnp.sum(jnp.where(id_match, image_tiles[None, :], 0), axis=1).reshape(dp_count, -1)
    my_slots = lax.dynamic_index_in_dim(slots, me, 0, keepdims=False)
    my_tiles = lax.dynamic_index_in_dim(tiles, me, 0, keepdims=False)
    first = jnp.concatenate(
        [jnp.ones((1,), jnp.int32), (my_slots[1:] != my_slots[:-1]).astype(jnp.int32)]
    )
    pos = jnp.max(jnp.where(slots // images == me, slots % images, -1), axis=1)
    place = jnp.stack([my_y, my_z, tensor // 2, core])
    place = jnp.pad(place, (0, pos.shape[0] - place.shape[0]))
    table = jnp.stack([pos, my_slots // images, my_tiles * (tokens // TILES), first, place])

    v_line = jnp.concatenate([shift_y(v_weight, (NY - i) % NY) for i in range(NY)])
    k_ring, k_zones = ring_z(k_weight, [(0, 0)])
    v_ring, v_zones = ring_z(v_line, [(i, 0) for i in range(NY)])
    k_line = jnp.concatenate(k_ring)
    half = k_line.shape[0] // 2
    after, before = shift_y(k_line, -1), shift_y(k_line, 1)
    pieces = [k_line, after, before, shift_y(after[:half], -1), shift_y(before[half:], 1)]
    offsets = [z for ((_, z),) in k_zones]
    k_zones = [[(y, z) for z in offsets] for y in (0, 1, NY - 1)]
    far = [(NY // 2, z) for z in offsets]
    k_zones += [far[: NZ // 2], far[NZ // 2 :]]
    pieces, zones = pieces + v_ring, k_zones + v_zones

    send, raw = project(
        table, rows, pieces, zones, gain, dp_count, images, tokens
    )
    kv = lax.all_to_all(send, "dp", 0, 0, tiled=True)

    rows_later, _ = lax.optimization_barrier((features, raw))
    span = width // NY
    col_pieces = [
        shift_y(
            lax.dynamic_slice(
                rows_later, (core, 0, (my_y + s) % NY * span), (1, tokens, span)
            )[0],
            s,
        )
        for s in range(NY)
    ]

    parts, probs, d_scores = attend(table, queries, cotangent, kv)
    parts, col_pieces = lax.optimization_barrier((parts, col_pieces))
    parts = lax.all_to_all(parts, "dp", 0, 0, tiled=True)
    own_cols = transpose_pieces(col_pieces)
    other_cols = swap_cores(own_cols, tensor_count)
    attended, grad_queries = apply(table, kv, probs, d_scores, queries.shape)
    parts, other_cols, attended, grad_queries = lax.optimization_barrier(
        (parts, other_cols, attended, grad_queries)
    )
    grads, by_core = owner_grads(table, parts, raw, gain, images)

    lines = [shift_y(by_core, s) for s in range(NY)]
    shares = weight_terms(own_cols, other_cols, lines)
    shares, grads = lax.optimization_barrier((shares, grads))
    shares = lax.all_to_all(shares, "dp", 0, 0, tiled=True, axis_index_groups=Z_GROUPS)

    own, other = feature_terms(table, grads, pieces, zones, width, tensor_count)
    other = swap_cores(other, tensor_count)
    share = own.shape[0] * 2 // tensor_count
    pairs = [
        own[s * share : (s + 1) * share].astype(F32)
        + other[s * share : (s + 1) * share].astype(F32)
        for s in range(tensor_count // 2)
    ]
    grad_features = pairs[0]
    for s in range(1, tensor_count // 2):
        grad_features = grad_features + lax.ppermute(
            pairs[s].astype(BF16),
            "tensor",
            [(t, (t + 2 * s) % tensor_count) for t in range(tensor_count)],
        ).astype(F32)
    grad_features = grad_features.astype(BF16).reshape(images, tokens // tensor_count, width)
    weight_grads = jnp.sum(shares.astype(F32), axis=0)
    return (
        attended,
        grad_queries,
        grad_features,
        weight_grads[:, :head_dim],
        weight_grads[:, head_dim:],
    )


def solution(mesh):
    in_specs = (
        P("dp", "tensor"),
        P("dp", None, None),
        P("dp", "tensor"),
        P("dp", "tensor"),
        P(),
        P(),
        P(),
        P(),
        P("dp", "tensor"),
    )
    out_specs = (
        P("dp", "tensor"),
        P("dp", "tensor"),
        P("dp", "tensor", None),
        P("dp", "tensor"),
        P("dp", "tensor"),
    )
    return jax.shard_map(local, mesh=mesh, in_specs=in_specs, out_specs=out_specs, check_vma=False)
```

```python
import functools

import jax
import jax.numpy as jnp
from jax import lax
from jax.experimental import pallas as pl
from jax.experimental.pallas import tpu as pltpu
from jax.sharding import PartitionSpec as P

TILES = 4
EPS = 1e-05
MASKED_SCORE = -1e30
NY, NZ = 4, 8
Y_GROUPS = [[y * NZ + z for y in range(NY)] for z in range(NZ)]
Z_GROUPS = [[y * NZ + z for z in range(NZ)] for y in range(NY)]
BF16, F32 = jnp.bfloat16, jnp.float32
MIB = 1024 * 1024
GROUP = 4
POS, OWNER, VALID, FIRST, PLACE = range(5)


def dot_dims(a, b, a_dim, b_dim):
    return lax.dot_general(
        a, b, (((a_dim,), (b_dim,)), ((), ())), preferred_element_type=F32
    )


def limit(mib):
    return pltpu.CompilerParams(vmem_limit_bytes=mib * MIB)


def cost(flops, mib):
    return pl.CostEstimate(flops=flops, bytes_accessed=mib * MIB, transcendentals=0)


def in_vmem():
    return pl.BlockSpec(memory_space=pltpu.VMEM)


def in_hbm():
    return pl.BlockSpec(memory_space=pltpu.HBM)


def weight_blocks(table_ref, w_refs, zones):
    spots = {}
    for n, blocks in enumerate(zones):
        for i, at in enumerate(blocks):
            size = w_refs[n].shape[0] // len(blocks)
            spots.setdefault(at, []).append((w_refs[n], slice(i * size, (i + 1) * size)))
    found = []
    for (y_off, z_off), spot in spots.items():
        y = lax.rem(table_ref[PLACE, 0] + y_off, NY)
        z = lax.rem(table_ref[PLACE, 1] + z_off, NZ)
        size = spot[0][1].stop - spot[0][1].start
        found.append((pl.ds(pl.multiple_of((y * NZ + z) * size, size), size), spot))
    return found


def side_by_side(spot):
    return jnp.concatenate([ref[rows, :] for ref, rows in spot], axis=1)


def project_kernel(table_ref, f_ref, *refs, zones):
    w_refs, (gain_ref, send_ref, raw_ref, kv) = refs[: len(zones)], refs[len(zones) :]
    head_dim = gain_ref.shape[1]
    tokens = send_ref.shape[1]
    total = jnp.zeros((f_ref.shape[0], 2 * head_dim), F32)
    for cols, spot in weight_blocks(table_ref, w_refs, zones):
        total = total + jnp.dot(f_ref[:, cols], side_by_side(spot), preferred_element_type=F32)
    raw = total[:, :head_dim]
    raw_ref[...] = raw
    scale = lax.rsqrt(jnp.mean(raw * raw, axis=-1, keepdims=True) + EPS)
    keys = (raw * scale * gain_ref[...]).astype(BF16)
    values = total[:, head_dim:].astype(BF16)
    for i in range(kv.shape[0]):
        kv[i, :, :head_dim] = keys[i * tokens : (i + 1) * tokens]
        kv[i, :, head_dim:] = values[i * tokens : (i + 1) * tokens]

    def put(d, carry):
        send_ref[d] = kv[jnp.maximum(table_ref[POS, d], 0)]
        return carry

    lax.fori_loop(0, send_ref.shape[0], put, 0, unroll=4)


def project(table, rows, pieces, zones, gain, dp, images, tokens):
    cols = 2 * gain.shape[1]
    return pl.pallas_call(
        functools.partial(project_kernel, zones=zones),
        grid_spec=pltpu.PrefetchScalarGridSpec(
            num_scalar_prefetch=1,
            grid=(),
            in_specs=[in_vmem()] * (2 + len(pieces)),
            out_specs=[in_vmem()] * 2,
            scratch_shapes=[pltpu.VMEM((images, tokens, cols), BF16)],
        ),
        out_shape=[
            pltpu.HBM((dp, tokens, cols), BF16),
            pltpu.HBM((rows.shape[0], cols // 2), F32),
        ],
        compiler_params=limit(14),
        cost_estimate=cost(2 * rows.size * cols, 10),
        name="project",
    )(table, *hold(rows), *pieces, gain)


def load_heads(ref, start, rows, head_dim):
    heads = ref.shape[1] // head_dim
    return jnp.concatenate(
        [ref[pl.ds(start, rows), g * head_dim : (g + 1) * head_dim] for g in range(heads)],
        axis=0,
    )


def store_heads(ref, start, rows, head_dim, full):
    for g in range(ref.shape[1] // head_dim):
        ref[pl.ds(start, rows), g * head_dim : (g + 1) * head_dim] = full[
            g * rows : (g + 1) * rows
        ]


def attend_kernel(table_ref, q_ref, ct_ref, kv_ref, part_ref, probs_ref, ds_ref, acc):
    blocks = table_ref.shape[1]
    rows = q_ref.shape[0] // blocks
    head_dim = kv_ref.shape[2] // 2
    tokens = kv_ref.shape[1]
    scale = head_dim**-0.5
    part_ref[...] = jnp.zeros_like(part_ref)
    acc[...] = jnp.zeros_like(acc)

    def some_blocks(step, carry):
        at = [step * GROUP + i for i in range(GROUP)]
        owners = [table_ref[OWNER, b] for b in at]
        starts = [pl.multiple_of(b * rows, rows) for b in at]
        queries = [load_heads(q_ref, s, rows, head_dim) for s in starts]
        grads = [load_heads(ct_ref, s, rows, head_dim) for s in starts]
        scores = [
            dot_dims(kv_ref[o, :, :head_dim], q, 1, 1) * scale for o, q in zip(owners, queries)
        ]
        d_probs = [dot_dims(kv_ref[o, :, head_dim:], g, 1, 1) for o, g in zip(owners, grads)]
        token = lax.broadcasted_iota(jnp.int32, (tokens, 1), 0)
        scores = [
            jnp.where(token < table_ref[VALID, b], s, MASKED_SCORE) for b, s in zip(at, scores)
        ]
        weights = [jnp.exp(s - jnp.max(s, axis=0, keepdims=True)) for s in scores]
        probs = [w * (1.0 / jnp.sum(w, axis=0, keepdims=True)) for w in weights]
        halves = [p.astype(BF16) for p in probs]
        deltas = [jnp.sum(p * d, axis=0, keepdims=True) for p, d in zip(probs, d_probs)]
        d_scores = [
            (p * (d - x) * scale).astype(BF16) for p, d, x in zip(probs, d_probs, deltas)
        ]
        key_parts = [
            jnp.dot(d, q, preferred_element_type=F32) for d, q in zip(d_scores, queries)
        ]
        value_parts = [
            jnp.dot(p, g, preferred_element_type=F32) for p, g in zip(halves, grads)
        ]
        key_run, value_run = acc[:, :head_dim], acc[:, head_dim:]
        for i, b in enumerate(at):
            keep = table_ref[FIRST, b] == 0
            key_run = key_parts[i] + jnp.where(keep, key_run, 0.0)
            value_run = value_parts[i] + jnp.where(keep, value_run, 0.0)
            part_ref[owners[i], :, :head_dim] = key_run.astype(BF16)
            part_ref[owners[i], :, head_dim:] = value_run.astype(BF16)
            probs_ref[b] = halves[i]
            ds_ref[b] = d_scores[i]
        acc[:, :head_dim] = key_run
        acc[:, head_dim:] = value_run
        return carry

    lax.fori_loop(0, blocks // GROUP, some_blocks, 0)


def hold(*arrays):
    return [pltpu.with_memory_space_constraint(x, pltpu.HBM) for x in arrays]


def attend(table, queries, cotangent, kv):
    blocks, (_, tokens, cols) = table.shape[1], kv.shape
    rows = queries.size * 2 // (blocks * cols)
    stash = pltpu.HBM((blocks, tokens, rows), BF16)
    return pl.pallas_call(
        attend_kernel,
        grid_spec=pltpu.PrefetchScalarGridSpec(
            num_scalar_prefetch=1,
            grid=(),
            in_specs=[in_vmem()] * 3,
            out_specs=[in_vmem()] * 3,
            scratch_shapes=[pltpu.VMEM(kv.shape[1:], F32)],
        ),
        out_shape=[pltpu.HBM(kv.shape, BF16), stash, stash],
        compiler_params=limit(13),
        cost_estimate=cost(8 * queries.size * tokens, 8),
        name="attend",
    )(table, *hold(queries, cotangent, kv))


def apply_kernel(table_ref, kv_ref, probs_ref, ds_ref, out_ref, gq_ref):
    blocks = table_ref.shape[1]
    rows = out_ref.shape[0] // blocks
    head_dim = kv_ref.shape[2] // 2

    def some_blocks(step, carry):
        at = [step * GROUP + i for i in range(GROUP)]
        owners = [table_ref[OWNER, b] for b in at]
        outs = [
            dot_dims(probs_ref[b], kv_ref[o, :, head_dim:], 0, 0) for b, o in zip(at, owners)
        ]
        gqs = [dot_dims(ds_ref[b], kv_ref[o, :, :head_dim], 0, 0) for b, o in zip(at, owners)]
        for i, b in enumerate(at):
            start = pl.multiple_of(b * rows, rows)
            store_heads(out_ref, start, rows, head_dim, outs[i].astype(BF16))
            store_heads(gq_ref, start, rows, head_dim, gqs[i].astype(BF16))
        return carry

    lax.fori_loop(0, blocks // GROUP, some_blocks, 0)


def apply(table, kv, probs, d_scores, shape):
    out = pltpu.HBM(shape, BF16)
    return pl.pallas_call(
        apply_kernel,
        grid_spec=pltpu.PrefetchScalarGridSpec(
            num_scalar_prefetch=1,
            grid=(),
            in_specs=[in_vmem()] * 3,
            out_specs=[in_vmem()] * 2,
        ),
        out_shape=[out, out],
        compiler_params=limit(9),
        cost_estimate=cost(4 * shape[0] * shape[1] * kv.shape[1], 6),
        name="apply",
    )(table, *hold(kv, probs, d_scores))


def owner_kernel(table_ref, part_ref, raw_ref, gain_ref, grad_ref, by_core_ref, acc):
    head_dim = gain_ref.shape[1]
    tokens = part_ref.shape[1]
    acc[...] = jnp.zeros_like(acc)

    def add(d, carry):
        @pl.when(table_ref[POS, d] >= 0)
        def _():
            acc[table_ref[POS, d]] += part_ref[d].astype(F32)

        return carry

    lax.fori_loop(0, part_ref.shape[0], add, 0)
    gain = gain_ref[...]
    for i in range(acc.shape[0]):
        here = slice(i * tokens, (i + 1) * tokens)
        raw = raw_ref[here]
        scale = lax.rsqrt(jnp.mean(raw * raw, axis=-1, keepdims=True) + EPS)
        scaled = acc[i, :, :head_dim] * gain
        pull = jnp.mean(raw * scaled, axis=-1, keepdims=True)
        grad = scale * scaled - raw * (scale * scale * scale * pull)
        grad_ref[here, :head_dim] = grad.astype(BF16)
        grad_ref[here, head_dim:] = acc[i, :, head_dim:].astype(BF16)
    for i in range(acc.shape[0]):
        at = pl.multiple_of(lax.rem(table_ref[PLACE, 3] + i, 2) * tokens, tokens)
        by_core_ref[i * tokens : (i + 1) * tokens, :] = grad_ref[pl.ds(at, tokens), :]


def owner_grads(table, parts, raw, gain, images):
    tokens, cols = parts.shape[1:]
    grads = jax.ShapeDtypeStruct((images * tokens, cols), BF16)
    return pl.pallas_call(
        owner_kernel,
        grid_spec=pltpu.PrefetchScalarGridSpec(
            num_scalar_prefetch=1,
            grid=(),
            in_specs=[in_vmem()] * 3,
            out_specs=[in_vmem()] * 2,
            scratch_shapes=[pltpu.VMEM((images, tokens, cols), F32)],
        ),
        out_shape=[grads, grads],
        compiler_params=limit(6),
        cost_estimate=cost(0, 3),
        name="owner_grads",
    )(table, *hold(parts, raw), gain)


def transpose_kernel(*refs):
    pieces, out_ref = refs[:-1], refs[-1]
    tokens = pieces[0].shape[0]
    for i, ref in enumerate(pieces):
        out_ref[:, i * tokens : (i + 1) * tokens] = ref[...].T


def transpose_pieces(pieces):
    tokens, width = pieces[0].shape
    return pl.pallas_call(
        transpose_kernel,
        in_specs=[in_vmem()] * len(pieces),
        out_specs=in_vmem(),
        out_shape=jax.ShapeDtypeStruct((width, tokens * len(pieces)), BF16),
        compiler_params=limit(7),
        cost_estimate=cost(0, 4),
        name="transpose_pieces",
    )(*pieces)


def weight_kernel(own_ref, other_ref, *refs):
    lines, out_ref = refs[:-1], refs[-1]
    half = lines[0].shape[0] // 2
    first = jnp.concatenate([ref[:half, :] for ref in lines], axis=0)
    second = jnp.concatenate([ref[half:, :] for ref in lines], axis=0)
    block = out_ref.shape[1]
    for i in range(out_ref.shape[0]):
        here = slice(i * block, (i + 1) * block)
        total = jnp.dot(own_ref[here, :], first, preferred_element_type=F32)
        total = total + jnp.dot(other_ref[here, :], second, preferred_element_type=F32)
        out_ref[i] = total.astype(BF16)


def weight_terms(own_cols, other_cols, lines):
    width, cols = own_cols.shape[0], lines[0].shape[1]
    return pl.pallas_call(
        weight_kernel,
        in_specs=[in_vmem()] * (2 + len(lines)),
        out_specs=in_vmem(),
        out_shape=pltpu.HBM((NZ, width // NZ, cols), BF16),
        compiler_params=limit(9),
        cost_estimate=cost(4 * own_cols.size * cols, 6),
        name="weight_terms",
    )(own_cols, other_cols, *lines)


def assemble_kernel(table_ref, *refs, zones):
    w_refs, out_ref = refs[:-1], refs[-1]
    for rows, spot in weight_blocks(table_ref, w_refs, zones):
        out_ref[rows, :] = side_by_side(spot)


def assemble(table, pieces, zones, width, cols):
    return pl.pallas_call(
        functools.partial(assemble_kernel, zones=zones),
        grid_spec=pltpu.PrefetchScalarGridSpec(
            num_scalar_prefetch=1,
            grid=(),
            in_specs=[in_vmem()] * len(pieces),
            out_specs=in_vmem(),
        ),
        out_shape=pltpu.HBM((width, cols), BF16),
        compiler_params=limit(10),
        cost_estimate=cost(0, 8),
        name="assemble",
    )(table, *pieces)


def feature_kernel(table_ref, own_ref, other_ref, w_own_ref, w_other_ref, *refs, targets):
    out_refs, (lhs, held, sems) = refs[:-3], refs[-3:]
    chips = len(out_refs)
    tokens = own_ref.shape[0] // 2
    share = tokens // targets
    steps, block = held.shape[1:3]
    copies = []
    for step in range(steps):
        for core, w_ref in enumerate((w_own_ref, w_other_ref)):
            here = pl.ds(step * block, block)
            copies.append(
                pltpu.make_async_copy(w_ref.at[here, :], held.at[core, step], sems.at[core, step])
            )
    for copy in copies:
        copy.start()
    for core, ref in enumerate((own_ref, other_ref)):
        for chip in range(chips):
            target = lax.rem(table_ref[PLACE, 2] + chip, chips) * 2 + table_ref[PLACE, 3]
            for i in range(2):
                at = pl.multiple_of(i * tokens + target * share, share)
                to = (chip * 2 + i) * share
                lhs[core, to : to + share, :] = ref[pl.ds(at, share), :]
    for step in range(steps):
        copies[2 * step].wait()
        part = dot_dims(lhs[0], held[0, step], 1, 1)
        copies[2 * step + 1].wait()
        part = (part + dot_dims(lhs[1], held[1, step], 1, 1)).astype(BF16)
        for chip, ref in enumerate(out_refs):
            ref[:, step * block : (step + 1) * block] = part[
                chip * 2 * share : (chip + 1) * 2 * share
            ]


def feature_terms(table, own, other, w_own, w_other, targets):
    width, cols = w_own.shape
    chips, steps = targets // 2, 8
    rows = own.shape[0] // targets
    return pl.pallas_call(
        functools.partial(feature_kernel, targets=targets),
        grid_spec=pltpu.PrefetchScalarGridSpec(
            num_scalar_prefetch=1,
            grid=(),
            in_specs=[in_vmem()] * 2 + [in_hbm()] * 2,
            out_specs=[in_vmem()] * chips,
            scratch_shapes=[
                pltpu.VMEM((2, own.shape[0] // 2, cols), BF16),
                pltpu.VMEM((2, steps, width // steps, cols), BF16),
                pltpu.SemaphoreType.DMA((2, steps)),
            ],
        ),
        out_shape=[jax.ShapeDtypeStruct((rows, width), BF16)] * chips,
        compiler_params=limit(14),
        cost_estimate=cost(4 * own.size * width, 10),
        name="feature_terms",
    )(table, own, other, w_own, w_other)


def shift_y(x, by):
    if by == 0:
        return x
    pairs = [(y * NZ + z, (y + by) % NY * NZ + z) for y in range(NY) for z in range(NZ)]
    return lax.ppermute(x, "dp", pairs)


def shift_z(x, by):
    pairs = [(y * NZ + z, y * NZ + (z + by) % NZ) for y in range(NY) for z in range(NZ)]
    return lax.ppermute(x, "dp", pairs)


def ring_z(x, blocks):
    pieces, zones = [x], [blocks]
    below = above = x
    for hop in range(1, NZ // 2):
        below, above = shift_z(below, 1), shift_z(above, -1)
        pieces += [below, above]
        zones += [[(y, off) for y, _ in blocks] for off in (NZ - hop, hop)]
    pieces += [shift_z(below, 1)]
    zones += [[(y, NZ // 2) for y, _ in blocks]]
    return pieces, zones


def swap_cores(x, count):
    return lax.ppermute(x, "tensor", [(t, t ^ 1) for t in range(count)])


def local(
    queries, features, k_weight, v_weight, k_gain, block_image, image_slot, image_tiles, cotangent
):
    dp_count = lax.axis_size("dp")
    tensor_count = lax.axis_size("tensor")
    me = lax.axis_index("dp")
    images, tokens, width = features.shape
    head_dim = k_gain.shape[0]
    rows = features.reshape(images * tokens, width)
    gain = k_gain.reshape(1, head_dim)
    my_y, my_z = me // NZ, lax.rem(me, NZ)
    tensor = lax.axis_index("tensor")
    core = lax.rem(tensor, 2)

    image_ids = lax.broadcasted_iota(jnp.int32, (1, image_slot.shape[0]), 1)
    id_match = block_image[:, None] == image_ids
    slots = jnp.sum(jnp.where(id_match, image_slot[None, :], 0), axis=1).reshape(dp_count, -1)
    tiles = jnp.sum(jnp.where(id_match, image_tiles[None, :], 0), axis=1).reshape(dp_count, -1)
    my_slots = lax.dynamic_index_in_dim(slots, me, 0, keepdims=False)
    my_tiles = lax.dynamic_index_in_dim(tiles, me, 0, keepdims=False)
    first = jnp.concatenate(
        [jnp.ones((1,), jnp.int32), (my_slots[1:] != my_slots[:-1]).astype(jnp.int32)]
    )
    pos = jnp.max(jnp.where(slots // images == me, slots % images, -1), axis=1)
    place = jnp.stack([my_y, my_z, tensor // 2, core])
    place = jnp.pad(place, (0, pos.shape[0] - place.shape[0]))
    table = jnp.stack([pos, my_slots // images, my_tiles * (tokens // TILES), first, place])

    v_line = jnp.concatenate([shift_y(v_weight, (NY - i) % NY) for i in range(NY)])
    k_ring, k_zones = ring_z(k_weight, [(0, 0)])
    v_ring, v_zones = ring_z(v_line, [(i, 0) for i in range(NY)])
    k_line = jnp.concatenate(k_ring)
    half = k_line.shape[0] // 2
    after, before = shift_y(k_line, -1), shift_y(k_line, 1)
    pieces = [k_line, after, before, shift_y(after[:half], -1), shift_y(before[half:], 1)]
    offsets = [z for ((_, z),) in k_zones]
    k_zones = [[(y, z) for z in offsets] for y in (0, 1, NY - 1)]
    far = [(NY // 2, z) for z in offsets]
    k_zones += [far[: NZ // 2], far[NZ // 2 :]]
    pieces, zones = pieces + v_ring, k_zones + v_zones

    send, raw = project(
        table, rows, pieces, zones, gain, dp_count, images, tokens
    )
    kv = lax.all_to_all(send, "dp", 0, 0, tiled=True)

    rows_later, pieces_later, _ = lax.optimization_barrier((features, pieces, raw))
    span = width // NY
    col_pieces = [
        shift_y(
            lax.dynamic_slice(
                rows_later, (core, 0, (my_y + s) % NY * span), (1, tokens, span)
            )[0],
            s,
        )
        for s in range(NY)
    ]

    w_own = assemble(table, pieces_later, zones, width, 2 * head_dim)
    w_other = swap_cores(w_own, tensor_count)

    parts, probs, d_scores = attend(table, queries, cotangent, kv)
    parts, col_pieces, w_other = lax.optimization_barrier((parts, col_pieces, w_other))
    parts = lax.all_to_all(parts, "dp", 0, 0, tiled=True)
    own_cols = transpose_pieces(col_pieces)
    other_cols = swap_cores(own_cols, tensor_count)
    attended, grad_queries = apply(table, kv, probs, d_scores, queries.shape)
    parts, other_cols, attended, grad_queries = lax.optimization_barrier(
        (parts, other_cols, attended, grad_queries)
    )
    grads, by_core = owner_grads(table, parts, raw, gain, images)

    lines = [shift_y(by_core, s) for s in range(NY)]
    shares = weight_terms(own_cols, other_cols, lines)
    other_grads = swap_cores(grads, tensor_count)
    shares, grads, other_grads = lax.optimization_barrier((shares, grads, other_grads))
    shares = lax.all_to_all(shares, "dp", 0, 0, tiled=True, axis_index_groups=Z_GROUPS)

    terms = feature_terms(table, grads, other_grads, w_own, w_other, tensor_count)
    grad_features = terms[0].astype(F32)
    for s in range(1, tensor_count // 2):
        pairs = [(t, (t + 2 * s) % tensor_count) for t in range(tensor_count)]
        grad_features = grad_features + lax.ppermute(terms[s], "tensor", pairs).astype(F32)
    grad_features = grad_features.astype(BF16).reshape(images, tokens // tensor_count, width)
    weight_grads = jnp.sum(shares.astype(F32), axis=0)
    return (
        attended,
        grad_queries,
        grad_features,
        weight_grads[:, :head_dim],
        weight_grads[:, head_dim:],
    )


def solution(mesh):
    in_specs = (
        P("dp", "tensor"),
        P("dp", None, None),
        P("dp", "tensor"),
        P("dp", "tensor"),
        P(),
        P(),
        P(),
        P(),
        P("dp", "tensor"),
    )
    out_specs = (
        P("dp", "tensor"),
        P("dp", "tensor"),
        P("dp", "tensor", None),
        P("dp", "tensor"),
        P("dp", "tensor"),
    )
    return jax.shard_map(local, mesh=mesh, in_specs=in_specs, out_specs=out_specs, check_vma=False)
```

```python
import functools

import jax
import jax.numpy as jnp
from jax import lax
from jax.experimental import pallas as pl
from jax.experimental.pallas import tpu as pltpu
from jax.sharding import PartitionSpec as P

TILES = 4
EPS = 1e-05
MASKED_SCORE = -1e30
NY, NZ = 4, 8
Y_GROUPS = [[y * NZ + z for y in range(NY)] for z in range(NZ)]
Z_GROUPS = [[y * NZ + z for z in range(NZ)] for y in range(NY)]
BF16, F32 = jnp.bfloat16, jnp.float32
MIB = 1024 * 1024
GROUP = 4
POS, OWNER, VALID, FIRST, PLACE = range(5)


def dot_dims(a, b, a_dim, b_dim):
    return lax.dot_general(
        a, b, (((a_dim,), (b_dim,)), ((), ())), preferred_element_type=F32
    )


def limit(mib):
    return pltpu.CompilerParams(vmem_limit_bytes=mib * MIB)


def cost(flops, mib):
    return pl.CostEstimate(flops=flops, bytes_accessed=mib * MIB, transcendentals=0)


def in_vmem():
    return pl.BlockSpec(memory_space=pltpu.VMEM)


def in_hbm():
    return pl.BlockSpec(memory_space=pltpu.HBM)


def weight_blocks(table_ref, w_refs, zones):
    spots = {}
    for n, blocks in enumerate(zones):
        for i, at in enumerate(blocks):
            size = w_refs[n].shape[0] // len(blocks)
            spots.setdefault(at, []).append((w_refs[n], slice(i * size, (i + 1) * size)))
    found = []
    for (y_off, z_off), spot in spots.items():
        y = lax.rem(table_ref[PLACE, 0] + y_off, NY)
        z = lax.rem(table_ref[PLACE, 1] + z_off, NZ)
        size = spot[0][1].stop - spot[0][1].start
        found.append((pl.ds(pl.multiple_of((y * NZ + z) * size, size), size), spot))
    return found


def side_by_side(spot):
    return jnp.concatenate([ref[rows, :] for ref, rows in spot], axis=1)


def project_kernel(table_ref, f_ref, *refs, zones):
    w_refs, (gain_ref, send_ref, raw_ref, kv) = refs[: len(zones)], refs[len(zones) :]
    head_dim = gain_ref.shape[1]
    tokens = send_ref.shape[1]
    total = jnp.zeros((f_ref.shape[0], 2 * head_dim), F32)
    for cols, spot in weight_blocks(table_ref, w_refs, zones):
        total = total + jnp.dot(f_ref[:, cols], side_by_side(spot), preferred_element_type=F32)
    raw = total[:, :head_dim]
    raw_ref[...] = raw
    scale = lax.rsqrt(jnp.mean(raw * raw, axis=-1, keepdims=True) + EPS)
    keys = (raw * scale * gain_ref[...]).astype(BF16)
    values = total[:, head_dim:].astype(BF16)
    for i in range(kv.shape[0]):
        kv[i, :, :head_dim] = keys[i * tokens : (i + 1) * tokens]
        kv[i, :, head_dim:] = values[i * tokens : (i + 1) * tokens]

    def put(d, carry):
        send_ref[d] = kv[jnp.maximum(table_ref[POS, d], 0)]
        return carry

    lax.fori_loop(0, send_ref.shape[0], put, 0, unroll=4)


def project(table, rows, pieces, zones, gain, dp, images, tokens):
    cols = 2 * gain.shape[1]
    return pl.pallas_call(
        functools.partial(project_kernel, zones=zones),
        grid_spec=pltpu.PrefetchScalarGridSpec(
            num_scalar_prefetch=1,
            grid=(),
            in_specs=[in_vmem()] * (2 + len(pieces)),
            out_specs=[in_vmem()] * 2,
            scratch_shapes=[pltpu.VMEM((images, tokens, cols), BF16)],
        ),
        out_shape=[
            pltpu.HBM((dp, tokens, cols), BF16),
            pltpu.HBM((rows.shape[0], cols // 2), F32),
        ],
        compiler_params=limit(14),
        cost_estimate=cost(2 * rows.size * cols, 10),
        name="project",
    )(table, *hold(rows), *pieces, gain)


def load_heads(ref, start, rows, head_dim):
    heads = ref.shape[1] // head_dim
    return jnp.concatenate(
        [ref[pl.ds(start, rows), g * head_dim : (g + 1) * head_dim] for g in range(heads)],
        axis=0,
    )


def store_heads(ref, start, rows, head_dim, full):
    for g in range(ref.shape[1] // head_dim):
        ref[pl.ds(start, rows), g * head_dim : (g + 1) * head_dim] = full[
            g * rows : (g + 1) * rows
        ]


def attend_kernel(table_ref, q_ref, ct_ref, kv_ref, part_ref, probs_ref, ds_ref, acc):
    blocks = table_ref.shape[1]
    rows = q_ref.shape[0] // blocks
    head_dim = kv_ref.shape[2] // 2
    tokens = kv_ref.shape[1]
    scale = head_dim**-0.5
    part_ref[...] = jnp.zeros_like(part_ref)
    acc[...] = jnp.zeros_like(acc)

    def some_blocks(step, carry):
        at = [step * GROUP + i for i in range(GROUP)]
        owners = [table_ref[OWNER, b] for b in at]
        starts = [pl.multiple_of(b * rows, rows) for b in at]
        queries = [load_heads(q_ref, s, rows, head_dim) for s in starts]
        grads = [load_heads(ct_ref, s, rows, head_dim) for s in starts]
        scores = [
            dot_dims(kv_ref[o, :, :head_dim], q, 1, 1) * scale for o, q in zip(owners, queries)
        ]
        d_probs = [dot_dims(kv_ref[o, :, head_dim:], g, 1, 1) for o, g in zip(owners, grads)]
        token = lax.broadcasted_iota(jnp.int32, (tokens, 1), 0)
        scores = [
            jnp.where(token < table_ref[VALID, b], s, MASKED_SCORE) for b, s in zip(at, scores)
        ]
        weights = [jnp.exp(s - jnp.max(s, axis=0, keepdims=True)) for s in scores]
        probs = [w * (1.0 / jnp.sum(w, axis=0, keepdims=True)) for w in weights]
        halves = [p.astype(BF16) for p in probs]
        deltas = [jnp.sum(p * d, axis=0, keepdims=True) for p, d in zip(probs, d_probs)]
        d_scores = [
            (p * (d - x) * scale).astype(BF16) for p, d, x in zip(probs, d_probs, deltas)
        ]
        key_parts = [
            jnp.dot(d, q, preferred_element_type=F32) for d, q in zip(d_scores, queries)
        ]
        value_parts = [
            jnp.dot(p, g, preferred_element_type=F32) for p, g in zip(halves, grads)
        ]
        key_run, value_run = acc[:, :head_dim], acc[:, head_dim:]
        for i, b in enumerate(at):
            keep = table_ref[FIRST, b] == 0
            key_run = key_parts[i] + jnp.where(keep, key_run, 0.0)
            value_run = value_parts[i] + jnp.where(keep, value_run, 0.0)
            part_ref[owners[i], :, :head_dim] = key_run.astype(BF16)
            part_ref[owners[i], :, head_dim:] = value_run.astype(BF16)
            probs_ref[b] = halves[i]
            ds_ref[b] = d_scores[i]
        acc[:, :head_dim] = key_run
        acc[:, head_dim:] = value_run
        return carry

    lax.fori_loop(0, blocks // GROUP, some_blocks, 0)


def hold(*arrays):
    return [pltpu.with_memory_space_constraint(x, pltpu.HBM) for x in arrays]


def attend(table, queries, cotangent, kv):
    blocks, (_, tokens, cols) = table.shape[1], kv.shape
    rows = queries.size * 2 // (blocks * cols)
    stash = pltpu.HBM((blocks, tokens, rows), BF16)
    return pl.pallas_call(
        attend_kernel,
        grid_spec=pltpu.PrefetchScalarGridSpec(
            num_scalar_prefetch=1,
            grid=(),
            in_specs=[in_vmem()] * 3,
            out_specs=[in_vmem()] * 3,
            scratch_shapes=[pltpu.VMEM(kv.shape[1:], F32)],
        ),
        out_shape=[pltpu.HBM(kv.shape, BF16), stash, stash],
        compiler_params=limit(13),
        cost_estimate=cost(8 * queries.size * tokens, 8),
        name="attend",
    )(table, *hold(queries, cotangent, kv))


def apply_kernel(table_ref, kv_ref, probs_ref, ds_ref, out_ref, gq_ref):
    blocks = table_ref.shape[1]
    rows = out_ref.shape[0] // blocks
    head_dim = kv_ref.shape[2] // 2

    def some_blocks(step, carry):
        at = [step * GROUP + i for i in range(GROUP)]
        owners = [table_ref[OWNER, b] for b in at]
        outs = [
            dot_dims(probs_ref[b], kv_ref[o, :, head_dim:], 0, 0) for b, o in zip(at, owners)
        ]
        gqs = [dot_dims(ds_ref[b], kv_ref[o, :, :head_dim], 0, 0) for b, o in zip(at, owners)]
        for i, b in enumerate(at):
            start = pl.multiple_of(b * rows, rows)
            store_heads(out_ref, start, rows, head_dim, outs[i].astype(BF16))
            store_heads(gq_ref, start, rows, head_dim, gqs[i].astype(BF16))
        return carry

    lax.fori_loop(0, blocks // GROUP, some_blocks, 0)


def apply(table, kv, probs, d_scores, shape):
    out = pltpu.HBM(shape, BF16)
    return pl.pallas_call(
        apply_kernel,
        grid_spec=pltpu.PrefetchScalarGridSpec(
            num_scalar_prefetch=1,
            grid=(),
            in_specs=[in_vmem()] * 3,
            out_specs=[in_vmem()] * 2,
        ),
        out_shape=[out, out],
        compiler_params=limit(9),
        cost_estimate=cost(4 * shape[0] * shape[1] * kv.shape[1], 6),
        name="apply",
    )(table, *hold(kv, probs, d_scores))


def owner_kernel(table_ref, part_ref, raw_ref, gain_ref, grad_ref, by_core_ref, acc):
    head_dim = gain_ref.shape[1]
    tokens = part_ref.shape[1]
    acc[...] = jnp.zeros_like(acc)

    def add(d, carry):
        @pl.when(table_ref[POS, d] >= 0)
        def _():
            acc[table_ref[POS, d]] += part_ref[d].astype(F32)

        return carry

    lax.fori_loop(0, part_ref.shape[0], add, 0)
    gain = gain_ref[...]
    for i in range(acc.shape[0]):
        here = slice(i * tokens, (i + 1) * tokens)
        raw = raw_ref[here]
        scale = lax.rsqrt(jnp.mean(raw * raw, axis=-1, keepdims=True) + EPS)
        scaled = acc[i, :, :head_dim] * gain
        pull = jnp.mean(raw * scaled, axis=-1, keepdims=True)
        grad = scale * scaled - raw * (scale * scale * scale * pull)
        grad_ref[here, :head_dim] = grad.astype(BF16)
        grad_ref[here, head_dim:] = acc[i, :, head_dim:].astype(BF16)
    for i in range(acc.shape[0]):
        at = pl.multiple_of(lax.rem(table_ref[PLACE, 3] + i, 2) * tokens, tokens)
        by_core_ref[i * tokens : (i + 1) * tokens, :] = grad_ref[pl.ds(at, tokens), :]


def owner_grads(table, parts, raw, gain, images):
    tokens, cols = parts.shape[1:]
    grads = jax.ShapeDtypeStruct((images * tokens, cols), BF16)
    return pl.pallas_call(
        owner_kernel,
        grid_spec=pltpu.PrefetchScalarGridSpec(
            num_scalar_prefetch=1,
            grid=(),
            in_specs=[in_vmem()] * 3,
            out_specs=[in_vmem()] * 2,
            scratch_shapes=[pltpu.VMEM((images, tokens, cols), F32)],
        ),
        out_shape=[grads, grads],
        compiler_params=limit(6),
        cost_estimate=cost(0, 3),
        name="owner_grads",
    )(table, *hold(parts, raw), gain)


def transpose_kernel(*refs):
    pieces, out_ref = refs[:-1], refs[-1]
    tokens = pieces[0].shape[0]
    for i, ref in enumerate(pieces):
        out_ref[:, i * tokens : (i + 1) * tokens] = ref[...].T


def transpose_pieces(pieces):
    tokens, width = pieces[0].shape
    return pl.pallas_call(
        transpose_kernel,
        in_specs=[in_vmem()] * len(pieces),
        out_specs=in_vmem(),
        out_shape=jax.ShapeDtypeStruct((width, tokens * len(pieces)), BF16),
        compiler_params=limit(7),
        cost_estimate=cost(0, 4),
        name="transpose_pieces",
    )(*pieces)


def weight_kernel(own_ref, other_ref, *refs):
    lines, out_ref = refs[:-1], refs[-1]
    half = lines[0].shape[0] // 2
    first = jnp.concatenate([ref[:half, :] for ref in lines], axis=0)
    second = jnp.concatenate([ref[half:, :] for ref in lines], axis=0)
    block = out_ref.shape[1]
    for i in range(out_ref.shape[0]):
        here = slice(i * block, (i + 1) * block)
        total = jnp.dot(own_ref[here, :], first, preferred_element_type=F32)
        total = total + jnp.dot(other_ref[here, :], second, preferred_element_type=F32)
        out_ref[i] = total.astype(BF16)


def weight_terms(own_cols, other_cols, lines):
    width, cols = own_cols.shape[0], lines[0].shape[1]
    return pl.pallas_call(
        weight_kernel,
        in_specs=[in_vmem()] * (2 + len(lines)),
        out_specs=in_vmem(),
        out_shape=pltpu.HBM((NZ, width // NZ, cols), BF16),
        compiler_params=limit(9),
        cost_estimate=cost(4 * own_cols.size * cols, 6),
        name="weight_terms",
    )(own_cols, other_cols, *lines)


def assemble_kernel(table_ref, *refs, zones):
    w_refs, out_refs = refs[:-2], refs[-2:]
    for here, spot in weight_blocks(table_ref, w_refs, zones):
        for out_ref, (ref, rows) in zip(out_refs, spot):
            out_ref[here, :] = ref[rows, :]


def assemble(table, pieces, zones, width, head_dim):
    return pl.pallas_call(
        functools.partial(assemble_kernel, zones=zones),
        grid_spec=pltpu.PrefetchScalarGridSpec(
            num_scalar_prefetch=1,
            grid=(),
            in_specs=[in_vmem()] * len(pieces),
            out_specs=[in_vmem()] * 2,
        ),
        out_shape=[pltpu.HBM((width, head_dim), BF16)] * 2,
        compiler_params=limit(10),
        cost_estimate=cost(0, 1),
        name="assemble",
    )(table, *pieces)


def feature_kernel(table_ref, own_ref, other_ref, *refs, targets):
    w_refs, out_refs, (lhs, held, sems) = refs[:4], refs[4:-3], refs[-3:]
    chips = len(out_refs)
    tokens, head_dim = own_ref.shape[0] // 2, own_ref.shape[1] // 2
    share = tokens // targets
    steps, block = held.shape[1:3]
    copies = [
        [
            pltpu.make_async_copy(
                w_ref.at[pl.ds(step * block, block), :], held.at[n, step], sems.at[n, step]
            )
            for n, w_ref in enumerate(w_refs)
        ]
        for step in range(steps)
    ]
    for step in range(steps):
        for copy in copies[step]:
            copy.start()
    for core, ref in enumerate((own_ref, other_ref)):
        for chip in range(chips):
            target = lax.rem(table_ref[PLACE, 2] + chip, chips) * 2 + table_ref[PLACE, 3]
            for i in range(2):
                at = pl.multiple_of(i * tokens + target * share, share)
                to = (chip * 2 + i) * share
                for n in range(2):
                    lhs[core, n, to : to + share, :] = ref[
                        pl.ds(at, share), n * head_dim : (n + 1) * head_dim
                    ]
    for step in range(steps):
        part = 0.0
        for core in range(2):
            for n in range(2):
                copies[step][2 * core + n].wait()
            left = jnp.concatenate([lhs[core, 0], lhs[core, 1]], axis=1)
            right = jnp.concatenate([held[2 * core, step], held[2 * core + 1, step]], axis=1)
            part = part + dot_dims(left, right, 1, 1)
        for chip, ref in enumerate(out_refs):
            ref[:, step * block : (step + 1) * block] = part[
                chip * 2 * share : (chip + 1) * 2 * share
            ].astype(BF16)


def feature_terms(table, own, other, weights, targets):
    width, head_dim = weights[0].shape
    chips, steps = targets // 2, 8
    rows = own.shape[0] // targets
    return pl.pallas_call(
        functools.partial(feature_kernel, targets=targets),
        grid_spec=pltpu.PrefetchScalarGridSpec(
            num_scalar_prefetch=1,
            grid=(),
            in_specs=[in_vmem()] * 2 + [in_hbm()] * 4,
            out_specs=[in_vmem()] * chips,
            scratch_shapes=[
                pltpu.VMEM((2, 2, own.shape[0] // 2, head_dim), BF16),
                pltpu.VMEM((4, steps, width // steps, head_dim), BF16),
                pltpu.SemaphoreType.DMA((4, steps)),
            ],
        ),
        out_shape=[jax.ShapeDtypeStruct((rows, width), BF16)] * chips,
        compiler_params=limit(14),
        cost_estimate=cost(4 * own.size * width, 10),
        name="feature_terms",
    )(table, own, other, *weights)


def shift_y(x, by):
    if by == 0:
        return x
    pairs = [(y * NZ + z, (y + by) % NY * NZ + z) for y in range(NY) for z in range(NZ)]
    return lax.ppermute(x, "dp", pairs)


def shift_z(x, by):
    pairs = [(y * NZ + z, y * NZ + (z + by) % NZ) for y in range(NY) for z in range(NZ)]
    return lax.ppermute(x, "dp", pairs)


def ring_z(x, blocks):
    pieces, zones = [x], [blocks]
    below = above = x
    for hop in range(1, NZ // 2):
        below, above = shift_z(below, 1), shift_z(above, -1)
        pieces += [below, above]
        zones += [[(y, off) for y, _ in blocks] for off in (NZ - hop, hop)]
    pieces += [shift_z(below, 1)]
    zones += [[(y, NZ // 2) for y, _ in blocks]]
    return pieces, zones


def swap_cores(x, count):
    return lax.ppermute(x, "tensor", [(t, t ^ 1) for t in range(count)])


def local(
    queries, features, k_weight, v_weight, k_gain, block_image, image_slot, image_tiles, cotangent
):
    dp_count = lax.axis_size("dp")
    tensor_count = lax.axis_size("tensor")
    me = lax.axis_index("dp")
    images, tokens, width = features.shape
    head_dim = k_gain.shape[0]
    rows = features.reshape(images * tokens, width)
    gain = k_gain.reshape(1, head_dim)
    my_y, my_z = me // NZ, lax.rem(me, NZ)
    tensor = lax.axis_index("tensor")
    core = lax.rem(tensor, 2)

    image_ids = lax.broadcasted_iota(jnp.int32, (1, image_slot.shape[0]), 1)
    id_match = block_image[:, None] == image_ids
    slots = jnp.sum(jnp.where(id_match, image_slot[None, :], 0), axis=1).reshape(dp_count, -1)
    tiles = jnp.sum(jnp.where(id_match, image_tiles[None, :], 0), axis=1).reshape(dp_count, -1)
    my_slots = lax.dynamic_index_in_dim(slots, me, 0, keepdims=False)
    my_tiles = lax.dynamic_index_in_dim(tiles, me, 0, keepdims=False)
    first = jnp.concatenate(
        [jnp.ones((1,), jnp.int32), (my_slots[1:] != my_slots[:-1]).astype(jnp.int32)]
    )
    pos = jnp.max(jnp.where(slots // images == me, slots % images, -1), axis=1)
    place = jnp.stack([my_y, my_z, tensor // 2, core])
    place = jnp.pad(place, (0, pos.shape[0] - place.shape[0]))
    table = jnp.stack([pos, my_slots // images, my_tiles * (tokens // TILES), first, place])

    v_line = jnp.concatenate([shift_y(v_weight, (NY - i) % NY) for i in range(NY)])
    k_ring, k_zones = ring_z(k_weight, [(0, 0)])
    v_ring, v_zones = ring_z(v_line, [(i, 0) for i in range(NY)])
    k_line = jnp.concatenate(k_ring)
    half = k_line.shape[0] // 2
    after, before = shift_y(k_line, -1), shift_y(k_line, 1)
    pieces = [k_line, after, before, shift_y(after[:half], -1), shift_y(before[half:], 1)]
    offsets = [z for ((_, z),) in k_zones]
    k_zones = [[(y, z) for z in offsets] for y in (0, 1, NY - 1)]
    far = [(NY // 2, z) for z in offsets]
    k_zones += [far[: NZ // 2], far[NZ // 2 :]]
    pieces, zones = pieces + v_ring, k_zones + v_zones

    send, raw = project(
        table, rows, pieces, zones, gain, dp_count, images, tokens
    )
    kv = lax.all_to_all(send, "dp", 0, 0, tiled=True)

    rows_later, _ = lax.optimization_barrier((features, raw))
    span = width // NY
    col_pieces = [
        shift_y(
            lax.dynamic_slice(
                rows_later, (core, 0, (my_y + s) % NY * span), (1, tokens, span)
            )[0],
            s,
        )
        for s in range(NY)
    ]

    parts, probs, d_scores = attend(table, queries, cotangent, kv)
    parts, col_pieces, pieces = lax.optimization_barrier((parts, col_pieces, pieces))
    parts = lax.all_to_all(parts, "dp", 0, 0, tiled=True)
    own_cols = transpose_pieces(col_pieces)
    other_cols = swap_cores(own_cols, tensor_count)
    weights = list(assemble(table, pieces, zones, width, head_dim))
    weights += [swap_cores(w, tensor_count) for w in weights]
    attended, grad_queries = apply(table, kv, probs, d_scores, queries.shape)
    parts, other_cols, attended, grad_queries, weights = lax.optimization_barrier(
        (parts, other_cols, attended, grad_queries, weights)
    )
    grads, by_core = owner_grads(table, parts, raw, gain, images)

    lines = [shift_y(by_core, s) for s in range(NY)]
    shares = weight_terms(own_cols, other_cols, lines)
    other_grads = swap_cores(grads, tensor_count)
    shares, grads, other_grads = lax.optimization_barrier((shares, grads, other_grads))
    shares = lax.all_to_all(shares, "dp", 0, 0, tiled=True, axis_index_groups=Z_GROUPS)

    terms = list(feature_terms(table, grads, other_grads, weights, tensor_count))
    for s in range(1, tensor_count // 2):
        pairs = [(t, (t + 2 * s) % tensor_count) for t in range(tensor_count)]
        terms[s] = lax.ppermute(terms[s], "tensor", pairs)
    shares, terms = lax.optimization_barrier((shares, terms))
    grad_features = sum(term.astype(F32) for term in terms).astype(BF16)
    grad_features = grad_features.reshape(images, tokens // tensor_count, width)
    weight_grads = jnp.sum(shares.astype(F32), axis=0)
    return (
        attended,
        grad_queries,
        grad_features,
        weight_grads[:, :head_dim],
        weight_grads[:, head_dim:],
    )


def solution(mesh):
    in_specs = (
        P("dp", "tensor"),
        P("dp", None, None),
        P("dp", "tensor"),
        P("dp", "tensor"),
        P(),
        P(),
        P(),
        P(),
        P("dp", "tensor"),
    )
    out_specs = (
        P("dp", "tensor"),
        P("dp", "tensor"),
        P("dp", "tensor", None),
        P("dp", "tensor"),
        P("dp", "tensor"),
    )
    return jax.shard_map(local, mesh=mesh, in_specs=in_specs, out_specs=out_specs, check_vma=False)
```

```python
import functools

import jax
import jax.numpy as jnp
from jax import lax
from jax.experimental import pallas as pl
from jax.experimental.pallas import tpu as pltpu
from jax.sharding import PartitionSpec as P

TILES = 4
EPS = 1e-05
MASKED_SCORE = -1e30
NY, NZ = 4, 8
Y_GROUPS = [[y * NZ + z for y in range(NY)] for z in range(NZ)]
Z_GROUPS = [[y * NZ + z for z in range(NZ)] for y in range(NY)]
BF16, F32 = jnp.bfloat16, jnp.float32
MIB = 1024 * 1024
GROUP = 4
POS, OWNER, VALID, FIRST, PLACE = range(5)


def dot_dims(a, b, a_dim, b_dim):
    return lax.dot_general(
        a, b, (((a_dim,), (b_dim,)), ((), ())), preferred_element_type=F32
    )


def limit(mib):
    return pltpu.CompilerParams(vmem_limit_bytes=mib * MIB)


def cost(flops, mib):
    return pl.CostEstimate(flops=flops, bytes_accessed=mib * MIB, transcendentals=0)


def in_vmem():
    return pl.BlockSpec(memory_space=pltpu.VMEM)


def weight_blocks(table_ref, w_refs, zones):
    spots = {}
    for n, blocks in enumerate(zones):
        for i, at in enumerate(blocks):
            size = w_refs[n].shape[0] // len(blocks)
            spots.setdefault(at, []).append((w_refs[n], slice(i * size, (i + 1) * size)))
    found = []
    for (y_off, z_off), spot in spots.items():
        y = lax.rem(table_ref[PLACE, 0] + y_off, NY)
        z = lax.rem(table_ref[PLACE, 1] + z_off, NZ)
        size = spot[0][1].stop - spot[0][1].start
        found.append((pl.ds(pl.multiple_of((y * NZ + z) * size, size), size), spot))
    return found


def side_by_side(spot):
    return jnp.concatenate([ref[rows, :] for ref, rows in spot], axis=1)


def project_kernel(table_ref, f_ref, *refs, zones):
    w_refs, (gain_ref, send_ref, raw_ref, kv) = refs[: len(zones)], refs[len(zones) :]
    head_dim = gain_ref.shape[1]
    tokens = send_ref.shape[1]
    total = jnp.zeros((f_ref.shape[0], 2 * head_dim), F32)
    for cols, spot in weight_blocks(table_ref, w_refs, zones):
        total = total + jnp.dot(f_ref[:, cols], side_by_side(spot), preferred_element_type=F32)
    raw = total[:, :head_dim]
    raw_ref[...] = raw
    scale = lax.rsqrt(jnp.mean(raw * raw, axis=-1, keepdims=True) + EPS)
    keys = (raw * scale * gain_ref[...]).astype(BF16)
    values = total[:, head_dim:].astype(BF16)
    for i in range(kv.shape[0]):
        kv[i, :, :head_dim] = keys[i * tokens : (i + 1) * tokens]
        kv[i, :, head_dim:] = values[i * tokens : (i + 1) * tokens]

    def put(d, carry):
        send_ref[d] = kv[jnp.maximum(table_ref[POS, d], 0)]
        return carry

    lax.fori_loop(0, send_ref.shape[0], put, 0, unroll=4)


def project(table, rows, pieces, zones, gain, dp, images, tokens):
    cols = 2 * gain.shape[1]
    return pl.pallas_call(
        functools.partial(project_kernel, zones=zones),
        grid_spec=pltpu.PrefetchScalarGridSpec(
            num_scalar_prefetch=1,
            grid=(),
            in_specs=[in_vmem()] * (2 + len(pieces)),
            out_specs=[in_vmem()] * 2,
            scratch_shapes=[pltpu.VMEM((images, tokens, cols), BF16)],
        ),
        out_shape=[
            pltpu.HBM((dp, tokens, cols), BF16),
            pltpu.HBM((rows.shape[0], cols // 2), F32),
        ],
        compiler_params=limit(14),
        cost_estimate=cost(2 * rows.size * cols, 10),
        name="project",
    )(table, *hold(rows), *pieces, gain)


def load_heads(ref, start, rows, head_dim):
    heads = ref.shape[1] // head_dim
    return jnp.concatenate(
        [ref[pl.ds(start, rows), g * head_dim : (g + 1) * head_dim] for g in range(heads)],
        axis=0,
    )


def store_heads(ref, start, rows, head_dim, full):
    for g in range(ref.shape[1] // head_dim):
        ref[pl.ds(start, rows), g * head_dim : (g + 1) * head_dim] = full[
            g * rows : (g + 1) * rows
        ]


def attend_kernel(table_ref, q_ref, ct_ref, kv_ref, part_ref, probs_ref, ds_ref, acc):
    blocks = table_ref.shape[1]
    rows = q_ref.shape[0] // blocks
    head_dim = kv_ref.shape[2] // 2
    tokens = kv_ref.shape[1]
    scale = head_dim**-0.5
    part_ref[...] = jnp.zeros_like(part_ref)
    acc[...] = jnp.zeros_like(acc)

    def some_blocks(step, carry):
        at = [step * GROUP + i for i in range(GROUP)]
        owners = [table_ref[OWNER, b] for b in at]
        starts = [pl.multiple_of(b * rows, rows) for b in at]
        queries = [load_heads(q_ref, s, rows, head_dim) for s in starts]
        grads = [load_heads(ct_ref, s, rows, head_dim) for s in starts]
        scores = [
            dot_dims(kv_ref[o, :, :head_dim], q, 1, 1) * scale for o, q in zip(owners, queries)
        ]
        d_probs = [dot_dims(kv_ref[o, :, head_dim:], g, 1, 1) for o, g in zip(owners, grads)]
        token = lax.broadcasted_iota(jnp.int32, (tokens, 1), 0)
        scores = [
            jnp.where(token < table_ref[VALID, b], s, MASKED_SCORE) for b, s in zip(at, scores)
        ]
        weights = [jnp.exp(s - jnp.max(s, axis=0, keepdims=True)) for s in scores]
        probs = [w * (1.0 / jnp.sum(w, axis=0, keepdims=True)) for w in weights]
        halves = [p.astype(BF16) for p in probs]
        deltas = [jnp.sum(p * d, axis=0, keepdims=True) for p, d in zip(probs, d_probs)]
        d_scores = [
            (p * (d - x) * scale).astype(BF16) for p, d, x in zip(probs, d_probs, deltas)
        ]
        key_parts = [
            jnp.dot(d, q, preferred_element_type=F32) for d, q in zip(d_scores, queries)
        ]
        value_parts = [
            jnp.dot(p, g, preferred_element_type=F32) for p, g in zip(halves, grads)
        ]
        key_run, value_run = acc[:, :head_dim], acc[:, head_dim:]
        for i, b in enumerate(at):
            keep = table_ref[FIRST, b] == 0
            key_run = key_parts[i] + jnp.where(keep, key_run, 0.0)
            value_run = value_parts[i] + jnp.where(keep, value_run, 0.0)
            part_ref[owners[i], :, :head_dim] = key_run.astype(BF16)
            part_ref[owners[i], :, head_dim:] = value_run.astype(BF16)
            probs_ref[b] = halves[i]
            ds_ref[b] = d_scores[i]
        acc[:, :head_dim] = key_run
        acc[:, head_dim:] = value_run
        return carry

    lax.fori_loop(0, blocks // GROUP, some_blocks, 0)


def hold(*arrays):
    return [pltpu.with_memory_space_constraint(x, pltpu.HBM) for x in arrays]


def attend(table, queries, cotangent, kv):
    blocks, (_, tokens, cols) = table.shape[1], kv.shape
    rows = queries.size * 2 // (blocks * cols)
    stash = pltpu.HBM((blocks, tokens, rows), BF16)
    return pl.pallas_call(
        attend_kernel,
        grid_spec=pltpu.PrefetchScalarGridSpec(
            num_scalar_prefetch=1,
            grid=(),
            in_specs=[in_vmem()] * 3,
            out_specs=[in_vmem()] * 3,
            scratch_shapes=[pltpu.VMEM(kv.shape[1:], F32)],
        ),
        out_shape=[pltpu.HBM(kv.shape, BF16), stash, stash],
        compiler_params=limit(13),
        cost_estimate=cost(8 * queries.size * tokens, 8),
        name="attend",
    )(table, *hold(queries, cotangent, kv))


def apply_kernel(table_ref, kv_ref, probs_ref, ds_ref, out_ref, gq_ref):
    blocks = table_ref.shape[1]
    rows = out_ref.shape[0] // blocks
    head_dim = kv_ref.shape[2] // 2

    def some_blocks(step, carry):
        at = [step * GROUP + i for i in range(GROUP)]
        owners = [table_ref[OWNER, b] for b in at]
        outs = [
            dot_dims(probs_ref[b], kv_ref[o, :, head_dim:], 0, 0) for b, o in zip(at, owners)
        ]
        gqs = [dot_dims(ds_ref[b], kv_ref[o, :, :head_dim], 0, 0) for b, o in zip(at, owners)]
        for i, b in enumerate(at):
            start = pl.multiple_of(b * rows, rows)
            store_heads(out_ref, start, rows, head_dim, outs[i].astype(BF16))
            store_heads(gq_ref, start, rows, head_dim, gqs[i].astype(BF16))
        return carry

    lax.fori_loop(0, blocks // GROUP, some_blocks, 0)


def apply(table, kv, probs, d_scores, shape):
    out = pltpu.HBM(shape, BF16)
    return pl.pallas_call(
        apply_kernel,
        grid_spec=pltpu.PrefetchScalarGridSpec(
            num_scalar_prefetch=1,
            grid=(),
            in_specs=[in_vmem()] * 3,
            out_specs=[in_vmem()] * 2,
        ),
        out_shape=[out, out],
        compiler_params=limit(9),
        cost_estimate=cost(4 * shape[0] * shape[1] * kv.shape[1], 6),
        name="apply",
    )(table, *hold(kv, probs, d_scores))


def owner_kernel(table_ref, part_ref, raw_ref, gain_ref, grad_ref, by_core_ref, acc):
    head_dim = gain_ref.shape[1]
    tokens = part_ref.shape[1]
    acc[...] = jnp.zeros_like(acc)

    def add(d, carry):
        @pl.when(table_ref[POS, d] >= 0)
        def _():
            acc[table_ref[POS, d]] += part_ref[d].astype(F32)

        return carry

    lax.fori_loop(0, part_ref.shape[0], add, 0)
    gain = gain_ref[...]
    for i in range(acc.shape[0]):
        here = slice(i * tokens, (i + 1) * tokens)
        raw = raw_ref[here]
        scale = lax.rsqrt(jnp.mean(raw * raw, axis=-1, keepdims=True) + EPS)
        scaled = acc[i, :, :head_dim] * gain
        pull = jnp.mean(raw * scaled, axis=-1, keepdims=True)
        grad = scale * scaled - raw * (scale * scale * scale * pull)
        grad_ref[here, :head_dim] = grad.astype(BF16)
        grad_ref[here, head_dim:] = acc[i, :, head_dim:].astype(BF16)
    for i in range(acc.shape[0]):
        at = pl.multiple_of(lax.rem(table_ref[PLACE, 3] + i, 2) * tokens, tokens)
        by_core_ref[i * tokens : (i + 1) * tokens, :] = grad_ref[pl.ds(at, tokens), :]


def owner_grads(table, parts, raw, gain, images):
    tokens, cols = parts.shape[1:]
    grads = jax.ShapeDtypeStruct((images * tokens, cols), BF16)
    return pl.pallas_call(
        owner_kernel,
        grid_spec=pltpu.PrefetchScalarGridSpec(
            num_scalar_prefetch=1,
            grid=(),
            in_specs=[in_vmem()] * 3,
            out_specs=[in_vmem()] * 2,
            scratch_shapes=[pltpu.VMEM((images, tokens, cols), F32)],
        ),
        out_shape=[grads, grads],
        compiler_params=limit(6),
        cost_estimate=cost(0, 3),
        name="owner_grads",
    )(table, *hold(parts, raw), gain)


def transpose_kernel(*refs):
    pieces, out_ref = refs[:-1], refs[-1]
    tokens = pieces[0].shape[0]
    for i, ref in enumerate(pieces):
        out_ref[:, i * tokens : (i + 1) * tokens] = ref[...].T


def transpose_pieces(pieces):
    tokens, width = pieces[0].shape
    return pl.pallas_call(
        transpose_kernel,
        in_specs=[in_vmem()] * len(pieces),
        out_specs=in_vmem(),
        out_shape=jax.ShapeDtypeStruct((width, tokens * len(pieces)), BF16),
        compiler_params=limit(7),
        cost_estimate=cost(0, 4),
        name="transpose_pieces",
    )(*pieces)


def weight_kernel(own_ref, other_ref, *refs):
    lines, out_ref = refs[:-1], refs[-1]
    half = lines[0].shape[0] // 2
    first = jnp.concatenate([ref[:half, :] for ref in lines], axis=0)
    second = jnp.concatenate([ref[half:, :] for ref in lines], axis=0)
    block = out_ref.shape[1]
    for i in range(out_ref.shape[0]):
        here = slice(i * block, (i + 1) * block)
        total = jnp.dot(own_ref[here, :], first, preferred_element_type=F32)
        total = total + jnp.dot(other_ref[here, :], second, preferred_element_type=F32)
        out_ref[i] = total.astype(BF16)


def weight_terms(own_cols, other_cols, lines):
    width, cols = own_cols.shape[0], lines[0].shape[1]
    return pl.pallas_call(
        weight_kernel,
        in_specs=[in_vmem()] * (2 + len(lines)),
        out_specs=in_vmem(),
        out_shape=pltpu.HBM((NZ, width // NZ, cols), BF16),
        compiler_params=limit(9),
        cost_estimate=cost(4 * own_cols.size * cols, 6),
        name="weight_terms",
    )(own_cols, other_cols, *lines)


def assemble_kernel(table_ref, *refs, zones):
    w_refs, out_refs = refs[:-2], refs[-2:]
    for here, spot in weight_blocks(table_ref, w_refs, zones):
        for out_ref, (ref, rows) in zip(out_refs, spot):
            out_ref[here, :] = ref[rows, :]


def assemble(table, pieces, zones, width, head_dim):
    return pl.pallas_call(
        functools.partial(assemble_kernel, zones=zones),
        grid_spec=pltpu.PrefetchScalarGridSpec(
            num_scalar_prefetch=1,
            grid=(),
            in_specs=[in_vmem()] * len(pieces),
            out_specs=[in_vmem()] * 2,
        ),
        out_shape=[jax.ShapeDtypeStruct((width, head_dim), BF16)] * 2,
        compiler_params=limit(10),
        cost_estimate=cost(0, 1),
        name="assemble",
    )(table, *pieces)


def feature_kernel(table_ref, own_ref, other_ref, *refs, targets):
    w_refs, out_refs, lhs = refs[:4], refs[4:-1], refs[-1]
    chips = len(out_refs)
    tokens, head_dim = own_ref.shape[0] // 2, own_ref.shape[1] // 2
    share = tokens // targets
    block = w_refs[0].shape[0] // NZ
    for core, ref in enumerate((own_ref, other_ref)):
        for chip in range(chips):
            target = lax.rem(table_ref[PLACE, 2] + chip, chips) * 2 + table_ref[PLACE, 3]
            for i in range(2):
                at = pl.multiple_of(i * tokens + target * share, share)
                to = (chip * 2 + i) * share
                for n in range(2):
                    lhs[core, n, to : to + share, :] = ref[
                        pl.ds(at, share), n * head_dim : (n + 1) * head_dim
                    ]
    for step in range(NZ):
        here = slice(step * block, (step + 1) * block)
        part = 0.0
        for core in range(2):
            left = jnp.concatenate([lhs[core, 0], lhs[core, 1]], axis=1)
            right = jnp.concatenate(
                [w_refs[2 * core][here, :], w_refs[2 * core + 1][here, :]], axis=1
            )
            part = part + dot_dims(left, right, 1, 1)
        for chip, ref in enumerate(out_refs):
            ref[:, here] = part[chip * 2 * share : (chip + 1) * 2 * share].astype(BF16)


def feature_terms(table, own, other, weights, targets):
    width, head_dim = weights[0].shape
    chips = targets // 2
    rows = own.shape[0] // targets
    return pl.pallas_call(
        functools.partial(feature_kernel, targets=targets),
        grid_spec=pltpu.PrefetchScalarGridSpec(
            num_scalar_prefetch=1,
            grid=(),
            in_specs=[in_vmem()] * 6,
            out_specs=[in_vmem()] * chips,
            scratch_shapes=[pltpu.VMEM((2, 2, own.shape[0] // 2, head_dim), BF16)],
        ),
        out_shape=[jax.ShapeDtypeStruct((rows, width), BF16)] * chips,
        compiler_params=limit(14),
        cost_estimate=cost(4 * own.size * width, 10),
        name="feature_terms",
    )(table, own, other, *weights)


def shift_y(x, by):
    if by == 0:
        return x
    pairs = [(y * NZ + z, (y + by) % NY * NZ + z) for y in range(NY) for z in range(NZ)]
    return lax.ppermute(x, "dp", pairs)


def shift_z(x, by):
    if by == 0:
        return x
    pairs = [(y * NZ + z, y * NZ + (z + by) % NZ) for y in range(NY) for z in range(NZ)]
    return lax.ppermute(x, "dp", pairs)


def ring_z(x, blocks):
    pieces, zones = [x], [blocks]
    below = above = x
    for hop in range(1, NZ // 2):
        below, above = shift_z(below, 1), shift_z(above, -1)
        pieces += [below, above]
        zones += [[(y, off) for y, _ in blocks] for off in (NZ - hop, hop)]
    pieces += [shift_z(below, 1)]
    zones += [[(y, NZ // 2) for y, _ in blocks]]
    return pieces, zones


def swap_cores(x, count):
    return lax.ppermute(x, "tensor", [(t, t ^ 1) for t in range(count)])


def local(
    queries, features, k_weight, v_weight, k_gain, block_image, image_slot, image_tiles, cotangent
):
    dp_count = lax.axis_size("dp")
    tensor_count = lax.axis_size("tensor")
    me = lax.axis_index("dp")
    images, tokens, width = features.shape
    head_dim = k_gain.shape[0]
    rows = features.reshape(images * tokens, width)
    gain = k_gain.reshape(1, head_dim)
    my_y, my_z = me // NZ, lax.rem(me, NZ)
    tensor = lax.axis_index("tensor")
    core = lax.rem(tensor, 2)

    image_ids = lax.broadcasted_iota(jnp.int32, (1, image_slot.shape[0]), 1)
    id_match = block_image[:, None] == image_ids
    slots = jnp.sum(jnp.where(id_match, image_slot[None, :], 0), axis=1).reshape(dp_count, -1)
    tiles = jnp.sum(jnp.where(id_match, image_tiles[None, :], 0), axis=1).reshape(dp_count, -1)
    my_slots = lax.dynamic_index_in_dim(slots, me, 0, keepdims=False)
    my_tiles = lax.dynamic_index_in_dim(tiles, me, 0, keepdims=False)
    first = jnp.concatenate(
        [jnp.ones((1,), jnp.int32), (my_slots[1:] != my_slots[:-1]).astype(jnp.int32)]
    )
    pos = jnp.max(jnp.where(slots // images == me, slots % images, -1), axis=1)
    place = jnp.stack([my_y, my_z, tensor // 2, core])
    place = jnp.pad(place, (0, pos.shape[0] - place.shape[0]))
    table = jnp.stack([pos, my_slots // images, my_tiles * (tokens // TILES), first, place])

    v_line = jnp.concatenate([shift_y(v_weight, (NY - i) % NY) for i in range(NY)])
    k_line = jnp.concatenate([shift_z(k_weight, s) for s in range(NZ)])
    v_ring, v_zones = ring_z(v_line, [(i, 0) for i in range(NY)])
    half = k_line.shape[0] // 2
    after, before = shift_y(k_line, -1), shift_y(k_line, 1)
    pieces = [k_line, after, before, shift_y(after[:half], -1), shift_y(before[half:], 1)]
    offsets = [(NZ - s) % NZ for s in range(NZ)]
    k_zones = [[(y, z) for z in offsets] for y in (0, 1, NY - 1)]
    far = [(NY // 2, z) for z in offsets]
    k_zones += [far[: NZ // 2], far[NZ // 2 :]]
    pieces, zones = pieces + v_ring, k_zones + v_zones

    send, raw = project(
        table, rows, pieces, zones, gain, dp_count, images, tokens
    )
    kv = lax.all_to_all(send, "dp", 0, 0, tiled=True)

    rows_later, _ = lax.optimization_barrier((features, raw))
    span = width // NY
    col_pieces = [
        shift_y(
            lax.dynamic_slice(
                rows_later, (core, 0, (my_y + s) % NY * span), (1, tokens, span)
            )[0],
            s,
        )
        for s in range(NY)
    ]

    parts, probs, d_scores = attend(table, queries, cotangent, kv)
    parts, col_pieces, pieces = lax.optimization_barrier((parts, col_pieces, pieces))
    parts = lax.all_to_all(parts, "dp", 0, 0, tiled=True)
    own_cols = transpose_pieces(col_pieces)
    other_cols = swap_cores(own_cols, tensor_count)
    weights = list(assemble(table, pieces, zones, width, head_dim))
    weights += [swap_cores(w, tensor_count) for w in weights]
    attended, grad_queries = apply(table, kv, probs, d_scores, queries.shape)
    parts, other_cols, attended, grad_queries, weights = lax.optimization_barrier(
        (parts, other_cols, attended, grad_queries, weights)
    )
    grads, by_core = owner_grads(table, parts, raw, gain, images)

    lines = [shift_y(by_core, s) for s in range(NY)]
    shares = weight_terms(own_cols, other_cols, lines)
    other_grads = swap_cores(grads, tensor_count)
    shares, grads, other_grads = lax.optimization_barrier((shares, grads, other_grads))
    shares = lax.all_to_all(shares, "dp", 0, 0, tiled=True, axis_index_groups=Z_GROUPS)

    terms = list(feature_terms(table, grads, other_grads, weights, tensor_count))
    for s in range(1, tensor_count // 2):
        pairs = [(t, (t + 2 * s) % tensor_count) for t in range(tensor_count)]
        terms[s] = lax.ppermute(terms[s], "tensor", pairs)
    shares, terms = lax.optimization_barrier((shares, terms))
    grad_features = sum(term.astype(F32) for term in terms).astype(BF16)
    grad_features = grad_features.reshape(images, tokens // tensor_count, width)
    weight_grads = jnp.sum(shares.astype(F32), axis=0)
    return (
        attended,
        grad_queries,
        grad_features,
        weight_grads[:, :head_dim],
        weight_grads[:, head_dim:],
    )


def solution(mesh):
    in_specs = (
        P("dp", "tensor"),
        P("dp", None, None),
        P("dp", "tensor"),
        P("dp", "tensor"),
        P(),
        P(),
        P(),
        P(),
        P("dp", "tensor"),
    )
    out_specs = (
        P("dp", "tensor"),
        P("dp", "tensor"),
        P("dp", "tensor", None),
        P("dp", "tensor"),
        P("dp", "tensor"),
    )
    return jax.shard_map(local, mesh=mesh, in_specs=in_specs, out_specs=out_specs, check_vma=False)
```

```python
import functools

import jax
import jax.numpy as jnp
from jax import lax
from jax.experimental import pallas as pl
from jax.experimental.pallas import tpu as pltpu
from jax.sharding import PartitionSpec as P

TILES = 4
EPS = 1e-05
MASKED_SCORE = -1e30
NY, NZ = 4, 8
Y_GROUPS = [[y * NZ + z for y in range(NY)] for z in range(NZ)]
Z_GROUPS = [[y * NZ + z for z in range(NZ)] for y in range(NY)]
BF16, F32 = jnp.bfloat16, jnp.float32
MIB = 1024 * 1024
GROUP = 4
POS, OWNER, VALID, FIRST, PLACE = range(5)


def dot_dims(a, b, a_dim, b_dim):
    return lax.dot_general(
        a, b, (((a_dim,), (b_dim,)), ((), ())), preferred_element_type=F32
    )


def limit(mib):
    return pltpu.CompilerParams(vmem_limit_bytes=mib * MIB)


def cost(flops, mib):
    return pl.CostEstimate(flops=flops, bytes_accessed=mib * MIB, transcendentals=0)


def in_vmem():
    return pl.BlockSpec(memory_space=pltpu.VMEM)


def in_hbm():
    return pl.BlockSpec(memory_space=pltpu.HBM)


def weight_blocks(table_ref, w_refs, zones):
    spots = {}
    for n, blocks in enumerate(zones):
        for i, at in enumerate(blocks):
            size = w_refs[n].shape[0] // len(blocks)
            spots.setdefault(at, []).append((w_refs[n], slice(i * size, (i + 1) * size)))
    found = []
    for (y_off, z_off), spot in spots.items():
        y = lax.rem(table_ref[PLACE, 0] + y_off, NY)
        z = lax.rem(table_ref[PLACE, 1] + z_off, NZ)
        size = spot[0][1].stop - spot[0][1].start
        found.append((pl.ds(pl.multiple_of((y * NZ + z) * size, size), size), spot))
    return found


def side_by_side(spot):
    return jnp.concatenate([ref[rows, :] for ref, rows in spot], axis=1)


def project_kernel(table_ref, f_ref, *refs, zones):
    w_refs, (gain_ref, send_ref, raw_ref, kv) = refs[: len(zones)], refs[len(zones) :]
    head_dim = gain_ref.shape[1]
    tokens = send_ref.shape[1]
    total = jnp.zeros((f_ref.shape[0], 2 * head_dim), F32)
    for cols, spot in weight_blocks(table_ref, w_refs, zones):
        total = total + jnp.dot(f_ref[:, cols], side_by_side(spot), preferred_element_type=F32)
    raw = total[:, :head_dim]
    raw_ref[...] = raw
    scale = lax.rsqrt(jnp.mean(raw * raw, axis=-1, keepdims=True) + EPS)
    keys = (raw * scale * gain_ref[...]).astype(BF16)
    values = total[:, head_dim:].astype(BF16)
    for i in range(kv.shape[0]):
        kv[i, :, :head_dim] = keys[i * tokens : (i + 1) * tokens]
        kv[i, :, head_dim:] = values[i * tokens : (i + 1) * tokens]

    def put(d, carry):
        send_ref[d] = kv[jnp.maximum(table_ref[POS, d], 0)]
        return carry

    lax.fori_loop(0, send_ref.shape[0], put, 0, unroll=4)


def project(table, rows, pieces, zones, gain, dp, images, tokens):
    cols = 2 * gain.shape[1]
    return pl.pallas_call(
        functools.partial(project_kernel, zones=zones),
        grid_spec=pltpu.PrefetchScalarGridSpec(
            num_scalar_prefetch=1,
            grid=(),
            in_specs=[in_vmem()] * (2 + len(pieces)),
            out_specs=[in_vmem()] * 2,
            scratch_shapes=[pltpu.VMEM((images, tokens, cols), BF16)],
        ),
        out_shape=[
            pltpu.HBM((dp, tokens, cols), BF16),
            pltpu.HBM((rows.shape[0], cols // 2), F32),
        ],
        compiler_params=limit(14),
        cost_estimate=cost(2 * rows.size * cols, 10),
        name="project",
    )(table, *hold(rows), *pieces, gain)


def load_heads(ref, start, rows, head_dim):
    heads = ref.shape[1] // head_dim
    return jnp.concatenate(
        [ref[pl.ds(start, rows), g * head_dim : (g + 1) * head_dim] for g in range(heads)],
        axis=0,
    )


def store_heads(ref, start, rows, head_dim, full):
    for g in range(ref.shape[1] // head_dim):
        ref[pl.ds(start, rows), g * head_dim : (g + 1) * head_dim] = full[
            g * rows : (g + 1) * rows
        ]


def attend_kernel(table_ref, q_ref, ct_ref, kv_ref, part_ref, probs_ref, ds_ref, acc):
    blocks = table_ref.shape[1]
    rows = q_ref.shape[0] // blocks
    head_dim = kv_ref.shape[2] // 2
    tokens = kv_ref.shape[1]
    scale = head_dim**-0.5
    part_ref[...] = jnp.zeros_like(part_ref)
    acc[...] = jnp.zeros_like(acc)

    def some_blocks(step, carry):
        at = [step * GROUP + i for i in range(GROUP)]
        owners = [table_ref[OWNER, b] for b in at]
        starts = [pl.multiple_of(b * rows, rows) for b in at]
        queries = [load_heads(q_ref, s, rows, head_dim) for s in starts]
        grads = [load_heads(ct_ref, s, rows, head_dim) for s in starts]
        scores = [
            dot_dims(kv_ref[o, :, :head_dim], q, 1, 1) * scale for o, q in zip(owners, queries)
        ]
        d_probs = [dot_dims(kv_ref[o, :, head_dim:], g, 1, 1) for o, g in zip(owners, grads)]
        token = lax.broadcasted_iota(jnp.int32, (tokens, 1), 0)
        scores = [
            jnp.where(token < table_ref[VALID, b], s, MASKED_SCORE) for b, s in zip(at, scores)
        ]
        weights = [jnp.exp(s - jnp.max(s, axis=0, keepdims=True)) for s in scores]
        probs = [w * (1.0 / jnp.sum(w, axis=0, keepdims=True)) for w in weights]
        halves = [p.astype(BF16) for p in probs]
        deltas = [jnp.sum(p * d, axis=0, keepdims=True) for p, d in zip(probs, d_probs)]
        d_scores = [
            (p * (d - x) * scale).astype(BF16) for p, d, x in zip(probs, d_probs, deltas)
        ]
        key_parts = [
            jnp.dot(d, q, preferred_element_type=F32) for d, q in zip(d_scores, queries)
        ]
        value_parts = [
            jnp.dot(p, g, preferred_element_type=F32) for p, g in zip(halves, grads)
        ]
        key_run, value_run = acc[:, :head_dim], acc[:, head_dim:]
        for i, b in enumerate(at):
            keep = table_ref[FIRST, b] == 0
            key_run = key_parts[i] + jnp.where(keep, key_run, 0.0)
            value_run = value_parts[i] + jnp.where(keep, value_run, 0.0)
            part_ref[owners[i], :, :head_dim] = key_run.astype(BF16)
            part_ref[owners[i], :, head_dim:] = value_run.astype(BF16)
            probs_ref[b] = halves[i]
            ds_ref[b] = d_scores[i]
        acc[:, :head_dim] = key_run
        acc[:, head_dim:] = value_run
        return carry

    lax.fori_loop(0, blocks // GROUP, some_blocks, 0)


def hold(*arrays):
    return [pltpu.with_memory_space_constraint(x, pltpu.HBM) for x in arrays]


def attend(table, queries, cotangent, kv):
    blocks, (_, tokens, cols) = table.shape[1], kv.shape
    rows = queries.size * 2 // (blocks * cols)
    stash = pltpu.HBM((blocks, tokens, rows), BF16)
    return pl.pallas_call(
        attend_kernel,
        grid_spec=pltpu.PrefetchScalarGridSpec(
            num_scalar_prefetch=1,
            grid=(),
            in_specs=[in_vmem()] * 3,
            out_specs=[in_vmem()] * 3,
            scratch_shapes=[pltpu.VMEM(kv.shape[1:], F32)],
        ),
        out_shape=[pltpu.HBM(kv.shape, BF16), stash, stash],
        compiler_params=limit(13),
        cost_estimate=cost(8 * queries.size * tokens, 8),
        name="attend",
    )(table, *hold(queries, cotangent, kv))


def apply_kernel(table_ref, kv_ref, probs_ref, ds_ref, out_ref, gq_ref):
    blocks = table_ref.shape[1]
    rows = out_ref.shape[0] // blocks
    head_dim = kv_ref.shape[2] // 2

    def some_blocks(step, carry):
        at = [step * GROUP + i for i in range(GROUP)]
        owners = [table_ref[OWNER, b] for b in at]
        outs = [
            dot_dims(probs_ref[b], kv_ref[o, :, head_dim:], 0, 0) for b, o in zip(at, owners)
        ]
        gqs = [dot_dims(ds_ref[b], kv_ref[o, :, :head_dim], 0, 0) for b, o in zip(at, owners)]
        for i, b in enumerate(at):
            start = pl.multiple_of(b * rows, rows)
            store_heads(out_ref, start, rows, head_dim, outs[i].astype(BF16))
            store_heads(gq_ref, start, rows, head_dim, gqs[i].astype(BF16))
        return carry

    lax.fori_loop(0, blocks // GROUP, some_blocks, 0)


def apply(table, kv, probs, d_scores, shape):
    out = pltpu.HBM(shape, BF16)
    return pl.pallas_call(
        apply_kernel,
        grid_spec=pltpu.PrefetchScalarGridSpec(
            num_scalar_prefetch=1,
            grid=(),
            in_specs=[in_vmem()] * 3,
            out_specs=[in_vmem()] * 2,
        ),
        out_shape=[out, out],
        compiler_params=limit(9),
        cost_estimate=cost(4 * shape[0] * shape[1] * kv.shape[1], 6),
        name="apply",
    )(table, *hold(kv, probs, d_scores))


def owner_kernel(table_ref, part_ref, raw_ref, gain_ref, grad_ref, by_core_ref, acc):
    head_dim = gain_ref.shape[1]
    tokens = part_ref.shape[1]
    acc[...] = jnp.zeros_like(acc)

    def add(d, carry):
        @pl.when(table_ref[POS, d] >= 0)
        def _():
            acc[table_ref[POS, d]] += part_ref[d].astype(F32)

        return carry

    lax.fori_loop(0, part_ref.shape[0], add, 0)
    gain = gain_ref[...]
    for i in range(acc.shape[0]):
        here = slice(i * tokens, (i + 1) * tokens)
        raw = raw_ref[here]
        scale = lax.rsqrt(jnp.mean(raw * raw, axis=-1, keepdims=True) + EPS)
        scaled = acc[i, :, :head_dim] * gain
        pull = jnp.mean(raw * scaled, axis=-1, keepdims=True)
        grad = scale * scaled - raw * (scale * scale * scale * pull)
        grad_ref[here, :head_dim] = grad.astype(BF16)
        grad_ref[here, head_dim:] = acc[i, :, head_dim:].astype(BF16)
    for i in range(acc.shape[0]):
        at = pl.multiple_of(lax.rem(table_ref[PLACE, 3] + i, 2) * tokens, tokens)
        by_core_ref[i * tokens : (i + 1) * tokens, :] = grad_ref[pl.ds(at, tokens), :]


def owner_grads(table, parts, raw, gain, images):
    tokens, cols = parts.shape[1:]
    grads = jax.ShapeDtypeStruct((images * tokens, cols), BF16)
    return pl.pallas_call(
        owner_kernel,
        grid_spec=pltpu.PrefetchScalarGridSpec(
            num_scalar_prefetch=1,
            grid=(),
            in_specs=[in_vmem()] * 3,
            out_specs=[in_vmem()] * 2,
            scratch_shapes=[pltpu.VMEM((images, tokens, cols), F32)],
        ),
        out_shape=[grads, grads],
        compiler_params=limit(6),
        cost_estimate=cost(0, 3),
        name="owner_grads",
    )(table, *hold(parts, raw), gain)


def transpose_kernel(*refs):
    pieces, out_ref = refs[:-1], refs[-1]
    tokens = pieces[0].shape[0]
    for i, ref in enumerate(pieces):
        out_ref[:, i * tokens : (i + 1) * tokens] = ref[...].T


def transpose_pieces(pieces):
    tokens, width = pieces[0].shape
    return pl.pallas_call(
        transpose_kernel,
        in_specs=[in_vmem()] * len(pieces),
        out_specs=in_vmem(),
        out_shape=jax.ShapeDtypeStruct((width, tokens * len(pieces)), BF16),
        compiler_params=limit(7),
        cost_estimate=cost(0, 4),
        name="transpose_pieces",
    )(*hold(*pieces))


def weight_kernel(own_ref, other_ref, *refs):
    lines, out_ref = refs[:-1], refs[-1]
    half = lines[0].shape[0] // 2
    first = jnp.concatenate([ref[:half, :] for ref in lines], axis=0)
    second = jnp.concatenate([ref[half:, :] for ref in lines], axis=0)
    block = out_ref.shape[1]
    for i in range(out_ref.shape[0]):
        here = slice(i * block, (i + 1) * block)
        total = jnp.dot(own_ref[here, :], first, preferred_element_type=F32)
        total = total + jnp.dot(other_ref[here, :], second, preferred_element_type=F32)
        out_ref[i] = total.astype(BF16)


def weight_terms(own_cols, other_cols, lines):
    width, cols = own_cols.shape[0], lines[0].shape[1]
    return pl.pallas_call(
        weight_kernel,
        in_specs=[in_vmem()] * (2 + len(lines)),
        out_specs=in_vmem(),
        out_shape=pltpu.HBM((NZ, width // NZ, cols), BF16),
        compiler_params=limit(9),
        cost_estimate=cost(4 * own_cols.size * cols, 6),
        name="weight_terms",
    )(own_cols, other_cols, *lines)


def assemble_kernel(table_ref, *refs, zones):
    w_refs, out_refs = refs[:-2], refs[-2:]
    for here, spot in weight_blocks(table_ref, w_refs, zones):
        for out_ref, (ref, rows) in zip(out_refs, spot):
            out_ref[here, :] = ref[rows, :]


def assemble(table, pieces, zones, width, head_dim):
    return pl.pallas_call(
        functools.partial(assemble_kernel, zones=zones),
        grid_spec=pltpu.PrefetchScalarGridSpec(
            num_scalar_prefetch=1,
            grid=(),
            in_specs=[in_vmem()] * len(pieces),
            out_specs=[in_vmem()] * 2,
        ),
        out_shape=[pltpu.HBM((width, head_dim), BF16)] * 2,
        compiler_params=limit(10),
        cost_estimate=cost(0, 1),
        name="assemble",
    )(table, *pieces)


def feature_kernel(table_ref, own_ref, other_ref, *refs, targets):
    w_refs, out_refs, (lhs, held, sems) = refs[:4], refs[4:-3], refs[-3:]
    chips = len(out_refs)
    tokens, head_dim = own_ref.shape[0] // 2, own_ref.shape[1] // 2
    share = tokens // targets
    steps, block = held.shape[1:3]
    copies = [
        [
            pltpu.make_async_copy(
                w_ref.at[pl.ds(step * block, block), :], held.at[n, step], sems.at[n, step]
            )
            for n, w_ref in enumerate(w_refs)
        ]
        for step in range(steps)
    ]
    for step in range(steps):
        for copy in copies[step]:
            copy.start()
    for core, ref in enumerate((own_ref, other_ref)):
        for chip in range(chips):
            target = lax.rem(table_ref[PLACE, 2] + chip, chips) * 2 + table_ref[PLACE, 3]
            for i in range(2):
                at = pl.multiple_of(i * tokens + target * share, share)
                to = (chip * 2 + i) * share
                for n in range(2):
                    lhs[core, n, to : to + share, :] = ref[
                        pl.ds(at, share), n * head_dim : (n + 1) * head_dim
                    ]
    for step in range(steps):
        part = 0.0
        for core in range(2):
            for n in range(2):
                copies[step][2 * core + n].wait()
            left = jnp.concatenate([lhs[core, 0], lhs[core, 1]], axis=1)
            right = jnp.concatenate([held[2 * core, step], held[2 * core + 1, step]], axis=1)
            part = part + dot_dims(left, right, 1, 1)
        for chip, ref in enumerate(out_refs):
            ref[:, step * block : (step + 1) * block] = part[
                chip * 2 * share : (chip + 1) * 2 * share
            ].astype(BF16)


def feature_terms(table, own, other, weights, targets):
    width, head_dim = weights[0].shape
    chips, steps = targets // 2, 8
    rows = own.shape[0] // targets
    return pl.pallas_call(
        functools.partial(feature_kernel, targets=targets),
        grid_spec=pltpu.PrefetchScalarGridSpec(
            num_scalar_prefetch=1,
            grid=(),
            in_specs=[in_vmem()] * 2 + [in_hbm()] * 4,
            out_specs=[in_vmem()] * chips,
            scratch_shapes=[
                pltpu.VMEM((2, 2, own.shape[0] // 2, head_dim), BF16),
                pltpu.VMEM((4, steps, width // steps, head_dim), BF16),
                pltpu.SemaphoreType.DMA((4, steps)),
            ],
        ),
        out_shape=[jax.ShapeDtypeStruct((rows, width), BF16)] * chips,
        compiler_params=limit(14),
        cost_estimate=cost(4 * own.size * width, 10),
        name="feature_terms",
    )(table, own, other, *hold(*weights))


def shift_y(x, by):
    if by == 0:
        return x
    pairs = [(y * NZ + z, (y + by) % NY * NZ + z) for y in range(NY) for z in range(NZ)]
    return lax.ppermute(x, "dp", pairs)


def shift_z(x, by):
    pairs = [(y * NZ + z, y * NZ + (z + by) % NZ) for y in range(NY) for z in range(NZ)]
    return lax.ppermute(x, "dp", pairs)


def swap_cores(x, count):
    return lax.ppermute(x, "tensor", [(t, t ^ 1) for t in range(count)])


def local(
    queries, features, k_weight, v_weight, k_gain, block_image, image_slot, image_tiles, cotangent
):
    dp_count = lax.axis_size("dp")
    tensor_count = lax.axis_size("tensor")
    me = lax.axis_index("dp")
    images, tokens, width = features.shape
    head_dim = k_gain.shape[0]
    rows = features.reshape(images * tokens, width)
    gain = k_gain.reshape(1, head_dim)
    my_y, my_z = me // NZ, lax.rem(me, NZ)
    tensor = lax.axis_index("tensor")
    core = lax.rem(tensor, 2)

    image_ids = lax.broadcasted_iota(jnp.int32, (1, image_slot.shape[0]), 1)
    id_match = block_image[:, None] == image_ids
    slots = jnp.sum(jnp.where(id_match, image_slot[None, :], 0), axis=1).reshape(dp_count, -1)
    tiles = jnp.sum(jnp.where(id_match, image_tiles[None, :], 0), axis=1).reshape(dp_count, -1)
    my_slots = lax.dynamic_index_in_dim(slots, me, 0, keepdims=False)
    my_tiles = lax.dynamic_index_in_dim(tiles, me, 0, keepdims=False)
    first = jnp.concatenate(
        [jnp.ones((1,), jnp.int32), (my_slots[1:] != my_slots[:-1]).astype(jnp.int32)]
    )
    pos = jnp.max(jnp.where(slots // images == me, slots % images, -1), axis=1)
    place = jnp.stack([my_y, my_z, tensor // 2, core])
    place = jnp.pad(place, (0, pos.shape[0] - place.shape[0]))
    table = jnp.stack([pos, my_slots // images, my_tiles * (tokens // TILES), first, place])

    v_line = jnp.concatenate([shift_y(v_weight, (NY - i) % NY) for i in range(NY)])
    k_ring, v_ring = [k_weight], [v_line]
    for hop in range(1, NZ // 2):
        k_ring += [shift_z(k_ring[max(-2, -len(k_ring))], 1), shift_z(k_ring[-1], -1)]
        if hop == 1:
            v_ring += [shift_z(v_line, 1), shift_z(v_line, -1)]
    k_ring[-2], k_ring[-1], v_ring[-2], v_ring[-1] = lax.optimization_barrier(
        (k_ring[-2], k_ring[-1], v_ring[-2], v_ring[-1])
    )
    for hop in range(2, NZ // 2):
        v_ring += [shift_z(v_ring[-2], 1), shift_z(v_ring[-1], -1)]
    k_ring += [shift_z(k_ring[-2], 1)]
    v_ring += [shift_z(v_ring[-2], 1)]
    offsets = [0] + [z for hop in range(1, NZ // 2) for z in (NZ - hop, hop)] + [NZ // 2]
    v_zones = [[(y, z) for y in range(NY)] for z in offsets]
    k_line = jnp.concatenate(k_ring)
    half = k_line.shape[0] // 2
    after, before = shift_y(k_line, -1), shift_y(k_line, 1)
    pieces = [k_line, after, before, shift_y(after[:half], -1), shift_y(before[half:], 1)]
    k_zones = [[(y, z) for z in offsets] for y in (0, 1, NY - 1)]
    far = [(NY // 2, z) for z in offsets]
    k_zones += [far[: NZ // 2], far[NZ // 2 :]]
    pieces, zones = pieces + v_ring, k_zones + v_zones

    send, raw = project(
        table, rows, pieces, zones, gain, dp_count, images, tokens
    )
    kv = lax.all_to_all(send, "dp", 0, 0, tiled=True)

    rows_later, _ = lax.optimization_barrier((features, raw))
    span = width // NY
    col_pieces = [
        shift_y(
            lax.dynamic_slice(
                rows_later, (core, 0, (my_y + s) % NY * span), (1, tokens, span)
            )[0],
            s,
        )
        for s in range(NY)
    ]

    parts, probs, d_scores = attend(table, queries, cotangent, kv)
    parts, col_pieces, pieces = lax.optimization_barrier((parts, col_pieces, pieces))
    parts = lax.all_to_all(parts, "dp", 0, 0, tiled=True)
    own_cols = transpose_pieces(col_pieces)
    other_cols = swap_cores(own_cols, tensor_count)
    weights = list(assemble(table, pieces, zones, width, head_dim))
    weights += [swap_cores(w, tensor_count) for w in weights]
    attended, grad_queries = apply(table, kv, probs, d_scores, queries.shape)
    parts, other_cols, attended, grad_queries, weights = lax.optimization_barrier(
        (parts, other_cols, attended, grad_queries, weights)
    )
    grads, by_core = owner_grads(table, parts, raw, gain, images)

    lines = [shift_y(by_core, s) for s in range(NY)]
    shares = weight_terms(own_cols, other_cols, lines)
    other_grads = swap_cores(grads, tensor_count)
    shares, grads, other_grads = lax.optimization_barrier((shares, grads, other_grads))
    shares = lax.all_to_all(shares, "dp", 0, 0, tiled=True, axis_index_groups=Z_GROUPS)

    terms = list(feature_terms(table, grads, other_grads, weights, tensor_count))
    for s in range(1, tensor_count // 2):
        pairs = [(t, (t + 2 * s) % tensor_count) for t in range(tensor_count)]
        terms[s] = lax.ppermute(terms[s], "tensor", pairs)
    shares, terms = lax.optimization_barrier((shares, terms))
    grad_features = sum(term.astype(F32) for term in terms).astype(BF16)
    grad_features = grad_features.reshape(images, tokens // tensor_count, width)
    weight_grads = jnp.sum(shares.astype(F32), axis=0)
    return (
        attended,
        grad_queries,
        grad_features,
        weight_grads[:, :head_dim],
        weight_grads[:, head_dim:],
    )


def solution(mesh):
    in_specs = (
        P("dp", "tensor"),
        P("dp", None, None),
        P("dp", "tensor"),
        P("dp", "tensor"),
        P(),
        P(),
        P(),
        P(),
        P("dp", "tensor"),
    )
    out_specs = (
        P("dp", "tensor"),
        P("dp", "tensor"),
        P("dp", "tensor", None),
        P("dp", "tensor"),
        P("dp", "tensor"),
    )
    return jax.shard_map(local, mesh=mesh, in_specs=in_specs, out_specs=out_specs, check_vma=False)
```

```python
import functools

import jax
import jax.numpy as jnp
from jax import lax
from jax.experimental import pallas as pl
from jax.experimental.pallas import tpu as pltpu
from jax.sharding import PartitionSpec as P

TILES = 4
EPS = 1e-05
MASKED_SCORE = -1e30
NY, NZ = 4, 8
Y_GROUPS = [[y * NZ + z for y in range(NY)] for z in range(NZ)]
Z_GROUPS = [[y * NZ + z for z in range(NZ)] for y in range(NY)]
BF16, F32 = jnp.bfloat16, jnp.float32
MIB = 1024 * 1024
GROUP = 4
POS, OWNER, VALID, FIRST, PLACE = range(5)


def dot_dims(a, b, a_dim, b_dim):
    return lax.dot_general(
        a, b, (((a_dim,), (b_dim,)), ((), ())), preferred_element_type=F32
    )


def limit(mib):
    return pltpu.CompilerParams(vmem_limit_bytes=mib * MIB)


def cost(flops, mib):
    return pl.CostEstimate(flops=flops, bytes_accessed=mib * MIB, transcendentals=0)


def in_hbm():
    return pl.BlockSpec(memory_space=pltpu.HBM)


def in_vmem():
    return pl.BlockSpec(memory_space=pltpu.VMEM)


def in_hbm():
    return pl.BlockSpec(memory_space=pltpu.HBM)


def weight_blocks(table_ref, w_refs, zones):
    spots = {}
    for n, blocks in enumerate(zones):
        for i, at in enumerate(blocks):
            size = w_refs[n].shape[0] // len(blocks)
            spots.setdefault(at, []).append((w_refs[n], slice(i * size, (i + 1) * size)))
    found = []
    for (y_off, z_off), spot in spots.items():
        y = lax.rem(table_ref[PLACE, 0] + y_off, NY)
        z = lax.rem(table_ref[PLACE, 1] + z_off, NZ)
        size = spot[0][1].stop - spot[0][1].start
        found.append((pl.ds(pl.multiple_of((y * NZ + z) * size, size), size), spot, y_off, z))
    return found


def side_by_side(spot):
    return jnp.concatenate([ref[rows, :] for ref, rows in spot], axis=1)


def project_kernel(table_ref, f_ref, *refs, zones):
    w_refs, refs = refs[: len(zones)], refs[len(zones) :]
    gain_ref, send_ref, raw_ref, kv, held, sems = refs
    head_dim = gain_ref.shape[1]
    tokens = send_ref.shape[1]
    span = held.shape[2]
    copies = []
    for y_off in range(NY):
        y = lax.rem(table_ref[PLACE, 0] + y_off, NY)
        here = pl.ds(pl.multiple_of(y * span, span), span)
        copies.append(
            pltpu.make_async_copy(f_ref.at[:, here], held.at[y_off], sems.at[y_off])
        )
    for copy in copies:
        copy.start()
    total = jnp.zeros((f_ref.shape[0], 2 * head_dim), F32)
    blocks = weight_blocks(table_ref, w_refs, zones)
    for y_off in range(NY):
        copies[y_off].wait()
        for cols, spot, y_at, z in blocks:
            if y_at == y_off:
                here = pl.ds(pl.multiple_of(z * cols.size, cols.size), cols.size)
                total = total + jnp.dot(
                    held[y_off, :, here], side_by_side(spot), preferred_element_type=F32
                )
    raw = total[:, :head_dim]
    raw_ref[...] = raw
    scale = lax.rsqrt(jnp.mean(raw * raw, axis=-1, keepdims=True) + EPS)
    keys = (raw * scale * gain_ref[...]).astype(BF16)
    values = total[:, head_dim:].astype(BF16)
    for i in range(kv.shape[0]):
        kv[i, :, :head_dim] = keys[i * tokens : (i + 1) * tokens]
        kv[i, :, head_dim:] = values[i * tokens : (i + 1) * tokens]

    def put(d, carry):
        send_ref[d] = kv[jnp.maximum(table_ref[POS, d], 0)]
        return carry

    lax.fori_loop(0, send_ref.shape[0], put, 0, unroll=4)


def project(table, rows, pieces, zones, gain, dp, images, tokens):
    cols = 2 * gain.shape[1]
    return pl.pallas_call(
        functools.partial(project_kernel, zones=zones),
        grid_spec=pltpu.PrefetchScalarGridSpec(
            num_scalar_prefetch=1,
            grid=(),
            in_specs=[in_hbm()] + [in_vmem()] * (1 + len(pieces)),
            out_specs=[in_vmem()] * 2,
            scratch_shapes=[
                pltpu.VMEM((images, tokens, cols), BF16),
                pltpu.VMEM((NY, rows.shape[0], rows.shape[1] // NY), BF16),
                pltpu.SemaphoreType.DMA((NY,)),
            ],
        ),
        out_shape=[
            pltpu.HBM((dp, tokens, cols), BF16),
            pltpu.HBM((rows.shape[0], cols // 2), F32),
        ],
        compiler_params=limit(14),
        cost_estimate=cost(2 * rows.size * cols, 10),
        name="project",
    )(table, *hold(rows), *pieces, gain)


def load_heads(ref, start, rows, head_dim):
    heads = ref.shape[1] // head_dim
    return jnp.concatenate(
        [ref[pl.ds(start, rows), g * head_dim : (g + 1) * head_dim] for g in range(heads)],
        axis=0,
    )


def store_heads(ref, start, rows, head_dim, full):
    for g in range(ref.shape[1] // head_dim):
        ref[pl.ds(start, rows), g * head_dim : (g + 1) * head_dim] = full[
            g * rows : (g + 1) * rows
        ]


def attend_kernel(table_ref, q_hbm, ct_hbm, kv_ref, part_ref, probs_hbm, ds_hbm, *scratch):
    q_ref, ct_ref, probs_ref, ds_ref, acc, in_sems, out_sems = scratch
    blocks = table_ref.shape[1]
    steps = blocks // GROUP
    text = q_ref.shape[0] // steps

    def moves(step, pairs, size, sems):
        here = pl.ds(pl.multiple_of(step * size, size), size)
        return [
            pltpu.make_async_copy(a.at[here], b.at[here], sems.at[n, step])
            for n, (a, b) in enumerate(pairs)
        ]

    def fetch(step):
        return moves(step, ((q_hbm, q_ref), (ct_hbm, ct_ref)), text, in_sems)

    def stash(step):
        return moves(step, ((probs_ref, probs_hbm), (ds_ref, ds_hbm)), GROUP, out_sems)

    for step in range(steps):
        for copy in fetch(step):
            copy.start()
    rows = q_ref.shape[0] // blocks
    head_dim = kv_ref.shape[2] // 2
    tokens = kv_ref.shape[1]
    scale = head_dim**-0.5
    part_ref[...] = jnp.zeros_like(part_ref)
    acc[...] = jnp.zeros_like(acc)

    def some_blocks(step, carry):
        for copy in fetch(step):
            copy.wait()
        at = [step * GROUP + i for i in range(GROUP)]
        owners = [table_ref[OWNER, b] for b in at]
        starts = [pl.multiple_of(b * rows, rows) for b in at]
        queries = [load_heads(q_ref, s, rows, head_dim) for s in starts]
        grads = [load_heads(ct_ref, s, rows, head_dim) for s in starts]
        scores = [
            dot_dims(kv_ref[o, :, :head_dim], q, 1, 1) * scale for o, q in zip(owners, queries)
        ]
        d_probs = [dot_dims(kv_ref[o, :, head_dim:], g, 1, 1) for o, g in zip(owners, grads)]
        token = lax.broadcasted_iota(jnp.int32, (tokens, 1), 0)
        scores = [
            jnp.where(token < table_ref[VALID, b], s, MASKED_SCORE) for b, s in zip(at, scores)
        ]
        weights = [jnp.exp(s - jnp.max(s, axis=0, keepdims=True)) for s in scores]
        probs = [w * (1.0 / jnp.sum(w, axis=0, keepdims=True)) for w in weights]
        halves = [p.astype(BF16) for p in probs]
        deltas = [jnp.sum(p * d, axis=0, keepdims=True) for p, d in zip(probs, d_probs)]
        d_scores = [
            (p * (d - x) * scale).astype(BF16) for p, d, x in zip(probs, d_probs, deltas)
        ]
        key_parts = [
            jnp.dot(d, q, preferred_element_type=F32) for d, q in zip(d_scores, queries)
        ]
        value_parts = [
            jnp.dot(p, g, preferred_element_type=F32) for p, g in zip(halves, grads)
        ]
        key_run, value_run = acc[:, :head_dim], acc[:, head_dim:]
        for i, b in enumerate(at):
            keep = table_ref[FIRST, b] == 0
            key_run = key_parts[i] + jnp.where(keep, key_run, 0.0)
            value_run = value_parts[i] + jnp.where(keep, value_run, 0.0)
            part_ref[owners[i], :, :head_dim] = key_run.astype(BF16)
            part_ref[owners[i], :, head_dim:] = value_run.astype(BF16)
            probs_ref[b] = halves[i]
            ds_ref[b] = d_scores[i]
        acc[:, :head_dim] = key_run
        acc[:, head_dim:] = value_run
        for copy in stash(step):
            copy.start()
        return carry

    lax.fori_loop(0, steps, some_blocks, 0)
    for step in range(steps):
        for copy in stash(step):
            copy.wait()


def hold(*arrays):
    return [pltpu.with_memory_space_constraint(x, pltpu.HBM) for x in arrays]


def attend(table, queries, cotangent, kv):
    blocks, (_, tokens, cols) = table.shape[1], kv.shape
    rows = queries.size * 2 // (blocks * cols)
    stash = pltpu.HBM((blocks, tokens, rows), BF16)
    return pl.pallas_call(
        attend_kernel,
        grid_spec=pltpu.PrefetchScalarGridSpec(
            num_scalar_prefetch=1,
            grid=(),
            in_specs=[in_hbm()] * 2 + [in_vmem()],
            out_specs=[in_vmem()] + [in_hbm()] * 2,
            scratch_shapes=[pltpu.VMEM(queries.shape, BF16)] * 2
            + [pltpu.VMEM(stash.shape, BF16)] * 2
            + [pltpu.VMEM(kv.shape[1:], F32)]
            + [pltpu.SemaphoreType.DMA((2, blocks // GROUP))] * 2,
        ),
        out_shape=[pltpu.HBM(kv.shape, BF16), stash, stash],
        compiler_params=limit(13),
        cost_estimate=cost(8 * queries.size * tokens, 8),
        name="attend",
    )(table, *hold(queries, cotangent), kv)


def apply_kernel(table_ref, kv_ref, probs_ref, ds_ref, out_ref, gq_ref):
    blocks = table_ref.shape[1]
    rows = out_ref.shape[0] // blocks
    head_dim = kv_ref.shape[2] // 2

    def some_blocks(step, carry):
        at = [step * GROUP + i for i in range(GROUP)]
        owners = [table_ref[OWNER, b] for b in at]
        outs = [
            dot_dims(probs_ref[b], kv_ref[o, :, head_dim:], 0, 0) for b, o in zip(at, owners)
        ]
        gqs = [dot_dims(ds_ref[b], kv_ref[o, :, :head_dim], 0, 0) for b, o in zip(at, owners)]
        for i, b in enumerate(at):
            start = pl.multiple_of(b * rows, rows)
            store_heads(out_ref, start, rows, head_dim, outs[i].astype(BF16))
            store_heads(gq_ref, start, rows, head_dim, gqs[i].astype(BF16))
        return carry

    lax.fori_loop(0, blocks // GROUP, some_blocks, 0)


def apply(table, kv, probs, d_scores, shape):
    out = pltpu.HBM(shape, BF16)
    return pl.pallas_call(
        apply_kernel,
        grid_spec=pltpu.PrefetchScalarGridSpec(
            num_scalar_prefetch=1,
            grid=(),
            in_specs=[in_vmem()] * 3,
            out_specs=[in_vmem()] * 2,
        ),
        out_shape=[out, out],
        compiler_params=limit(9),
        cost_estimate=cost(4 * shape[0] * shape[1] * kv.shape[1], 6),
        name="apply",
    )(table, *hold(kv, probs, d_scores))


def owner_kernel(table_ref, part_ref, raw_ref, gain_ref, grad_ref, by_core_ref, acc):
    head_dim = gain_ref.shape[1]
    tokens = part_ref.shape[1]
    acc[...] = jnp.zeros_like(acc)

    def add(d, carry):
        @pl.when(table_ref[POS, d] >= 0)
        def _():
            acc[table_ref[POS, d]] += part_ref[d].astype(F32)

        return carry

    lax.fori_loop(0, part_ref.shape[0], add, 0)
    gain = gain_ref[...]
    for i in range(acc.shape[0]):
        here = slice(i * tokens, (i + 1) * tokens)
        raw = raw_ref[here]
        scale = lax.rsqrt(jnp.mean(raw * raw, axis=-1, keepdims=True) + EPS)
        scaled = acc[i, :, :head_dim] * gain
        pull = jnp.mean(raw * scaled, axis=-1, keepdims=True)
        grad = scale * scaled - raw * (scale * scale * scale * pull)
        grad_ref[here, :head_dim] = grad.astype(BF16)
        grad_ref[here, head_dim:] = acc[i, :, head_dim:].astype(BF16)
    for i in range(acc.shape[0]):
        at = pl.multiple_of(lax.rem(table_ref[PLACE, 3] + i, 2) * tokens, tokens)
        by_core_ref[i * tokens : (i + 1) * tokens, :] = grad_ref[pl.ds(at, tokens), :]


def owner_grads(table, parts, raw, gain, images):
    tokens, cols = parts.shape[1:]
    grads = jax.ShapeDtypeStruct((images * tokens, cols), BF16)
    return pl.pallas_call(
        owner_kernel,
        grid_spec=pltpu.PrefetchScalarGridSpec(
            num_scalar_prefetch=1,
            grid=(),
            in_specs=[in_vmem()] * 3,
            out_specs=[in_vmem()] * 2,
            scratch_shapes=[pltpu.VMEM((images, tokens, cols), F32)],
        ),
        out_shape=[grads, grads],
        compiler_params=limit(6),
        cost_estimate=cost(0, 3),
        name="owner_grads",
    )(table, *hold(parts, raw), gain)


def transpose_kernel(*refs):
    pieces, out_ref = refs[:-1], refs[-1]
    tokens = pieces[0].shape[0]
    for i, ref in enumerate(pieces):
        out_ref[:, i * tokens : (i + 1) * tokens] = ref[...].T


def transpose_pieces(pieces):
    tokens, width = pieces[0].shape
    return pl.pallas_call(
        transpose_kernel,
        in_specs=[in_vmem()] * len(pieces),
        out_specs=in_vmem(),
        out_shape=jax.ShapeDtypeStruct((width, tokens * len(pieces)), BF16),
        compiler_params=limit(7),
        cost_estimate=cost(0, 4),
        name="transpose_pieces",
    )(*hold(*pieces))


def weight_kernel(own_ref, other_ref, *refs):
    lines, out_ref = refs[:-1], refs[-1]
    half = lines[0].shape[0] // 2
    first = jnp.concatenate([ref[:half, :] for ref in lines], axis=0)
    second = jnp.concatenate([ref[half:, :] for ref in lines], axis=0)
    block = out_ref.shape[1]
    for i in range(out_ref.shape[0]):
        here = slice(i * block, (i + 1) * block)
        total = jnp.dot(own_ref[here, :], first, preferred_element_type=F32)
        total = total + jnp.dot(other_ref[here, :], second, preferred_element_type=F32)
        out_ref[i] = total.astype(BF16)


def weight_terms(own_cols, other_cols, lines):
    width, cols = own_cols.shape[0], lines[0].shape[1]
    return pl.pallas_call(
        weight_kernel,
        in_specs=[in_vmem()] * (2 + len(lines)),
        out_specs=in_vmem(),
        out_shape=pltpu.HBM((NZ, width // NZ, cols), BF16),
        compiler_params=limit(9),
        cost_estimate=cost(4 * own_cols.size * cols, 6),
        name="weight_terms",
    )(own_cols, other_cols, *lines)


def assemble_kernel(table_ref, *refs, zones):
    w_refs, out_refs = refs[:-2], refs[-2:]
    for here, spot, _, _ in weight_blocks(table_ref, w_refs, zones):
        for out_ref, (ref, rows) in zip(out_refs, spot):
            out_ref[here, :] = ref[rows, :]


def assemble(table, pieces, zones, width, head_dim):
    return pl.pallas_call(
        functools.partial(assemble_kernel, zones=zones),
        grid_spec=pltpu.PrefetchScalarGridSpec(
            num_scalar_prefetch=1,
            grid=(),
            in_specs=[in_vmem()] * len(pieces),
            out_specs=[in_vmem()] * 2,
        ),
        out_shape=[pltpu.HBM((width, head_dim), BF16)] * 2,
        compiler_params=limit(10),
        cost_estimate=cost(0, 1),
        name="assemble",
    )(table, *pieces)


def feature_kernel(table_ref, own_ref, other_ref, *refs, targets):
    w_refs, out_refs, (lhs, held, sems) = refs[:4], refs[4:-3], refs[-3:]
    chips = len(out_refs)
    tokens, head_dim = own_ref.shape[0] // 2, own_ref.shape[1] // 2
    share = tokens // targets
    steps, block = held.shape[1:3]
    copies = [
        [
            pltpu.make_async_copy(
                w_ref.at[pl.ds(step * block, block), :], held.at[n, step], sems.at[n, step]
            )
            for n, w_ref in enumerate(w_refs)
        ]
        for step in range(steps)
    ]
    for step in range(steps):
        for copy in copies[step]:
            copy.start()
    for core, ref in enumerate((own_ref, other_ref)):
        for chip in range(chips):
            target = lax.rem(table_ref[PLACE, 2] + chip, chips) * 2 + table_ref[PLACE, 3]
            for i in range(2):
                at = pl.multiple_of(i * tokens + target * share, share)
                to = (chip * 2 + i) * share
                for n in range(2):
                    lhs[core, n, to : to + share, :] = ref[
                        pl.ds(at, share), n * head_dim : (n + 1) * head_dim
                    ]
    for step in range(steps):
        part = 0.0
        for core in range(2):
            for n in range(2):
                copies[step][2 * core + n].wait()
            left = jnp.concatenate([lhs[core, 0], lhs[core, 1]], axis=1)
            right = jnp.concatenate([held[2 * core, step], held[2 * core + 1, step]], axis=1)
            part = part + dot_dims(left, right, 1, 1)
        for chip, ref in enumerate(out_refs):
            ref[:, step * block : (step + 1) * block] = part[
                chip * 2 * share : (chip + 1) * 2 * share
            ].astype(BF16)


def feature_terms(table, own, other, weights, targets):
    width, head_dim = weights[0].shape
    chips, steps = targets // 2, 8
    rows = own.shape[0] // targets
    return pl.pallas_call(
        functools.partial(feature_kernel, targets=targets),
        grid_spec=pltpu.PrefetchScalarGridSpec(
            num_scalar_prefetch=1,
            grid=(),
            in_specs=[in_vmem()] * 2 + [in_hbm()] * 4,
            out_specs=[in_vmem()] * chips,
            scratch_shapes=[
                pltpu.VMEM((2, 2, own.shape[0] // 2, head_dim), BF16),
                pltpu.VMEM((4, steps, width // steps, head_dim), BF16),
                pltpu.SemaphoreType.DMA((4, steps)),
            ],
        ),
        out_shape=[jax.ShapeDtypeStruct((rows, width), BF16)] * chips,
        compiler_params=limit(14),
        cost_estimate=cost(4 * own.size * width, 10),
        name="feature_terms",
    )(table, own, other, *hold(*weights))


def shift_y(x, by):
    if by == 0:
        return x
    pairs = [(y * NZ + z, (y + by) % NY * NZ + z) for y in range(NY) for z in range(NZ)]
    return lax.ppermute(x, "dp", pairs)


def shift_z(x, by):
    pairs = [(y * NZ + z, y * NZ + (z + by) % NZ) for y in range(NY) for z in range(NZ)]
    return lax.ppermute(x, "dp", pairs)


def swap_cores(x, count):
    return lax.ppermute(x, "tensor", [(t, t ^ 1) for t in range(count)])


def local(
    queries, features, k_weight, v_weight, k_gain, block_image, image_slot, image_tiles, cotangent
):
    dp_count = lax.axis_size("dp")
    tensor_count = lax.axis_size("tensor")
    me = lax.axis_index("dp")
    images, tokens, width = features.shape
    head_dim = k_gain.shape[0]
    rows = features.reshape(images * tokens, width)
    gain = k_gain.reshape(1, head_dim)
    my_y, my_z = me // NZ, lax.rem(me, NZ)
    tensor = lax.axis_index("tensor")
    core = lax.rem(tensor, 2)

    image_ids = lax.broadcasted_iota(jnp.int32, (1, image_slot.shape[0]), 1)
    id_match = block_image[:, None] == image_ids
    slots = jnp.sum(jnp.where(id_match, image_slot[None, :], 0), axis=1).reshape(dp_count, -1)
    tiles = jnp.sum(jnp.where(id_match, image_tiles[None, :], 0), axis=1).reshape(dp_count, -1)
    my_slots = lax.dynamic_index_in_dim(slots, me, 0, keepdims=False)
    my_tiles = lax.dynamic_index_in_dim(tiles, me, 0, keepdims=False)
    first = jnp.concatenate(
        [jnp.ones((1,), jnp.int32), (my_slots[1:] != my_slots[:-1]).astype(jnp.int32)]
    )
    pos = jnp.max(jnp.where(slots // images == me, slots % images, -1), axis=1)
    place = jnp.stack([my_y, my_z, tensor // 2, core])
    place = jnp.pad(place, (0, pos.shape[0] - place.shape[0]))
    table = jnp.stack([pos, my_slots // images, my_tiles * (tokens // TILES), first, place])

    v_line = jnp.concatenate([shift_y(v_weight, (NY - i) % NY) for i in range(NY)])
    k_ring, v_ring = [k_weight], [v_line]
    for hop in range(1, NZ // 2):
        k_ring += [shift_z(k_ring[max(-2, -len(k_ring))], 1), shift_z(k_ring[-1], -1)]
        if hop == 1:
            v_ring += [shift_z(v_line, 1), shift_z(v_line, -1)]
    k_ring[-2], k_ring[-1], v_ring[-2], v_ring[-1] = lax.optimization_barrier(
        (k_ring[-2], k_ring[-1], v_ring[-2], v_ring[-1])
    )
    for hop in range(2, NZ // 2):
        v_ring += [shift_z(v_ring[-2], 1), shift_z(v_ring[-1], -1)]
    k_ring += [shift_z(k_ring[-2], 1)]
    v_ring += [shift_z(v_ring[-2], 1)]
    offsets = [0] + [z for hop in range(1, NZ // 2) for z in (NZ - hop, hop)] + [NZ // 2]
    v_zones = [[(y, z) for y in range(NY)] for z in offsets]
    k_line = jnp.concatenate(k_ring)
    half = k_line.shape[0] // 2
    after, before = shift_y(k_line, -1), shift_y(k_line, 1)
    pieces = [k_line, after, before, shift_y(after[:half], -1), shift_y(before[half:], 1)]
    k_zones = [[(y, z) for z in offsets] for y in (0, 1, NY - 1)]
    far = [(NY // 2, z) for z in offsets]
    k_zones += [far[: NZ // 2], far[NZ // 2 :]]
    pieces, zones = pieces + v_ring, k_zones + v_zones

    send, raw = project(
        table, rows, pieces, zones, gain, dp_count, images, tokens
    )
    kv = lax.all_to_all(send, "dp", 0, 0, tiled=True)

    rows_later, _ = lax.optimization_barrier((features, raw))
    span = width // NY
    col_pieces = [
        shift_y(
            lax.dynamic_slice(
                rows_later, (core, 0, (my_y + s) % NY * span), (1, tokens, span)
            )[0],
            s,
        )
        for s in range(NY)
    ]

    parts, probs, d_scores = attend(table, queries, cotangent, kv)
    parts, col_pieces, pieces = lax.optimization_barrier((parts, col_pieces, pieces))
    parts = lax.all_to_all(parts, "dp", 0, 0, tiled=True)
    own_cols = transpose_pieces(col_pieces)
    other_cols = swap_cores(own_cols, tensor_count)
    weights = list(assemble(table, pieces, zones, width, head_dim))
    weights += [swap_cores(w, tensor_count) for w in weights]
    attended, grad_queries = apply(table, kv, probs, d_scores, queries.shape)
    parts, other_cols, attended, grad_queries, weights = lax.optimization_barrier(
        (parts, other_cols, attended, grad_queries, weights)
    )
    grads, by_core = owner_grads(table, parts, raw, gain, images)

    lines = [shift_y(by_core, s) for s in range(NY)]
    shares = weight_terms(own_cols, other_cols, lines)
    other_grads = swap_cores(grads, tensor_count)
    shares, grads, other_grads = lax.optimization_barrier((shares, grads, other_grads))
    shares = lax.all_to_all(shares, "dp", 0, 0, tiled=True, axis_index_groups=Z_GROUPS)

    terms = list(feature_terms(table, grads, other_grads, weights, tensor_count))
    for s in range(1, tensor_count // 2):
        pairs = [(t, (t + 2 * s) % tensor_count) for t in range(tensor_count)]
        terms[s] = lax.ppermute(terms[s], "tensor", pairs)
    shares, terms = lax.optimization_barrier((shares, terms))
    grad_features = sum(term.astype(F32) for term in terms).astype(BF16)
    grad_features = grad_features.reshape(images, tokens // tensor_count, width)
    weight_grads = jnp.sum(shares.astype(F32), axis=0)
    return (
        attended,
        grad_queries,
        grad_features,
        weight_grads[:, :head_dim],
        weight_grads[:, head_dim:],
    )


def solution(mesh):
    in_specs = (
        P("dp", "tensor"),
        P("dp", None, None),
        P("dp", "tensor"),
        P("dp", "tensor"),
        P(),
        P(),
        P(),
        P(),
        P("dp", "tensor"),
    )
    out_specs = (
        P("dp", "tensor"),
        P("dp", "tensor"),
        P("dp", "tensor", None),
        P("dp", "tensor"),
        P("dp", "tensor"),
    )
    return jax.shard_map(local, mesh=mesh, in_specs=in_specs, out_specs=out_specs, check_vma=False)
```

```python
import functools

import jax
import jax.numpy as jnp
from jax import lax
from jax.experimental import pallas as pl
from jax.experimental.pallas import tpu as pltpu
from jax.sharding import PartitionSpec as P

TILES = 4
EPS = 1e-05
MASKED_SCORE = -1e30
NY, NZ = 4, 8
Y_GROUPS = [[y * NZ + z for y in range(NY)] for z in range(NZ)]
Z_GROUPS = [[y * NZ + z for z in range(NZ)] for y in range(NY)]
BF16, F32 = jnp.bfloat16, jnp.float32
MIB = 1024 * 1024
GROUP = 4
POS, OWNER, VALID, FIRST, PLACE = range(5)


def dot_dims(a, b, a_dim, b_dim):
    return lax.dot_general(
        a, b, (((a_dim,), (b_dim,)), ((), ())), preferred_element_type=F32
    )


def limit(mib):
    return pltpu.CompilerParams(vmem_limit_bytes=mib * MIB)


def cost(flops, mib):
    return pl.CostEstimate(flops=flops, bytes_accessed=mib * MIB, transcendentals=0)


def in_hbm():
    return pl.BlockSpec(memory_space=pltpu.HBM)


def in_vmem():
    return pl.BlockSpec(memory_space=pltpu.VMEM)


def in_hbm():
    return pl.BlockSpec(memory_space=pltpu.HBM)


def weight_blocks(table_ref, w_refs, zones):
    spots = {}
    for n, blocks in enumerate(zones):
        for i, at in enumerate(blocks):
            size = w_refs[n].shape[0] // len(blocks)
            spots.setdefault(at, []).append((w_refs[n], slice(i * size, (i + 1) * size)))
    found = []
    for (y_off, z_off), spot in spots.items():
        y = lax.rem(table_ref[PLACE, 0] + y_off, NY)
        z = lax.rem(table_ref[PLACE, 1] + z_off, NZ)
        size = spot[0][1].stop - spot[0][1].start
        found.append((pl.ds(pl.multiple_of((y * NZ + z) * size, size), size), spot, y_off, z))
    return found


def side_by_side(spot):
    return jnp.concatenate([ref[rows, :] for ref, rows in spot], axis=1)


def project_kernel(table_ref, f_ref, *refs, zones):
    w_refs, (gain_ref, send_ref, raw_ref, kv) = refs[: len(zones)], refs[len(zones) :]
    head_dim = gain_ref.shape[1]
    tokens = send_ref.shape[1]
    total = jnp.zeros((f_ref.shape[0], 2 * head_dim), F32)
    for cols, spot, _, _ in weight_blocks(table_ref, w_refs, zones):
        total = total + jnp.dot(f_ref[:, cols], side_by_side(spot), preferred_element_type=F32)
    raw = total[:, :head_dim]
    raw_ref[...] = raw
    scale = lax.rsqrt(jnp.mean(raw * raw, axis=-1, keepdims=True) + EPS)
    keys = (raw * scale * gain_ref[...]).astype(BF16)
    values = total[:, head_dim:].astype(BF16)
    for i in range(kv.shape[0]):
        kv[i, :, :head_dim] = keys[i * tokens : (i + 1) * tokens]
        kv[i, :, head_dim:] = values[i * tokens : (i + 1) * tokens]

    def put(d, carry):
        send_ref[d] = kv[jnp.maximum(table_ref[POS, d], 0)]
        return carry

    lax.fori_loop(0, send_ref.shape[0], put, 0, unroll=4)


def project(table, rows, pieces, zones, gain, dp, images, tokens):
    cols = 2 * gain.shape[1]
    return pl.pallas_call(
        functools.partial(project_kernel, zones=zones),
        grid_spec=pltpu.PrefetchScalarGridSpec(
            num_scalar_prefetch=1,
            grid=(),
            in_specs=[in_vmem()] * (2 + len(pieces)),
            out_specs=[in_vmem()] * 2,
            scratch_shapes=[pltpu.VMEM((images, tokens, cols), BF16)],
        ),
        out_shape=[
            pltpu.HBM((dp, tokens, cols), BF16),
            pltpu.HBM((rows.shape[0], cols // 2), F32),
        ],
        compiler_params=limit(14),
        cost_estimate=cost(2 * rows.size * cols, 10),
        name="project",
    )(table, *hold(rows), *pieces, gain)


def load_heads(ref, start, rows, head_dim):
    heads = ref.shape[1] // head_dim
    return jnp.concatenate(
        [ref[pl.ds(start, rows), g * head_dim : (g + 1) * head_dim] for g in range(heads)],
        axis=0,
    )


def store_heads(ref, start, rows, head_dim, full):
    for g in range(ref.shape[1] // head_dim):
        ref[pl.ds(start, rows), g * head_dim : (g + 1) * head_dim] = full[
            g * rows : (g + 1) * rows
        ]


def attend_kernel(table_ref, q_hbm, ct_hbm, kv_ref, part_ref, probs_hbm, ds_hbm, *scratch):
    q_ref, ct_ref, probs_ref, ds_ref, acc, in_sems, out_sems = scratch
    blocks = table_ref.shape[1]
    steps = blocks // GROUP
    text = q_ref.shape[0] // steps

    def moves(step, pairs, size, sems):
        here = pl.ds(pl.multiple_of(step * size, size), size)
        return [
            pltpu.make_async_copy(a.at[here], b.at[here], sems.at[n, step])
            for n, (a, b) in enumerate(pairs)
        ]

    def fetch(step):
        return moves(step, ((q_hbm, q_ref), (ct_hbm, ct_ref)), text, in_sems)

    def stash(step):
        return moves(step, ((probs_ref, probs_hbm), (ds_ref, ds_hbm)), GROUP, out_sems)

    for step in range(steps):
        for copy in fetch(step):
            copy.start()
    rows = q_ref.shape[0] // blocks
    head_dim = kv_ref.shape[2] // 2
    tokens = kv_ref.shape[1]
    scale = head_dim**-0.5
    part_ref[...] = jnp.zeros_like(part_ref)
    acc[...] = jnp.zeros_like(acc)

    def some_blocks(step, carry):
        for copy in fetch(step):
            copy.wait()
        at = [step * GROUP + i for i in range(GROUP)]
        owners = [table_ref[OWNER, b] for b in at]
        starts = [pl.multiple_of(b * rows, rows) for b in at]
        queries = [load_heads(q_ref, s, rows, head_dim) for s in starts]
        grads = [load_heads(ct_ref, s, rows, head_dim) for s in starts]
        scores = [
            dot_dims(kv_ref[o, :, :head_dim], q, 1, 1) * scale for o, q in zip(owners, queries)
        ]
        d_probs = [dot_dims(kv_ref[o, :, head_dim:], g, 1, 1) for o, g in zip(owners, grads)]
        token = lax.broadcasted_iota(jnp.int32, (tokens, 1), 0)
        scores = [
            jnp.where(token < table_ref[VALID, b], s, MASKED_SCORE) for b, s in zip(at, scores)
        ]
        weights = [jnp.exp(s - jnp.max(s, axis=0, keepdims=True)) for s in scores]
        probs = [w * (1.0 / jnp.sum(w, axis=0, keepdims=True)) for w in weights]
        halves = [p.astype(BF16) for p in probs]
        deltas = [jnp.sum(p * d, axis=0, keepdims=True) for p, d in zip(probs, d_probs)]
        d_scores = [
            (p * (d - x) * scale).astype(BF16) for p, d, x in zip(probs, d_probs, deltas)
        ]
        key_parts = [
            jnp.dot(d, q, preferred_element_type=F32) for d, q in zip(d_scores, queries)
        ]
        value_parts = [
            jnp.dot(p, g, preferred_element_type=F32) for p, g in zip(halves, grads)
        ]
        key_run, value_run = acc[:, :head_dim], acc[:, head_dim:]
        for i, b in enumerate(at):
            keep = table_ref[FIRST, b] == 0
            key_run = key_parts[i] + jnp.where(keep, key_run, 0.0)
            value_run = value_parts[i] + jnp.where(keep, value_run, 0.0)
            part_ref[owners[i], :, :head_dim] = key_run.astype(BF16)
            part_ref[owners[i], :, head_dim:] = value_run.astype(BF16)
            probs_ref[b] = halves[i]
            ds_ref[b] = d_scores[i]
        acc[:, :head_dim] = key_run
        acc[:, head_dim:] = value_run
        for copy in stash(step):
            copy.start()
        return carry

    lax.fori_loop(0, steps, some_blocks, 0)
    for step in range(steps):
        for copy in stash(step):
            copy.wait()


def hold(*arrays):
    return [pltpu.with_memory_space_constraint(x, pltpu.HBM) for x in arrays]


def attend(table, queries, cotangent, kv):
    blocks, (_, tokens, cols) = table.shape[1], kv.shape
    rows = queries.size * 2 // (blocks * cols)
    stash = pltpu.HBM((blocks, tokens, rows), BF16)
    return pl.pallas_call(
        attend_kernel,
        grid_spec=pltpu.PrefetchScalarGridSpec(
            num_scalar_prefetch=1,
            grid=(),
            in_specs=[in_hbm()] * 2 + [in_vmem()],
            out_specs=[in_vmem()] + [in_hbm()] * 2,
            scratch_shapes=[pltpu.VMEM(queries.shape, BF16)] * 2
            + [pltpu.VMEM(stash.shape, BF16)] * 2
            + [pltpu.VMEM(kv.shape[1:], F32)]
            + [pltpu.SemaphoreType.DMA((2, blocks // GROUP))] * 2,
        ),
        out_shape=[pltpu.HBM(kv.shape, BF16), stash, stash],
        compiler_params=limit(13),
        cost_estimate=cost(8 * queries.size * tokens, 8),
        name="attend",
    )(table, *hold(queries, cotangent), kv)


def apply_kernel(table_ref, kv_ref, probs_ref, ds_ref, out_ref, gq_ref):
    blocks = table_ref.shape[1]
    rows = out_ref.shape[0] // blocks
    head_dim = kv_ref.shape[2] // 2

    def some_blocks(step, carry):
        at = [step * GROUP + i for i in range(GROUP)]
        owners = [table_ref[OWNER, b] for b in at]
        outs = [
            dot_dims(probs_ref[b], kv_ref[o, :, head_dim:], 0, 0) for b, o in zip(at, owners)
        ]
        gqs = [dot_dims(ds_ref[b], kv_ref[o, :, :head_dim], 0, 0) for b, o in zip(at, owners)]
        for i, b in enumerate(at):
            start = pl.multiple_of(b * rows, rows)
            store_heads(out_ref, start, rows, head_dim, outs[i].astype(BF16))
            store_heads(gq_ref, start, rows, head_dim, gqs[i].astype(BF16))
        return carry

    lax.fori_loop(0, blocks // GROUP, some_blocks, 0)


def apply(table, kv, probs, d_scores, shape):
    out = pltpu.HBM(shape, BF16)
    return pl.pallas_call(
        apply_kernel,
        grid_spec=pltpu.PrefetchScalarGridSpec(
            num_scalar_prefetch=1,
            grid=(),
            in_specs=[in_vmem()] * 3,
            out_specs=[in_vmem()] * 2,
        ),
        out_shape=[out, out],
        compiler_params=limit(9),
        cost_estimate=cost(4 * shape[0] * shape[1] * kv.shape[1], 6),
        name="apply",
    )(table, *hold(kv, probs, d_scores))


def owner_kernel(table_ref, part_ref, raw_ref, gain_ref, grad_ref, by_core_ref, acc):
    head_dim = gain_ref.shape[1]
    tokens = part_ref.shape[1]
    acc[...] = jnp.zeros_like(acc)

    def add(d, carry):
        @pl.when(table_ref[POS, d] >= 0)
        def _():
            acc[table_ref[POS, d]] += part_ref[d].astype(F32)

        return carry

    lax.fori_loop(0, part_ref.shape[0], add, 0)
    gain = gain_ref[...]
    for i in range(acc.shape[0]):
        here = slice(i * tokens, (i + 1) * tokens)
        raw = raw_ref[here]
        scale = lax.rsqrt(jnp.mean(raw * raw, axis=-1, keepdims=True) + EPS)
        scaled = acc[i, :, :head_dim] * gain
        pull = jnp.mean(raw * scaled, axis=-1, keepdims=True)
        grad = scale * scaled - raw * (scale * scale * scale * pull)
        grad_ref[here, :head_dim] = grad.astype(BF16)
        grad_ref[here, head_dim:] = acc[i, :, head_dim:].astype(BF16)
    for i in range(acc.shape[0]):
        at = pl.multiple_of(lax.rem(table_ref[PLACE, 3] + i, 2) * tokens, tokens)
        by_core_ref[i * tokens : (i + 1) * tokens, :] = grad_ref[pl.ds(at, tokens), :]


def owner_grads(table, parts, raw, gain, images):
    tokens, cols = parts.shape[1:]
    grads = jax.ShapeDtypeStruct((images * tokens, cols), BF16)
    return pl.pallas_call(
        owner_kernel,
        grid_spec=pltpu.PrefetchScalarGridSpec(
            num_scalar_prefetch=1,
            grid=(),
            in_specs=[in_vmem()] * 3,
            out_specs=[in_vmem()] * 2,
            scratch_shapes=[pltpu.VMEM((images, tokens, cols), F32)],
        ),
        out_shape=[grads, grads],
        compiler_params=limit(6),
        cost_estimate=cost(0, 3),
        name="owner_grads",
    )(table, *hold(parts, raw), gain)


def transpose_kernel(*refs):
    pieces, out_ref = refs[:-1], refs[-1]
    tokens = pieces[0].shape[0]
    for i, ref in enumerate(pieces):
        out_ref[:, i * tokens : (i + 1) * tokens] = ref[...].T


def transpose_pieces(pieces):
    tokens, width = pieces[0].shape
    return pl.pallas_call(
        transpose_kernel,
        in_specs=[in_vmem()] * len(pieces),
        out_specs=in_vmem(),
        out_shape=jax.ShapeDtypeStruct((width, tokens * len(pieces)), BF16),
        compiler_params=limit(7),
        cost_estimate=cost(0, 4),
        name="transpose_pieces",
    )(*hold(*pieces))


def weight_kernel(own_ref, other_ref, *refs):
    lines, out_ref = refs[:-1], refs[-1]
    half = lines[0].shape[0] // 2
    first = jnp.concatenate([ref[:half, :] for ref in lines], axis=0)
    second = jnp.concatenate([ref[half:, :] for ref in lines], axis=0)
    block = out_ref.shape[1]
    for i in range(out_ref.shape[0]):
        here = slice(i * block, (i + 1) * block)
        total = jnp.dot(own_ref[here, :], first, preferred_element_type=F32)
        total = total + jnp.dot(other_ref[here, :], second, preferred_element_type=F32)
        out_ref[i] = total.astype(BF16)


def weight_terms(own_cols, other_cols, lines):
    width, cols = own_cols.shape[0], lines[0].shape[1]
    return pl.pallas_call(
        weight_kernel,
        in_specs=[in_vmem()] * (2 + len(lines)),
        out_specs=in_vmem(),
        out_shape=pltpu.HBM((NZ, width // NZ, cols), BF16),
        compiler_params=limit(9),
        cost_estimate=cost(4 * own_cols.size * cols, 6),
        name="weight_terms",
    )(own_cols, other_cols, *lines)


def assemble_kernel(table_ref, *refs, zones):
    w_refs, out_refs = refs[:-2], refs[-2:]
    for here, spot, _, _ in weight_blocks(table_ref, w_refs, zones):
        for out_ref, (ref, rows) in zip(out_refs, spot):
            out_ref[here, :] = ref[rows, :]


def assemble(table, pieces, zones, width, head_dim):
    return pl.pallas_call(
        functools.partial(assemble_kernel, zones=zones),
        grid_spec=pltpu.PrefetchScalarGridSpec(
            num_scalar_prefetch=1,
            grid=(),
            in_specs=[in_vmem()] * len(pieces),
            out_specs=[in_vmem()] * 2,
        ),
        out_shape=[pltpu.HBM((width, head_dim), BF16)] * 2,
        compiler_params=limit(10),
        cost_estimate=cost(0, 1),
        name="assemble",
    )(table, *pieces)


def feature_kernel(table_ref, own_ref, other_ref, *refs, targets):
    w_refs, out_refs, (lhs, held, sems) = refs[:4], refs[4:-3], refs[-3:]
    chips = len(out_refs)
    tokens, head_dim = own_ref.shape[0] // 2, own_ref.shape[1] // 2
    share = tokens // targets
    steps, block = held.shape[1:3]
    copies = [
        [
            pltpu.make_async_copy(
                w_ref.at[pl.ds(step * block, block), :], held.at[n, step], sems.at[n, step]
            )
            for n, w_ref in enumerate(w_refs)
        ]
        for step in range(steps)
    ]
    for step in range(steps):
        for copy in copies[step]:
            copy.start()
    for core, ref in enumerate((own_ref, other_ref)):
        for chip in range(chips):
            target = lax.rem(table_ref[PLACE, 2] + chip, chips) * 2 + table_ref[PLACE, 3]
            for i in range(2):
                at = pl.multiple_of(i * tokens + target * share, share)
                to = (chip * 2 + i) * share
                for n in range(2):
                    lhs[core, n, to : to + share, :] = ref[
                        pl.ds(at, share), n * head_dim : (n + 1) * head_dim
                    ]
    for step in range(steps):
        part = 0.0
        for core in range(2):
            for n in range(2):
                copies[step][2 * core + n].wait()
            left = jnp.concatenate([lhs[core, 0], lhs[core, 1]], axis=1)
            right = jnp.concatenate([held[2 * core, step], held[2 * core + 1, step]], axis=1)
            part = part + dot_dims(left, right, 1, 1)
        for chip, ref in enumerate(out_refs):
            ref[:, step * block : (step + 1) * block] = part[
                chip * 2 * share : (chip + 1) * 2 * share
            ].astype(BF16)


def feature_terms(table, own, other, weights, targets):
    width, head_dim = weights[0].shape
    chips, steps = targets // 2, 8
    rows = own.shape[0] // targets
    return pl.pallas_call(
        functools.partial(feature_kernel, targets=targets),
        grid_spec=pltpu.PrefetchScalarGridSpec(
            num_scalar_prefetch=1,
            grid=(),
            in_specs=[in_vmem()] * 2 + [in_hbm()] * 4,
            out_specs=[in_vmem()] * chips,
            scratch_shapes=[
                pltpu.VMEM((2, 2, own.shape[0] // 2, head_dim), BF16),
                pltpu.VMEM((4, steps, width // steps, head_dim), BF16),
                pltpu.SemaphoreType.DMA((4, steps)),
            ],
        ),
        out_shape=[jax.ShapeDtypeStruct((rows, width), BF16)] * chips,
        compiler_params=limit(14),
        cost_estimate=cost(4 * own.size * width, 10),
        name="feature_terms",
    )(table, own, other, *hold(*weights))


def shift_y(x, by):
    if by == 0:
        return x
    pairs = [(y * NZ + z, (y + by) % NY * NZ + z) for y in range(NY) for z in range(NZ)]
    return lax.ppermute(x, "dp", pairs)


def shift_z(x, by):
    pairs = [(y * NZ + z, y * NZ + (z + by) % NZ) for y in range(NY) for z in range(NZ)]
    return lax.ppermute(x, "dp", pairs)


def swap_cores(x, count):
    return lax.ppermute(x, "tensor", [(t, t ^ 1) for t in range(count)])


def local(
    queries, features, k_weight, v_weight, k_gain, block_image, image_slot, image_tiles, cotangent
):
    dp_count = lax.axis_size("dp")
    tensor_count = lax.axis_size("tensor")
    me = lax.axis_index("dp")
    images, tokens, width = features.shape
    head_dim = k_gain.shape[0]
    rows = features.reshape(images * tokens, width)
    gain = k_gain.reshape(1, head_dim)
    my_y, my_z = me // NZ, lax.rem(me, NZ)
    tensor = lax.axis_index("tensor")
    core = lax.rem(tensor, 2)

    image_ids = lax.broadcasted_iota(jnp.int32, (1, image_slot.shape[0]), 1)
    id_match = block_image[:, None] == image_ids
    slots = jnp.sum(jnp.where(id_match, image_slot[None, :], 0), axis=1).reshape(dp_count, -1)
    tiles = jnp.sum(jnp.where(id_match, image_tiles[None, :], 0), axis=1).reshape(dp_count, -1)
    my_slots = lax.dynamic_index_in_dim(slots, me, 0, keepdims=False)
    my_tiles = lax.dynamic_index_in_dim(tiles, me, 0, keepdims=False)
    first = jnp.concatenate(
        [jnp.ones((1,), jnp.int32), (my_slots[1:] != my_slots[:-1]).astype(jnp.int32)]
    )
    pos = jnp.max(jnp.where(slots // images == me, slots % images, -1), axis=1)
    place = jnp.stack([my_y, my_z, tensor // 2, core])
    place = jnp.pad(place, (0, pos.shape[0] - place.shape[0]))
    table = jnp.stack([pos, my_slots // images, my_tiles * (tokens // TILES), first, place])

    v_line = jnp.concatenate([shift_y(v_weight, (NY - i) % NY) for i in range(NY)])
    k_ring, v_ring = [k_weight], [v_line]
    for hop in range(1, NZ // 2):
        k_ring += [shift_z(k_ring[max(-2, -len(k_ring))], 1), shift_z(k_ring[-1], -1)]
        if hop == 1:
            v_ring += [shift_z(v_line, 1), shift_z(v_line, -1)]
    k_ring[-2], k_ring[-1], v_ring[-2], v_ring[-1] = lax.optimization_barrier(
        (k_ring[-2], k_ring[-1], v_ring[-2], v_ring[-1])
    )
    for hop in range(2, NZ // 2):
        v_ring += [shift_z(v_ring[-2], 1), shift_z(v_ring[-1], -1)]
    k_ring += [shift_z(k_ring[-2], 1)]
    v_ring += [shift_z(v_ring[-2], 1)]
    offsets = [0] + [z for hop in range(1, NZ // 2) for z in (NZ - hop, hop)] + [NZ // 2]
    v_zones = [[(y, z) for y in range(NY)] for z in offsets]
    k_pieces, k_zones = [], []
    for part in (slice(0, NZ // 2), slice(NZ // 2, NZ)):
        k_line = jnp.concatenate(k_ring[part])
        after, before = shift_y(k_line, -1), shift_y(k_line, 1)
        far = shift_y(before, 1) if part.start else shift_y(after, -1)
        k_pieces += [k_line, after, before, far]
        k_zones += [[(y, z) for z in offsets[part]] for y in (0, 1, NY - 1, NY // 2)]
    pieces, zones = k_pieces + v_ring, k_zones + v_zones

    send, raw = project(
        table, rows, pieces, zones, gain, dp_count, images, tokens
    )
    kv = lax.all_to_all(send, "dp", 0, 0, tiled=True)

    rows_later, _ = lax.optimization_barrier((features, raw))
    span = width // NY
    col_pieces = [
        shift_y(
            lax.dynamic_slice(
                rows_later, (core, 0, (my_y + s) % NY * span), (1, tokens, span)
            )[0],
            s,
        )
        for s in range(NY)
    ]

    parts, probs, d_scores = attend(table, queries, cotangent, kv)
    parts, col_pieces, pieces = lax.optimization_barrier((parts, col_pieces, pieces))
    parts = lax.all_to_all(parts, "dp", 0, 0, tiled=True)
    own_cols = transpose_pieces(col_pieces)
    other_cols = swap_cores(own_cols, tensor_count)
    weights = list(assemble(table, pieces, zones, width, head_dim))
    weights += [swap_cores(w, tensor_count) for w in weights]
    attended, grad_queries = apply(table, kv, probs, d_scores, queries.shape)
    parts, other_cols, attended, grad_queries, weights = lax.optimization_barrier(
        (parts, other_cols, attended, grad_queries, weights)
    )
    grads, by_core = owner_grads(table, parts, raw, gain, images)

    lines = [shift_y(by_core, s) for s in range(NY)]
    shares = weight_terms(own_cols, other_cols, lines)
    other_grads = swap_cores(grads, tensor_count)
    shares, grads, other_grads = lax.optimization_barrier((shares, grads, other_grads))
    shares = lax.all_to_all(shares, "dp", 0, 0, tiled=True, axis_index_groups=Z_GROUPS)

    terms = list(feature_terms(table, grads, other_grads, weights, tensor_count))
    for s in range(1, tensor_count // 2):
        pairs = [(t, (t + 2 * s) % tensor_count) for t in range(tensor_count)]
        terms[s] = lax.ppermute(terms[s], "tensor", pairs)
    shares, terms = lax.optimization_barrier((shares, terms))
    grad_features = sum(term.astype(F32) for term in terms).astype(BF16)
    grad_features = grad_features.reshape(images, tokens // tensor_count, width)
    weight_grads = jnp.sum(shares.astype(F32), axis=0)
    return (
        attended,
        grad_queries,
        grad_features,
        weight_grads[:, :head_dim],
        weight_grads[:, head_dim:],
    )


def solution(mesh):
    in_specs = (
        P("dp", "tensor"),
        P("dp", None, None),
        P("dp", "tensor"),
        P("dp", "tensor"),
        P(),
        P(),
        P(),
        P(),
        P("dp", "tensor"),
    )
    out_specs = (
        P("dp", "tensor"),
        P("dp", "tensor"),
        P("dp", "tensor", None),
        P("dp", "tensor"),
        P("dp", "tensor"),
    )
    return jax.shard_map(local, mesh=mesh, in_specs=in_specs, out_specs=out_specs, check_vma=False)
```

```python
import functools

import jax
import jax.numpy as jnp
from jax import lax
from jax.experimental import pallas as pl
from jax.experimental.pallas import tpu as pltpu
from jax.sharding import PartitionSpec as P

TILES = 4
EPS = 1e-05
MASKED_SCORE = -1e30
NY, NZ = 4, 8
Y_GROUPS = [[y * NZ + z for y in range(NY)] for z in range(NZ)]
Z_GROUPS = [[y * NZ + z for z in range(NZ)] for y in range(NY)]
BF16, F32 = jnp.bfloat16, jnp.float32
MIB = 1024 * 1024
GROUP = 4
POS, OWNER, VALID, FIRST, PLACE = range(5)


def dot_dims(a, b, a_dim, b_dim):
    return lax.dot_general(
        a, b, (((a_dim,), (b_dim,)), ((), ())), preferred_element_type=F32
    )


def limit(mib):
    return pltpu.CompilerParams(vmem_limit_bytes=mib * MIB)


def cost(flops, mib):
    return pl.CostEstimate(flops=flops, bytes_accessed=mib * MIB, transcendentals=0)


def in_hbm():
    return pl.BlockSpec(memory_space=pltpu.HBM)


def in_vmem():
    return pl.BlockSpec(memory_space=pltpu.VMEM)


def in_hbm():
    return pl.BlockSpec(memory_space=pltpu.HBM)


def weight_blocks(table_ref, w_refs, zones):
    spots = {}
    for n, blocks in enumerate(zones):
        for i, at in enumerate(blocks):
            size = w_refs[n].shape[0] // len(blocks)
            spots.setdefault(at, []).append((w_refs[n], slice(i * size, (i + 1) * size)))
    found = []
    for (y_off, z_off), spot in spots.items():
        y = lax.rem(table_ref[PLACE, 0] + y_off, NY)
        z = lax.rem(table_ref[PLACE, 1] + z_off, NZ)
        size = spot[0][1].stop - spot[0][1].start
        found.append((pl.ds(pl.multiple_of((y * NZ + z) * size, size), size), spot, y_off, z))
    return found


def side_by_side(spot):
    return jnp.concatenate([ref[rows, :] for ref, rows in spot], axis=1)


def project_kernel(table_ref, f_ref, *refs, zones):
    w_refs, (gain_ref, send_ref, raw_ref, kv) = refs[: len(zones)], refs[len(zones) :]
    head_dim = gain_ref.shape[1]
    tokens = send_ref.shape[1]
    total = jnp.zeros((f_ref.shape[0], 2 * head_dim), F32)
    for cols, spot, _, _ in weight_blocks(table_ref, w_refs, zones):
        total = total + jnp.dot(f_ref[:, cols], side_by_side(spot), preferred_element_type=F32)
    raw = total[:, :head_dim]
    raw_ref[...] = raw
    scale = lax.rsqrt(jnp.mean(raw * raw, axis=-1, keepdims=True) + EPS)
    keys = (raw * scale * gain_ref[...]).astype(BF16)
    values = total[:, head_dim:].astype(BF16)
    for i in range(kv.shape[0]):
        kv[i, :, :head_dim] = keys[i * tokens : (i + 1) * tokens]
        kv[i, :, head_dim:] = values[i * tokens : (i + 1) * tokens]

    def put(d, carry):
        send_ref[d] = kv[jnp.maximum(table_ref[POS, d], 0)]
        return carry

    lax.fori_loop(0, send_ref.shape[0], put, 0, unroll=4)


def project(table, rows, pieces, zones, gain, dp, images, tokens):
    cols = 2 * gain.shape[1]
    return pl.pallas_call(
        functools.partial(project_kernel, zones=zones),
        grid_spec=pltpu.PrefetchScalarGridSpec(
            num_scalar_prefetch=1,
            grid=(),
            in_specs=[in_vmem()] * (2 + len(pieces)),
            out_specs=[in_vmem()] * 2,
            scratch_shapes=[pltpu.VMEM((images, tokens, cols), BF16)],
        ),
        out_shape=[
            pltpu.HBM((dp, tokens, cols), BF16),
            pltpu.HBM((rows.shape[0], cols // 2), F32),
        ],
        compiler_params=limit(14),
        cost_estimate=cost(2 * rows.size * cols, 10),
        name="project",
    )(table, *hold(rows), *pieces, gain)


def load_heads(ref, start, rows, head_dim):
    heads = ref.shape[1] // head_dim
    return jnp.concatenate(
        [ref[pl.ds(start, rows), g * head_dim : (g + 1) * head_dim] for g in range(heads)],
        axis=0,
    )


def store_heads(ref, start, rows, head_dim, full):
    for g in range(ref.shape[1] // head_dim):
        ref[pl.ds(start, rows), g * head_dim : (g + 1) * head_dim] = full[
            g * rows : (g + 1) * rows
        ]


def attend_kernel(table_ref, q_hbm, ct_hbm, kv_ref, part_ref, probs_hbm, ds_hbm, *scratch):
    q_ref, ct_ref, probs_ref, ds_ref, acc, in_sems, out_sems = scratch
    blocks = table_ref.shape[1]
    steps = blocks // GROUP
    text = q_ref.shape[0] // steps

    def moves(step, pairs, size, sems):
        here = pl.ds(pl.multiple_of(step * size, size), size)
        return [
            pltpu.make_async_copy(a.at[here], b.at[here], sems.at[n, step])
            for n, (a, b) in enumerate(pairs)
        ]

    def fetch(step):
        return moves(step, ((q_hbm, q_ref), (ct_hbm, ct_ref)), text, in_sems)

    def stash(step):
        return moves(step, ((probs_ref, probs_hbm), (ds_ref, ds_hbm)), GROUP, out_sems)

    for step in range(steps):
        for copy in fetch(step):
            copy.start()
    rows = q_ref.shape[0] // blocks
    head_dim = kv_ref.shape[2] // 2
    tokens = kv_ref.shape[1]
    scale = head_dim**-0.5
    part_ref[...] = jnp.zeros_like(part_ref)
    acc[...] = jnp.zeros_like(acc)

    def some_blocks(step, carry):
        for copy in fetch(step):
            copy.wait()
        at = [step * GROUP + i for i in range(GROUP)]
        owners = [table_ref[OWNER, b] for b in at]
        starts = [pl.multiple_of(b * rows, rows) for b in at]
        queries = [load_heads(q_ref, s, rows, head_dim) for s in starts]
        grads = [load_heads(ct_ref, s, rows, head_dim) for s in starts]
        scores = [
            dot_dims(kv_ref[o, :, :head_dim], q, 1, 1) * scale for o, q in zip(owners, queries)
        ]
        d_probs = [dot_dims(kv_ref[o, :, head_dim:], g, 1, 1) for o, g in zip(owners, grads)]
        token = lax.broadcasted_iota(jnp.int32, (tokens, 1), 0)
        scores = [
            jnp.where(token < table_ref[VALID, b], s, MASKED_SCORE) for b, s in zip(at, scores)
        ]
        weights = [jnp.exp(s - jnp.max(s, axis=0, keepdims=True)) for s in scores]
        probs = [w * (1.0 / jnp.sum(w, axis=0, keepdims=True)) for w in weights]
        halves = [p.astype(BF16) for p in probs]
        deltas = [jnp.sum(p * d, axis=0, keepdims=True) for p, d in zip(probs, d_probs)]
        d_scores = [
            (p * (d - x) * scale).astype(BF16) for p, d, x in zip(probs, d_probs, deltas)
        ]
        key_parts = [
            jnp.dot(d, q, preferred_element_type=F32) for d, q in zip(d_scores, queries)
        ]
        value_parts = [
            jnp.dot(p, g, preferred_element_type=F32) for p, g in zip(halves, grads)
        ]
        key_run, value_run = acc[:, :head_dim], acc[:, head_dim:]
        for i, b in enumerate(at):
            keep = table_ref[FIRST, b] == 0
            key_run = key_parts[i] + jnp.where(keep, key_run, 0.0)
            value_run = value_parts[i] + jnp.where(keep, value_run, 0.0)
            part_ref[owners[i], :, :head_dim] = key_run.astype(BF16)
            part_ref[owners[i], :, head_dim:] = value_run.astype(BF16)
            probs_ref[b] = halves[i]
            ds_ref[b] = d_scores[i]
        acc[:, :head_dim] = key_run
        acc[:, head_dim:] = value_run
        for copy in stash(step):
            copy.start()
        return carry

    lax.fori_loop(0, steps, some_blocks, 0)
    for step in range(steps):
        for copy in stash(step):
            copy.wait()


def hold(*arrays):
    return [pltpu.with_memory_space_constraint(x, pltpu.HBM) for x in arrays]


def attend(table, queries, cotangent, kv):
    blocks, (_, tokens, cols) = table.shape[1], kv.shape
    rows = queries.size * 2 // (blocks * cols)
    stash = pltpu.HBM((blocks, tokens, rows), BF16)
    return pl.pallas_call(
        attend_kernel,
        grid_spec=pltpu.PrefetchScalarGridSpec(
            num_scalar_prefetch=1,
            grid=(),
            in_specs=[in_hbm()] * 2 + [in_vmem()],
            out_specs=[in_vmem()] + [in_hbm()] * 2,
            scratch_shapes=[pltpu.VMEM(queries.shape, BF16)] * 2
            + [pltpu.VMEM(stash.shape, BF16)] * 2
            + [pltpu.VMEM(kv.shape[1:], F32)]
            + [pltpu.SemaphoreType.DMA((2, blocks // GROUP))] * 2,
        ),
        out_shape=[pltpu.HBM(kv.shape, BF16), stash, stash],
        compiler_params=limit(13),
        cost_estimate=cost(8 * queries.size * tokens, 8),
        name="attend",
    )(table, *hold(queries, cotangent), kv)


def apply_kernel(table_ref, kv_ref, probs_ref, ds_ref, out_ref, gq_ref):
    blocks = table_ref.shape[1]
    rows = out_ref.shape[0] // blocks
    head_dim = kv_ref.shape[2] // 2

    def some_blocks(step, carry):
        at = [step * GROUP + i for i in range(GROUP)]
        owners = [table_ref[OWNER, b] for b in at]
        outs = [
            dot_dims(probs_ref[b], kv_ref[o, :, head_dim:], 0, 0) for b, o in zip(at, owners)
        ]
        gqs = [dot_dims(ds_ref[b], kv_ref[o, :, :head_dim], 0, 0) for b, o in zip(at, owners)]
        for i, b in enumerate(at):
            start = pl.multiple_of(b * rows, rows)
            store_heads(out_ref, start, rows, head_dim, outs[i].astype(BF16))
            store_heads(gq_ref, start, rows, head_dim, gqs[i].astype(BF16))
        return carry

    lax.fori_loop(0, blocks // GROUP, some_blocks, 0)


def apply(table, kv, probs, d_scores, shape):
    out = pltpu.HBM(shape, BF16)
    return pl.pallas_call(
        apply_kernel,
        grid_spec=pltpu.PrefetchScalarGridSpec(
            num_scalar_prefetch=1,
            grid=(),
            in_specs=[in_vmem()] * 3,
            out_specs=[in_vmem()] * 2,
        ),
        out_shape=[out, out],
        compiler_params=limit(9),
        cost_estimate=cost(4 * shape[0] * shape[1] * kv.shape[1], 6),
        name="apply",
    )(table, *hold(kv, probs, d_scores))


def owner_kernel(table_ref, part_ref, raw_ref, gain_ref, grad_ref, by_core_ref, acc):
    head_dim = gain_ref.shape[1]
    tokens = part_ref.shape[1]
    acc[...] = jnp.zeros_like(acc)

    def add(d, carry):
        @pl.when(table_ref[POS, d] >= 0)
        def _():
            acc[table_ref[POS, d]] += part_ref[d].astype(F32)

        return carry

    lax.fori_loop(0, part_ref.shape[0], add, 0)
    gain = gain_ref[...]
    for i in range(acc.shape[0]):
        here = slice(i * tokens, (i + 1) * tokens)
        raw = raw_ref[here]
        scale = lax.rsqrt(jnp.mean(raw * raw, axis=-1, keepdims=True) + EPS)
        scaled = acc[i, :, :head_dim] * gain
        pull = jnp.mean(raw * scaled, axis=-1, keepdims=True)
        grad = scale * scaled - raw * (scale * scale * scale * pull)
        grad_ref[here, :head_dim] = grad.astype(BF16)
        grad_ref[here, head_dim:] = acc[i, :, head_dim:].astype(BF16)
    for i in range(acc.shape[0]):
        at = pl.multiple_of(lax.rem(table_ref[PLACE, 3] + i, 2) * tokens, tokens)
        by_core_ref[i * tokens : (i + 1) * tokens, :] = grad_ref[pl.ds(at, tokens), :]


def owner_grads(table, parts, raw, gain, images):
    tokens, cols = parts.shape[1:]
    grads = jax.ShapeDtypeStruct((images * tokens, cols), BF16)
    return pl.pallas_call(
        owner_kernel,
        grid_spec=pltpu.PrefetchScalarGridSpec(
            num_scalar_prefetch=1,
            grid=(),
            in_specs=[in_vmem()] * 3,
            out_specs=[in_vmem()] * 2,
            scratch_shapes=[pltpu.VMEM((images, tokens, cols), F32)],
        ),
        out_shape=[grads, grads],
        compiler_params=limit(6),
        cost_estimate=cost(0, 3),
        name="owner_grads",
    )(table, *hold(parts, raw), gain)


def transpose_kernel(*refs):
    pieces, out_ref = refs[:-1], refs[-1]
    tokens = pieces[0].shape[0]
    for i, ref in enumerate(pieces):
        out_ref[:, i * tokens : (i + 1) * tokens] = ref[...].T


def transpose_pieces(pieces):
    tokens, width = pieces[0].shape
    return pl.pallas_call(
        transpose_kernel,
        in_specs=[in_vmem()] * len(pieces),
        out_specs=in_vmem(),
        out_shape=jax.ShapeDtypeStruct((width, tokens * len(pieces)), BF16),
        compiler_params=limit(7),
        cost_estimate=cost(0, 4),
        name="transpose_pieces",
    )(*hold(*pieces))


def weight_kernel(own_ref, other_ref, *refs):
    lines, out_ref = refs[:-1], refs[-1]
    half = lines[0].shape[0] // 2
    first = jnp.concatenate([ref[:half, :] for ref in lines], axis=0)
    second = jnp.concatenate([ref[half:, :] for ref in lines], axis=0)
    block = out_ref.shape[1]
    for i in range(out_ref.shape[0]):
        here = slice(i * block, (i + 1) * block)
        total = jnp.dot(own_ref[here, :], first, preferred_element_type=F32)
        total = total + jnp.dot(other_ref[here, :], second, preferred_element_type=F32)
        out_ref[i] = total.astype(BF16)


def weight_terms(own_cols, other_cols, lines):
    width, cols = own_cols.shape[0], lines[0].shape[1]
    return pl.pallas_call(
        weight_kernel,
        in_specs=[in_vmem()] * (2 + len(lines)),
        out_specs=in_vmem(),
        out_shape=pltpu.HBM((NZ, width // NZ, cols), BF16),
        compiler_params=limit(9),
        cost_estimate=cost(4 * own_cols.size * cols, 6),
        name="weight_terms",
    )(own_cols, other_cols, *lines)


def assemble_kernel(table_ref, *refs, zones):
    w_refs, out_refs = refs[:-2], refs[-2:]
    for here, spot, _, _ in weight_blocks(table_ref, w_refs, zones):
        for out_ref, (ref, rows) in zip(out_refs, spot):
            out_ref[here, :] = ref[rows, :]


def assemble(table, pieces, zones, width, head_dim):
    return pl.pallas_call(
        functools.partial(assemble_kernel, zones=zones),
        grid_spec=pltpu.PrefetchScalarGridSpec(
            num_scalar_prefetch=1,
            grid=(),
            in_specs=[in_vmem()] * len(pieces),
            out_specs=[in_vmem()] * 2,
        ),
        out_shape=[pltpu.HBM((width, head_dim), BF16)] * 2,
        compiler_params=limit(10),
        cost_estimate=cost(0, 1),
        name="assemble",
    )(table, *pieces)


def feature_kernel(table_ref, own_ref, other_ref, *refs, targets):
    w_refs, out_refs, (lhs, held, sems) = refs[:4], refs[4:-3], refs[-3:]
    chips = len(out_refs)
    tokens, head_dim = own_ref.shape[0] // 2, own_ref.shape[1] // 2
    share = tokens // targets
    steps, block = held.shape[1:3]
    copies = [
        [
            pltpu.make_async_copy(
                w_ref.at[pl.ds(step * block, block), :], held.at[n, step], sems.at[n, step]
            )
            for n, w_ref in enumerate(w_refs)
        ]
        for step in range(steps)
    ]
    for step in range(steps):
        for copy in copies[step]:
            copy.start()
    for core, ref in enumerate((own_ref, other_ref)):
        for chip in range(chips):
            target = lax.rem(table_ref[PLACE, 2] + chip, chips) * 2 + table_ref[PLACE, 3]
            for i in range(2):
                at = pl.multiple_of(i * tokens + target * share, share)
                to = (chip * 2 + i) * share
                for n in range(2):
                    lhs[core, n, to : to + share, :] = ref[
                        pl.ds(at, share), n * head_dim : (n + 1) * head_dim
                    ]
    for step in range(steps):
        part = 0.0
        for core in range(2):
            for n in range(2):
                copies[step][2 * core + n].wait()
            left = jnp.concatenate([lhs[core, 0], lhs[core, 1]], axis=1)
            right = jnp.concatenate([held[2 * core, step], held[2 * core + 1, step]], axis=1)
            part = part + dot_dims(left, right, 1, 1)
        for chip, ref in enumerate(out_refs):
            ref[:, step * block : (step + 1) * block] = part[
                chip * 2 * share : (chip + 1) * 2 * share
            ].astype(BF16)


def feature_terms(table, own, other, weights, targets):
    width, head_dim = weights[0].shape
    chips, steps = targets // 2, 8
    rows = own.shape[0] // targets
    return pl.pallas_call(
        functools.partial(feature_kernel, targets=targets),
        grid_spec=pltpu.PrefetchScalarGridSpec(
            num_scalar_prefetch=1,
            grid=(),
            in_specs=[in_vmem()] * 2 + [in_hbm()] * 4,
            out_specs=[in_vmem()] * chips,
            scratch_shapes=[
                pltpu.VMEM((2, 2, own.shape[0] // 2, head_dim), BF16),
                pltpu.VMEM((4, steps, width // steps, head_dim), BF16),
                pltpu.SemaphoreType.DMA((4, steps)),
            ],
        ),
        out_shape=[jax.ShapeDtypeStruct((rows, width), BF16)] * chips,
        compiler_params=limit(14),
        cost_estimate=cost(4 * own.size * width, 10),
        name="feature_terms",
    )(table, own, other, *hold(*weights))


def shift_y(x, by):
    if by == 0:
        return x
    pairs = [(y * NZ + z, (y + by) % NY * NZ + z) for y in range(NY) for z in range(NZ)]
    return lax.ppermute(x, "dp", pairs)


def shift_z(x, by):
    pairs = [(y * NZ + z, y * NZ + (z + by) % NZ) for y in range(NY) for z in range(NZ)]
    return lax.ppermute(x, "dp", pairs)


def swap_cores(x, count):
    return lax.ppermute(x, "tensor", [(t, t ^ 1) for t in range(count)])


def local(
    queries, features, k_weight, v_weight, k_gain, block_image, image_slot, image_tiles, cotangent
):
    dp_count = lax.axis_size("dp")
    tensor_count = lax.axis_size("tensor")
    me = lax.axis_index("dp")
    images, tokens, width = features.shape
    head_dim = k_gain.shape[0]
    rows = features.reshape(images * tokens, width)
    gain = k_gain.reshape(1, head_dim)
    my_y, my_z = me // NZ, lax.rem(me, NZ)
    tensor = lax.axis_index("tensor")
    core = lax.rem(tensor, 2)

    image_ids = lax.broadcasted_iota(jnp.int32, (1, image_slot.shape[0]), 1)
    id_match = block_image[:, None] == image_ids
    slots = jnp.sum(jnp.where(id_match, image_slot[None, :], 0), axis=1).reshape(dp_count, -1)
    tiles = jnp.sum(jnp.where(id_match, image_tiles[None, :], 0), axis=1).reshape(dp_count, -1)
    my_slots = lax.dynamic_index_in_dim(slots, me, 0, keepdims=False)
    my_tiles = lax.dynamic_index_in_dim(tiles, me, 0, keepdims=False)
    first = jnp.concatenate(
        [jnp.ones((1,), jnp.int32), (my_slots[1:] != my_slots[:-1]).astype(jnp.int32)]
    )
    pos = jnp.max(jnp.where(slots // images == me, slots % images, -1), axis=1)
    place = jnp.stack([my_y, my_z, tensor // 2, core])
    place = jnp.pad(place, (0, pos.shape[0] - place.shape[0]))
    table = jnp.stack([pos, my_slots // images, my_tiles * (tokens // TILES), first, place])

    v_line = jnp.concatenate([shift_y(v_weight, (NY - i) % NY) for i in range(NY)])
    k_ring, v_ring = [k_weight], [v_line]
    for hop in range(1, NZ // 2):
        k_ring += [shift_z(k_ring[max(-2, -len(k_ring))], 1), shift_z(k_ring[-1], -1)]
        if hop == 1:
            v_ring += [shift_z(v_line, 1), shift_z(v_line, -1)]
        if hop == 2:
            k_ring[-2], k_ring[-1], v_ring[-2], v_ring[-1] = lax.optimization_barrier(
                (k_ring[-2], k_ring[-1], v_ring[-2], v_ring[-1])
            )
    for hop in range(2, NZ // 2):
        v_ring += [shift_z(v_ring[-2], 1), shift_z(v_ring[-1], -1)]
    k_ring += [shift_z(k_ring[-2], 1)]
    v_ring += [shift_z(v_ring[-2], 1)]
    offsets = [0] + [z for hop in range(1, NZ // 2) for z in (NZ - hop, hop)] + [NZ // 2]
    v_zones = [[(y, z) for y in range(NY)] for z in offsets]
    k_pieces, k_zones = [], []
    for part in (slice(0, NZ // 2), slice(NZ // 2, NZ)):
        k_line = jnp.concatenate(k_ring[part])
        after, before = shift_y(k_line, -1), shift_y(k_line, 1)
        far = shift_y(before, 1) if part.start else shift_y(after, -1)
        k_pieces += [k_line, after, before, far]
        k_zones += [[(y, z) for z in offsets[part]] for y in (0, 1, NY - 1, NY // 2)]
    pieces, zones = k_pieces + v_ring, k_zones + v_zones

    send, raw = project(
        table, rows, pieces, zones, gain, dp_count, images, tokens
    )
    kv = lax.all_to_all(send, "dp", 0, 0, tiled=True)

    rows_later, _ = lax.optimization_barrier((features, raw))
    span = width // NY
    col_pieces = [
        shift_y(
            lax.dynamic_slice(
                rows_later, (core, 0, (my_y + s) % NY * span), (1, tokens, span)
            )[0],
            s,
        )
        for s in range(NY)
    ]

    parts, probs, d_scores = attend(table, queries, cotangent, kv)
    parts, col_pieces, pieces = lax.optimization_barrier((parts, col_pieces, pieces))
    parts = lax.all_to_all(parts, "dp", 0, 0, tiled=True)
    own_cols = transpose_pieces(col_pieces)
    other_cols = swap_cores(own_cols, tensor_count)
    weights = list(assemble(table, pieces, zones, width, head_dim))
    weights += [swap_cores(w, tensor_count) for w in weights]
    attended, grad_queries = apply(table, kv, probs, d_scores, queries.shape)
    parts, other_cols, attended, grad_queries, weights = lax.optimization_barrier(
        (parts, other_cols, attended, grad_queries, weights)
    )
    grads, by_core = owner_grads(table, parts, raw, gain, images)

    lines = [shift_y(by_core, s) for s in range(NY)]
    shares = weight_terms(own_cols, other_cols, lines)
    other_grads = swap_cores(grads, tensor_count)
    shares, grads, other_grads = lax.optimization_barrier((shares, grads, other_grads))
    shares = lax.all_to_all(shares, "dp", 0, 0, tiled=True, axis_index_groups=Z_GROUPS)

    terms = list(feature_terms(table, grads, other_grads, weights, tensor_count))
    for s in (2, 1, 3):
        pairs = [(t, (t + 2 * s) % tensor_count) for t in range(tensor_count)]
        terms[s] = lax.ppermute(terms[s], "tensor", pairs)
    shares, terms = lax.optimization_barrier((shares, terms))
    grad_features = sum(term.astype(F32) for term in terms).astype(BF16)
    grad_features = grad_features.reshape(images, tokens // tensor_count, width)
    weight_grads = jnp.sum(shares.astype(F32), axis=0)
    return (
        attended,
        grad_queries,
        grad_features,
        weight_grads[:, :head_dim],
        weight_grads[:, head_dim:],
    )


def solution(mesh):
    in_specs = (
        P("dp", "tensor"),
        P("dp", None, None),
        P("dp", "tensor"),
        P("dp", "tensor"),
        P(),
        P(),
        P(),
        P(),
        P("dp", "tensor"),
    )
    out_specs = (
        P("dp", "tensor"),
        P("dp", "tensor"),
        P("dp", "tensor", None),
        P("dp", "tensor"),
        P("dp", "tensor"),
    )
    return jax.shard_map(local, mesh=mesh, in_specs=in_specs, out_specs=out_specs, check_vma=False)
```

```python
import functools

import jax
import jax.numpy as jnp
from jax import lax
from jax.experimental import pallas as pl
from jax.experimental.pallas import tpu as pltpu
from jax.sharding import PartitionSpec as P

TILES = 4
EPS = 1e-05
MASKED_SCORE = -1e30
NY, NZ = 4, 8
Y_GROUPS = [[y * NZ + z for y in range(NY)] for z in range(NZ)]
Z_GROUPS = [[y * NZ + z for z in range(NZ)] for y in range(NY)]
BF16, F32 = jnp.bfloat16, jnp.float32
MIB = 1024 * 1024
GROUP = 4
POS, OWNER, VALID, FIRST, PLACE = range(5)


def dot_dims(a, b, a_dim, b_dim):
    return lax.dot_general(
        a, b, (((a_dim,), (b_dim,)), ((), ())), preferred_element_type=F32
    )


def limit(mib):
    return pltpu.CompilerParams(vmem_limit_bytes=mib * MIB)


def cost(flops, mib):
    return pl.CostEstimate(flops=flops, bytes_accessed=mib * MIB, transcendentals=0)


def in_hbm():
    return pl.BlockSpec(memory_space=pltpu.HBM)


def in_vmem():
    return pl.BlockSpec(memory_space=pltpu.VMEM)


def in_hbm():
    return pl.BlockSpec(memory_space=pltpu.HBM)


def weight_blocks(table_ref, w_refs, zones):
    spots = {}
    for n, blocks in enumerate(zones):
        for i, at in enumerate(blocks):
            size = w_refs[n].shape[0] // len(blocks)
            spots.setdefault(at, []).append((w_refs[n], slice(i * size, (i + 1) * size)))
    found = []
    for (y_off, z_off), spot in spots.items():
        y = lax.rem(table_ref[PLACE, 0] + y_off, NY)
        z = lax.rem(table_ref[PLACE, 1] + z_off, NZ)
        size = spot[0][1].stop - spot[0][1].start
        found.append((pl.ds(pl.multiple_of((y * NZ + z) * size, size), size), spot, y_off, z))
    return found


def side_by_side(spot):
    return jnp.concatenate([ref[rows, :] for ref, rows in spot], axis=1)


def project_kernel(table_ref, f_ref, *refs, zones):
    w_refs, (gain_ref, send_ref, raw_ref, kv) = refs[: len(zones)], refs[len(zones) :]
    head_dim = gain_ref.shape[1]
    tokens = send_ref.shape[1]
    total = jnp.zeros((f_ref.shape[0], 2 * head_dim), F32)
    for cols, spot, _, _ in weight_blocks(table_ref, w_refs, zones):
        total = total + jnp.dot(f_ref[:, cols], side_by_side(spot), preferred_element_type=F32)
    raw = total[:, :head_dim]
    raw_ref[...] = raw
    scale = lax.rsqrt(jnp.mean(raw * raw, axis=-1, keepdims=True) + EPS)
    keys = (raw * scale * gain_ref[...]).astype(BF16)
    values = total[:, head_dim:].astype(BF16)
    for i in range(kv.shape[0]):
        kv[i, :, :head_dim] = keys[i * tokens : (i + 1) * tokens]
        kv[i, :, head_dim:] = values[i * tokens : (i + 1) * tokens]

    def put(d, carry):
        send_ref[d] = kv[jnp.maximum(table_ref[POS, d], 0)]
        return carry

    lax.fori_loop(0, send_ref.shape[0], put, 0, unroll=4)


def project(table, rows, pieces, zones, gain, dp, images, tokens):
    cols = 2 * gain.shape[1]
    return pl.pallas_call(
        functools.partial(project_kernel, zones=zones),
        grid_spec=pltpu.PrefetchScalarGridSpec(
            num_scalar_prefetch=1,
            grid=(),
            in_specs=[in_vmem()] * (2 + len(pieces)),
            out_specs=[in_vmem()] * 2,
            scratch_shapes=[pltpu.VMEM((images, tokens, cols), BF16)],
        ),
        out_shape=[
            pltpu.HBM((dp, tokens, cols), BF16),
            pltpu.HBM((rows.shape[0], cols // 2), F32),
        ],
        compiler_params=limit(14),
        cost_estimate=cost(2 * rows.size * cols, 10),
        name="project",
    )(table, *hold(rows), *pieces, gain)


def load_heads(ref, start, rows, head_dim):
    heads = ref.shape[1] // head_dim
    return jnp.concatenate(
        [ref[pl.ds(start, rows), g * head_dim : (g + 1) * head_dim] for g in range(heads)],
        axis=0,
    )


def store_heads(ref, start, rows, head_dim, full):
    for g in range(ref.shape[1] // head_dim):
        ref[pl.ds(start, rows), g * head_dim : (g + 1) * head_dim] = full[
            g * rows : (g + 1) * rows
        ]


def attend_kernel(table_ref, q_hbm, ct_hbm, kv_ref, part_ref, probs_hbm, ds_hbm, *scratch):
    q_ref, ct_ref, probs_ref, ds_ref, acc, in_sems, out_sems = scratch
    blocks = table_ref.shape[1]
    steps = blocks // GROUP
    text = q_ref.shape[0] // steps

    def moves(step, pairs, size, sems):
        here = pl.ds(pl.multiple_of(step * size, size), size)
        return [
            pltpu.make_async_copy(a.at[here], b.at[here], sems.at[n, step])
            for n, (a, b) in enumerate(pairs)
        ]

    def fetch(step):
        return moves(step, ((q_hbm, q_ref), (ct_hbm, ct_ref)), text, in_sems)

    def stash(step):
        return moves(step, ((probs_ref, probs_hbm), (ds_ref, ds_hbm)), GROUP, out_sems)

    for step in range(steps):
        for copy in fetch(step):
            copy.start()
    rows = q_ref.shape[0] // blocks
    head_dim = kv_ref.shape[2] // 2
    tokens = kv_ref.shape[1]
    scale = head_dim**-0.5
    part_ref[...] = jnp.zeros_like(part_ref)
    acc[...] = jnp.zeros_like(acc)

    def some_blocks(step, carry):
        for copy in fetch(step):
            copy.wait()
        at = [step * GROUP + i for i in range(GROUP)]
        owners = [table_ref[OWNER, b] for b in at]
        starts = [pl.multiple_of(b * rows, rows) for b in at]
        queries = [load_heads(q_ref, s, rows, head_dim) for s in starts]
        grads = [load_heads(ct_ref, s, rows, head_dim) for s in starts]
        scores = [
            dot_dims(kv_ref[o, :, :head_dim], q, 1, 1) * scale for o, q in zip(owners, queries)
        ]
        d_probs = [dot_dims(kv_ref[o, :, head_dim:], g, 1, 1) for o, g in zip(owners, grads)]
        token = lax.broadcasted_iota(jnp.int32, (tokens, 1), 0)
        scores = [
            jnp.where(token < table_ref[VALID, b], s, MASKED_SCORE) for b, s in zip(at, scores)
        ]
        weights = [jnp.exp(s - jnp.max(s, axis=0, keepdims=True)) for s in scores]
        probs = [w * (1.0 / jnp.sum(w, axis=0, keepdims=True)) for w in weights]
        halves = [p.astype(BF16) for p in probs]
        deltas = [jnp.sum(p * d, axis=0, keepdims=True) for p, d in zip(probs, d_probs)]
        d_scores = [
            (p * (d - x) * scale).astype(BF16) for p, d, x in zip(probs, d_probs, deltas)
        ]
        key_parts = [
            jnp.dot(d, q, preferred_element_type=F32) for d, q in zip(d_scores, queries)
        ]
        value_parts = [
            jnp.dot(p, g, preferred_element_type=F32) for p, g in zip(halves, grads)
        ]
        key_run, value_run = acc[:, :head_dim], acc[:, head_dim:]
        for i, b in enumerate(at):
            keep = table_ref[FIRST, b] == 0
            key_run = key_parts[i] + jnp.where(keep, key_run, 0.0)
            value_run = value_parts[i] + jnp.where(keep, value_run, 0.0)
            part_ref[owners[i], :, :head_dim] = key_run.astype(BF16)
            part_ref[owners[i], :, head_dim:] = value_run.astype(BF16)
            probs_ref[b] = halves[i]
            ds_ref[b] = d_scores[i]
        acc[:, :head_dim] = key_run
        acc[:, head_dim:] = value_run
        for copy in stash(step):
            copy.start()
        return carry

    lax.fori_loop(0, steps, some_blocks, 0)
    for step in range(steps):
        for copy in stash(step):
            copy.wait()


def hold(*arrays):
    return [pltpu.with_memory_space_constraint(x, pltpu.HBM) for x in arrays]


def attend(table, queries, cotangent, kv):
    blocks, (_, tokens, cols) = table.shape[1], kv.shape
    rows = queries.size * 2 // (blocks * cols)
    stash = pltpu.HBM((blocks, tokens, rows), BF16)
    return pl.pallas_call(
        attend_kernel,
        grid_spec=pltpu.PrefetchScalarGridSpec(
            num_scalar_prefetch=1,
            grid=(),
            in_specs=[in_hbm()] * 2 + [in_vmem()],
            out_specs=[in_vmem()] + [in_hbm()] * 2,
            scratch_shapes=[pltpu.VMEM(queries.shape, BF16)] * 2
            + [pltpu.VMEM(stash.shape, BF16)] * 2
            + [pltpu.VMEM(kv.shape[1:], F32)]
            + [pltpu.SemaphoreType.DMA((2, blocks // GROUP))] * 2,
        ),
        out_shape=[pltpu.HBM(kv.shape, BF16), stash, stash],
        compiler_params=limit(13),
        cost_estimate=cost(8 * queries.size * tokens, 8),
        name="attend",
    )(table, *hold(queries, cotangent), kv)


def apply_kernel(table_ref, kv_ref, probs_ref, ds_ref, out_ref, gq_ref):
    blocks = table_ref.shape[1]
    rows = out_ref.shape[0] // blocks
    head_dim = kv_ref.shape[2] // 2

    def some_blocks(step, carry):
        at = [step * GROUP + i for i in range(GROUP)]
        owners = [table_ref[OWNER, b] for b in at]
        outs = [
            dot_dims(probs_ref[b], kv_ref[o, :, head_dim:], 0, 0) for b, o in zip(at, owners)
        ]
        gqs = [dot_dims(ds_ref[b], kv_ref[o, :, :head_dim], 0, 0) for b, o in zip(at, owners)]
        for i, b in enumerate(at):
            start = pl.multiple_of(b * rows, rows)
            store_heads(out_ref, start, rows, head_dim, outs[i].astype(BF16))
            store_heads(gq_ref, start, rows, head_dim, gqs[i].astype(BF16))
        return carry

    lax.fori_loop(0, blocks // GROUP, some_blocks, 0)


def apply(table, kv, probs, d_scores, shape):
    out = pltpu.HBM(shape, BF16)
    return pl.pallas_call(
        apply_kernel,
        grid_spec=pltpu.PrefetchScalarGridSpec(
            num_scalar_prefetch=1,
            grid=(),
            in_specs=[in_vmem()] * 3,
            out_specs=[in_vmem()] * 2,
        ),
        out_shape=[out, out],
        compiler_params=limit(9),
        cost_estimate=cost(4 * shape[0] * shape[1] * kv.shape[1], 6),
        name="apply",
    )(table, *hold(kv, probs, d_scores))


def owner_kernel(table_ref, part_ref, raw_ref, gain_ref, grad_ref, by_core_ref, acc):
    head_dim = gain_ref.shape[1]
    tokens = part_ref.shape[1]
    acc[...] = jnp.zeros_like(acc)

    def add(d, carry):
        @pl.when(table_ref[POS, d] >= 0)
        def _():
            acc[table_ref[POS, d]] += part_ref[d].astype(F32)

        return carry

    lax.fori_loop(0, part_ref.shape[0], add, 0)
    gain = gain_ref[...]
    for i in range(acc.shape[0]):
        here = slice(i * tokens, (i + 1) * tokens)
        raw = raw_ref[here]
        scale = lax.rsqrt(jnp.mean(raw * raw, axis=-1, keepdims=True) + EPS)
        scaled = acc[i, :, :head_dim] * gain
        pull = jnp.mean(raw * scaled, axis=-1, keepdims=True)
        grad = scale * scaled - raw * (scale * scale * scale * pull)
        grad_ref[here, :head_dim] = grad.astype(BF16)
        grad_ref[here, head_dim:] = acc[i, :, head_dim:].astype(BF16)
    for i in range(acc.shape[0]):
        at = pl.multiple_of(lax.rem(table_ref[PLACE, 3] + i, 2) * tokens, tokens)
        by_core_ref[i * tokens : (i + 1) * tokens, :] = grad_ref[pl.ds(at, tokens), :]


def owner_grads(table, parts, raw, gain, images):
    tokens, cols = parts.shape[1:]
    grads = jax.ShapeDtypeStruct((images * tokens, cols), BF16)
    return pl.pallas_call(
        owner_kernel,
        grid_spec=pltpu.PrefetchScalarGridSpec(
            num_scalar_prefetch=1,
            grid=(),
            in_specs=[in_vmem()] * 3,
            out_specs=[in_vmem()] * 2,
            scratch_shapes=[pltpu.VMEM((images, tokens, cols), F32)],
        ),
        out_shape=[grads, grads],
        compiler_params=limit(6),
        cost_estimate=cost(0, 3),
        name="owner_grads",
    )(table, *hold(parts, raw), gain)


def transpose_kernel(*refs):
    pieces, out_ref = refs[:-1], refs[-1]
    tokens = pieces[0].shape[0]
    for i, ref in enumerate(pieces):
        out_ref[:, i * tokens : (i + 1) * tokens] = ref[...].T


def transpose_pieces(pieces):
    tokens, width = pieces[0].shape
    return pl.pallas_call(
        transpose_kernel,
        in_specs=[in_vmem()] * len(pieces),
        out_specs=in_vmem(),
        out_shape=jax.ShapeDtypeStruct((width, tokens * len(pieces)), BF16),
        compiler_params=limit(7),
        cost_estimate=cost(0, 4),
        name="transpose_pieces",
    )(*hold(*pieces))


def weight_kernel(own_ref, other_ref, *refs):
    lines, out_ref = refs[:-1], refs[-1]
    half = lines[0].shape[0] // 2
    first = jnp.concatenate([ref[:half, :] for ref in lines], axis=0)
    second = jnp.concatenate([ref[half:, :] for ref in lines], axis=0)
    block = out_ref.shape[1]
    for i in range(out_ref.shape[0]):
        here = slice(i * block, (i + 1) * block)
        total = jnp.dot(own_ref[here, :], first, preferred_element_type=F32)
        total = total + jnp.dot(other_ref[here, :], second, preferred_element_type=F32)
        out_ref[i] = total.astype(BF16)


def weight_terms(own_cols, other_cols, lines):
    width, cols = own_cols.shape[0], lines[0].shape[1]
    return pl.pallas_call(
        weight_kernel,
        in_specs=[in_vmem()] * (2 + len(lines)),
        out_specs=in_vmem(),
        out_shape=pltpu.HBM((NZ, width // NZ, cols), BF16),
        compiler_params=limit(9),
        cost_estimate=cost(4 * own_cols.size * cols, 6),
        name="weight_terms",
    )(own_cols, other_cols, *lines)


def assemble_kernel(table_ref, *refs, zones):
    w_refs, out_refs = refs[:-2], refs[-2:]
    for here, spot, _, _ in weight_blocks(table_ref, w_refs, zones):
        for out_ref, (ref, rows) in zip(out_refs, spot):
            out_ref[here, :] = ref[rows, :]


def assemble(table, pieces, zones, width, head_dim):
    return pl.pallas_call(
        functools.partial(assemble_kernel, zones=zones),
        grid_spec=pltpu.PrefetchScalarGridSpec(
            num_scalar_prefetch=1,
            grid=(),
            in_specs=[in_vmem()] * len(pieces),
            out_specs=[in_vmem()] * 2,
        ),
        out_shape=[pltpu.HBM((width, head_dim), BF16)] * 2,
        compiler_params=limit(10),
        cost_estimate=cost(0, 1),
        name="assemble",
    )(table, *pieces)


def feature_kernel(table_ref, own_ref, other_ref, *refs, targets):
    w_refs, out_refs, (lhs, held, sems) = refs[:4], refs[4:-3], refs[-3:]
    chips = len(out_refs)
    tokens, head_dim = own_ref.shape[0] // 2, own_ref.shape[1] // 2
    share = tokens // targets
    steps, block = held.shape[1:3]
    copies = [
        [
            pltpu.make_async_copy(
                w_ref.at[pl.ds(step * block, block), :], held.at[n, step], sems.at[n, step]
            )
            for n, w_ref in enumerate(w_refs)
        ]
        for step in range(steps)
    ]
    for step in range(steps):
        for copy in copies[step]:
            copy.start()
    for core, ref in enumerate((own_ref, other_ref)):
        for chip in range(chips):
            target = lax.rem(table_ref[PLACE, 2] + chip, chips) * 2 + table_ref[PLACE, 3]
            for i in range(2):
                at = pl.multiple_of(i * tokens + target * share, share)
                to = (chip * 2 + i) * share
                for n in range(2):
                    lhs[core, n, to : to + share, :] = ref[
                        pl.ds(at, share), n * head_dim : (n + 1) * head_dim
                    ]
    for step in range(steps):
        part = 0.0
        for core in range(2):
            for n in range(2):
                copies[step][2 * core + n].wait()
            left = jnp.concatenate([lhs[core, 0], lhs[core, 1]], axis=1)
            right = jnp.concatenate([held[2 * core, step], held[2 * core + 1, step]], axis=1)
            part = part + dot_dims(left, right, 1, 1)
        for chip, ref in enumerate(out_refs):
            ref[:, step * block : (step + 1) * block] = part[
                chip * 2 * share : (chip + 1) * 2 * share
            ].astype(BF16)


def feature_terms(table, own, other, weights, targets):
    width, head_dim = weights[0].shape
    chips, steps = targets // 2, 8
    rows = own.shape[0] // targets
    return pl.pallas_call(
        functools.partial(feature_kernel, targets=targets),
        grid_spec=pltpu.PrefetchScalarGridSpec(
            num_scalar_prefetch=1,
            grid=(),
            in_specs=[in_vmem()] * 2 + [in_hbm()] * 4,
            out_specs=[in_vmem()] * chips,
            scratch_shapes=[
                pltpu.VMEM((2, 2, own.shape[0] // 2, head_dim), BF16),
                pltpu.VMEM((4, steps, width // steps, head_dim), BF16),
                pltpu.SemaphoreType.DMA((4, steps)),
            ],
        ),
        out_shape=[jax.ShapeDtypeStruct((rows, width), BF16)] * chips,
        compiler_params=limit(14),
        cost_estimate=cost(4 * own.size * width, 10),
        name="feature_terms",
    )(table, own, other, *hold(*weights))


def finish_kernel(share_ref, *refs):
    terms, (features_ref, key_ref, value_ref) = refs[:-3], refs[-3:]
    head_dim = key_ref.shape[1]
    total = share_ref[0].astype(F32)
    for i in range(1, share_ref.shape[0]):
        total = total + share_ref[i].astype(F32)
    key_ref[...] = total[:, :head_dim]
    value_ref[...] = total[:, head_dim:]
    block = features_ref.shape[1] // NZ
    for i in range(NZ):
        here = slice(i * block, (i + 1) * block)
        total = terms[0][:, here].astype(F32)
        for term in terms[1:]:
            total = total + term[:, here].astype(F32)
        features_ref[:, here] = total.astype(BF16)


def finish(shares, terms):
    rows, cols = shares.shape[1:]
    weights = pltpu.HBM((rows, cols // 2), F32)
    return pl.pallas_call(
        finish_kernel,
        in_specs=[in_vmem()] * (1 + len(terms)),
        out_specs=[in_vmem()] * 3,
        out_shape=[pltpu.HBM(terms[0].shape, BF16), weights, weights],
        compiler_params=limit(6),
        cost_estimate=cost(0, 3),
        name="finish",
    )(shares, *terms)


def shift_y(x, by):
    if by == 0:
        return x
    pairs = [(y * NZ + z, (y + by) % NY * NZ + z) for y in range(NY) for z in range(NZ)]
    return lax.ppermute(x, "dp", pairs)


def shift_z(x, by):
    pairs = [(y * NZ + z, y * NZ + (z + by) % NZ) for y in range(NY) for z in range(NZ)]
    return lax.ppermute(x, "dp", pairs)


def swap_cores(x, count):
    return lax.ppermute(x, "tensor", [(t, t ^ 1) for t in range(count)])


def local(
    queries, features, k_weight, v_weight, k_gain, block_image, image_slot, image_tiles, cotangent
):
    dp_count = lax.axis_size("dp")
    tensor_count = lax.axis_size("tensor")
    me = lax.axis_index("dp")
    images, tokens, width = features.shape
    head_dim = k_gain.shape[0]
    rows = features.reshape(images * tokens, width)
    gain = k_gain.reshape(1, head_dim)
    my_y, my_z = me // NZ, lax.rem(me, NZ)
    tensor = lax.axis_index("tensor")
    core = lax.rem(tensor, 2)

    image_ids = lax.broadcasted_iota(jnp.int32, (1, image_slot.shape[0]), 1)
    id_match = block_image[:, None] == image_ids
    slots = jnp.sum(jnp.where(id_match, image_slot[None, :], 0), axis=1).reshape(dp_count, -1)
    tiles = jnp.sum(jnp.where(id_match, image_tiles[None, :], 0), axis=1).reshape(dp_count, -1)
    my_slots = lax.dynamic_index_in_dim(slots, me, 0, keepdims=False)
    my_tiles = lax.dynamic_index_in_dim(tiles, me, 0, keepdims=False)
    first = jnp.concatenate(
        [jnp.ones((1,), jnp.int32), (my_slots[1:] != my_slots[:-1]).astype(jnp.int32)]
    )
    pos = jnp.max(jnp.where(slots // images == me, slots % images, -1), axis=1)
    place = jnp.stack([my_y, my_z, tensor // 2, core])
    place = jnp.pad(place, (0, pos.shape[0] - place.shape[0]))
    table = jnp.stack([pos, my_slots // images, my_tiles * (tokens // TILES), first, place])

    v_line = jnp.concatenate([shift_y(v_weight, (NY - i) % NY) for i in range(NY)])
    k_ring, v_ring = [k_weight], [v_line]
    for hop in range(1, NZ // 2):
        k_ring += [shift_z(k_ring[max(-2, -len(k_ring))], 1), shift_z(k_ring[-1], -1)]
        if hop == 1:
            v_ring += [shift_z(v_line, 1), shift_z(v_line, -1)]
        if hop == 2:
            k_ring[-2], k_ring[-1], v_ring[-2], v_ring[-1] = lax.optimization_barrier(
                (k_ring[-2], k_ring[-1], v_ring[-2], v_ring[-1])
            )
    for hop in range(2, NZ // 2):
        v_ring += [shift_z(v_ring[-2], 1), shift_z(v_ring[-1], -1)]
    k_ring += [shift_z(k_ring[-2], 1)]
    v_ring += [shift_z(v_ring[-2], 1)]
    offsets = [0] + [z for hop in range(1, NZ // 2) for z in (NZ - hop, hop)] + [NZ // 2]
    v_zones = [[(y, z) for y in range(NY)] for z in offsets]
    k_pieces, k_zones = [], []
    for part in (slice(0, NZ // 2), slice(NZ // 2, NZ)):
        k_line = jnp.concatenate(k_ring[part])
        after, before = shift_y(k_line, -1), shift_y(k_line, 1)
        far = shift_y(before, 1) if part.start else shift_y(after, -1)
        k_pieces += [k_line, after, before, far]
        k_zones += [[(y, z) for z in offsets[part]] for y in (0, 1, NY - 1, NY // 2)]
    pieces, zones = k_pieces + v_ring, k_zones + v_zones

    send, raw = project(
        table, rows, pieces, zones, gain, dp_count, images, tokens
    )
    kv = lax.all_to_all(send, "dp", 0, 0, tiled=True)

    rows_later, _ = lax.optimization_barrier((features, raw))
    span = width // NY
    col_pieces = [
        shift_y(
            lax.dynamic_slice(
                rows_later, (core, 0, (my_y + s) % NY * span), (1, tokens, span)
            )[0],
            s,
        )
        for s in range(NY)
    ]

    parts, probs, d_scores = attend(table, queries, cotangent, kv)
    parts, col_pieces, pieces = lax.optimization_barrier((parts, col_pieces, pieces))
    parts = lax.all_to_all(parts, "dp", 0, 0, tiled=True)
    own_cols = transpose_pieces(col_pieces)
    other_cols = swap_cores(own_cols, tensor_count)
    weights = list(assemble(table, pieces, zones, width, head_dim))
    weights += [swap_cores(w, tensor_count) for w in weights]
    attended, grad_queries = apply(table, kv, probs, d_scores, queries.shape)
    parts, other_cols, attended, grad_queries, weights = lax.optimization_barrier(
        (parts, other_cols, attended, grad_queries, weights)
    )
    grads, by_core = owner_grads(table, parts, raw, gain, images)

    lines = [shift_y(by_core, s) for s in range(NY)]
    shares = weight_terms(own_cols, other_cols, lines)
    other_grads = swap_cores(grads, tensor_count)
    shares, grads, other_grads = lax.optimization_barrier((shares, grads, other_grads))
    shares = lax.all_to_all(shares, "dp", 0, 0, tiled=True, axis_index_groups=Z_GROUPS)

    terms = list(feature_terms(table, grads, other_grads, weights, tensor_count))
    for s in range(1, tensor_count // 2):
        pairs = [(t, (t + 2 * s) % tensor_count) for t in range(tensor_count)]
        terms[s] = lax.ppermute(terms[s], "tensor", pairs)
    grad_features, grad_k, grad_v = finish(shares, terms)
    grad_features = grad_features.reshape(images, tokens // tensor_count, width)
    return attended, grad_queries, grad_features, grad_k, grad_v


def solution(mesh):
    in_specs = (
        P("dp", "tensor"),
        P("dp", None, None),
        P("dp", "tensor"),
        P("dp", "tensor"),
        P(),
        P(),
        P(),
        P(),
        P("dp", "tensor"),
    )
    out_specs = (
        P("dp", "tensor"),
        P("dp", "tensor"),
        P("dp", "tensor", None),
        P("dp", "tensor"),
        P("dp", "tensor"),
    )
    return jax.shard_map(local, mesh=mesh, in_specs=in_specs, out_specs=out_specs, check_vma=False)
```

```python
import functools

import jax
import jax.numpy as jnp
from jax import lax
from jax.experimental import pallas as pl
from jax.experimental.pallas import tpu as pltpu
from jax.sharding import PartitionSpec as P

TILES = 4
EPS = 1e-05
MASKED_SCORE = -1e30
NY, NZ = 4, 8
Y_GROUPS = [[y * NZ + z for y in range(NY)] for z in range(NZ)]
Z_GROUPS = [[y * NZ + z for z in range(NZ)] for y in range(NY)]
BF16, F32 = jnp.bfloat16, jnp.float32
MIB = 1024 * 1024
GROUP = 4
POS, OWNER, VALID, FIRST, PLACE = range(5)


def dot_dims(a, b, a_dim, b_dim):
    return lax.dot_general(
        a, b, (((a_dim,), (b_dim,)), ((), ())), preferred_element_type=F32
    )


def limit(mib):
    return pltpu.CompilerParams(vmem_limit_bytes=mib * MIB)


def cost(flops, mib):
    return pl.CostEstimate(flops=flops, bytes_accessed=mib * MIB, transcendentals=0)


def in_hbm():
    return pl.BlockSpec(memory_space=pltpu.HBM)


def in_vmem():
    return pl.BlockSpec(memory_space=pltpu.VMEM)


def in_hbm():
    return pl.BlockSpec(memory_space=pltpu.HBM)


def weight_blocks(table_ref, w_refs, zones):
    spots = {}
    for n, blocks in enumerate(zones):
        for i, at in enumerate(blocks):
            size = w_refs[n].shape[0] // len(blocks)
            spots.setdefault(at, []).append((w_refs[n], slice(i * size, (i + 1) * size)))
    found = []
    for (y_off, z_off), spot in spots.items():
        y = lax.rem(table_ref[PLACE, 0] + y_off, NY)
        z = lax.rem(table_ref[PLACE, 1] + z_off, NZ)
        size = spot[0][1].stop - spot[0][1].start
        found.append((pl.ds(pl.multiple_of((y * NZ + z) * size, size), size), spot, y_off, z))
    return found


def side_by_side(spot):
    return jnp.concatenate([ref[rows, :] for ref, rows in spot], axis=1)


def project_kernel(table_ref, f_ref, *refs, zones):
    w_refs, (gain_ref, send_ref, raw_ref, kv) = refs[: len(zones)], refs[len(zones) :]
    head_dim = gain_ref.shape[1]
    tokens = send_ref.shape[1]
    total = jnp.zeros((f_ref.shape[0], 2 * head_dim), F32)
    for cols, spot, _, _ in weight_blocks(table_ref, w_refs, zones):
        total = total + jnp.dot(f_ref[:, cols], side_by_side(spot), preferred_element_type=F32)
    raw = total[:, :head_dim]
    raw_ref[...] = raw
    scale = lax.rsqrt(jnp.mean(raw * raw, axis=-1, keepdims=True) + EPS)
    keys = (raw * scale * gain_ref[...]).astype(BF16)
    values = total[:, head_dim:].astype(BF16)
    for i in range(kv.shape[0]):
        kv[i, :, :head_dim] = keys[i * tokens : (i + 1) * tokens]
        kv[i, :, head_dim:] = values[i * tokens : (i + 1) * tokens]

    def put(d, carry):
        send_ref[d] = kv[jnp.maximum(table_ref[POS, d], 0)]
        return carry

    lax.fori_loop(0, send_ref.shape[0], put, 0, unroll=4)


def project(table, rows, pieces, zones, gain, dp, images, tokens):
    cols = 2 * gain.shape[1]
    return pl.pallas_call(
        functools.partial(project_kernel, zones=zones),
        grid_spec=pltpu.PrefetchScalarGridSpec(
            num_scalar_prefetch=1,
            grid=(),
            in_specs=[in_vmem()] * (2 + len(pieces)),
            out_specs=[in_vmem()] * 2,
            scratch_shapes=[pltpu.VMEM((images, tokens, cols), BF16)],
        ),
        out_shape=[
            pltpu.HBM((dp, tokens, cols), BF16),
            pltpu.HBM((rows.shape[0], cols // 2), F32),
        ],
        compiler_params=limit(14),
        cost_estimate=cost(2 * rows.size * cols, 10),
        name="project",
    )(table, *hold(rows), *pieces, gain)


def load_heads(ref, start, rows, head_dim):
    heads = ref.shape[1] // head_dim
    return jnp.concatenate(
        [ref[pl.ds(start, rows), g * head_dim : (g + 1) * head_dim] for g in range(heads)],
        axis=0,
    )


def store_heads(ref, start, rows, head_dim, full):
    for g in range(ref.shape[1] // head_dim):
        ref[pl.ds(start, rows), g * head_dim : (g + 1) * head_dim] = full[
            g * rows : (g + 1) * rows
        ]


def attend_kernel(table_ref, q_hbm, ct_hbm, kv_ref, part_ref, probs_hbm, ds_hbm, *scratch):
    q_ref, ct_ref, probs_ref, ds_ref, acc, in_sems, out_sems = scratch
    blocks = table_ref.shape[1]
    steps = blocks // GROUP
    text = q_ref.shape[0] // steps

    def moves(step, pairs, size, sems):
        here = pl.ds(pl.multiple_of(step * size, size), size)
        return [
            pltpu.make_async_copy(a.at[here], b.at[here], sems.at[n, step])
            for n, (a, b) in enumerate(pairs)
        ]

    def fetch(step):
        return moves(step, ((q_hbm, q_ref), (ct_hbm, ct_ref)), text, in_sems)

    def stash(step):
        return moves(step, ((probs_ref, probs_hbm), (ds_ref, ds_hbm)), GROUP, out_sems)

    for step in range(steps):
        for copy in fetch(step):
            copy.start()
    rows = q_ref.shape[0] // blocks
    head_dim = kv_ref.shape[2] // 2
    tokens = kv_ref.shape[1]
    scale = head_dim**-0.5
    part_ref[...] = jnp.zeros_like(part_ref)
    acc[...] = jnp.zeros_like(acc)

    def some_blocks(step, carry):
        for copy in fetch(step):
            copy.wait()
        at = [step * GROUP + i for i in range(GROUP)]
        owners = [table_ref[OWNER, b] for b in at]
        starts = [pl.multiple_of(b * rows, rows) for b in at]
        queries = [load_heads(q_ref, s, rows, head_dim) for s in starts]
        grads = [load_heads(ct_ref, s, rows, head_dim) for s in starts]
        scores = [
            dot_dims(kv_ref[o, :, :head_dim], q, 1, 1) * scale for o, q in zip(owners, queries)
        ]
        d_probs = [dot_dims(kv_ref[o, :, head_dim:], g, 1, 1) for o, g in zip(owners, grads)]
        token = lax.broadcasted_iota(jnp.int32, (tokens, 1), 0)
        scores = [
            jnp.where(token < table_ref[VALID, b], s, MASKED_SCORE) for b, s in zip(at, scores)
        ]
        weights = [jnp.exp(s - jnp.max(s, axis=0, keepdims=True)) for s in scores]
        probs = [w * (1.0 / jnp.sum(w, axis=0, keepdims=True)) for w in weights]
        halves = [p.astype(BF16) for p in probs]
        deltas = [jnp.sum(p * d, axis=0, keepdims=True) for p, d in zip(probs, d_probs)]
        d_scores = [
            (p * (d - x) * scale).astype(BF16) for p, d, x in zip(probs, d_probs, deltas)
        ]
        key_parts = [
            jnp.dot(d, q, preferred_element_type=F32) for d, q in zip(d_scores, queries)
        ]
        value_parts = [
            jnp.dot(p, g, preferred_element_type=F32) for p, g in zip(halves, grads)
        ]
        key_run, value_run = acc[:, :head_dim], acc[:, head_dim:]
        for i, b in enumerate(at):
            keep = table_ref[FIRST, b] == 0
            key_run = key_parts[i] + jnp.where(keep, key_run, 0.0)
            value_run = value_parts[i] + jnp.where(keep, value_run, 0.0)
            part_ref[owners[i], :, :head_dim] = key_run.astype(BF16)
            part_ref[owners[i], :, head_dim:] = value_run.astype(BF16)
            probs_ref[b] = halves[i]
            ds_ref[b] = d_scores[i]
        acc[:, :head_dim] = key_run
        acc[:, head_dim:] = value_run
        for copy in stash(step):
            copy.start()
        return carry

    lax.fori_loop(0, steps, some_blocks, 0)
    for step in range(steps):
        for copy in stash(step):
            copy.wait()


def hold(*arrays):
    return [pltpu.with_memory_space_constraint(x, pltpu.HBM) for x in arrays]


def attend(table, queries, cotangent, kv):
    blocks, (_, tokens, cols) = table.shape[1], kv.shape
    rows = queries.size * 2 // (blocks * cols)
    stash = pltpu.HBM((blocks, tokens, rows), BF16)
    return pl.pallas_call(
        attend_kernel,
        grid_spec=pltpu.PrefetchScalarGridSpec(
            num_scalar_prefetch=1,
            grid=(),
            in_specs=[in_hbm()] * 2 + [in_vmem()],
            out_specs=[in_vmem()] + [in_hbm()] * 2,
            scratch_shapes=[pltpu.VMEM(queries.shape, BF16)] * 2
            + [pltpu.VMEM(stash.shape, BF16)] * 2
            + [pltpu.VMEM(kv.shape[1:], F32)]
            + [pltpu.SemaphoreType.DMA((2, blocks // GROUP))] * 2,
        ),
        out_shape=[pltpu.HBM(kv.shape, BF16), stash, stash],
        compiler_params=limit(13),
        cost_estimate=cost(8 * queries.size * tokens, 8),
        name="attend",
    )(table, *hold(queries, cotangent), kv)


def apply_kernel(table_ref, kv_ref, probs_ref, ds_ref, out_ref, gq_ref):
    blocks = table_ref.shape[1]
    rows = out_ref.shape[0] // blocks
    head_dim = kv_ref.shape[2] // 2

    def some_blocks(step, carry):
        at = [step * GROUP + i for i in range(GROUP)]
        owners = [table_ref[OWNER, b] for b in at]
        outs = [
            dot_dims(probs_ref[b], kv_ref[o, :, head_dim:], 0, 0) for b, o in zip(at, owners)
        ]
        gqs = [dot_dims(ds_ref[b], kv_ref[o, :, :head_dim], 0, 0) for b, o in zip(at, owners)]
        for i, b in enumerate(at):
            start = pl.multiple_of(b * rows, rows)
            store_heads(out_ref, start, rows, head_dim, outs[i].astype(BF16))
            store_heads(gq_ref, start, rows, head_dim, gqs[i].astype(BF16))
        return carry

    lax.fori_loop(0, blocks // GROUP, some_blocks, 0)


def apply(table, kv, probs, d_scores, shape):
    out = pltpu.HBM(shape, BF16)
    return pl.pallas_call(
        apply_kernel,
        grid_spec=pltpu.PrefetchScalarGridSpec(
            num_scalar_prefetch=1,
            grid=(),
            in_specs=[in_vmem()] * 3,
            out_specs=[in_vmem()] * 2,
        ),
        out_shape=[out, out],
        compiler_params=limit(9),
        cost_estimate=cost(4 * shape[0] * shape[1] * kv.shape[1], 6),
        name="apply",
    )(table, *hold(kv, probs, d_scores))


def owner_kernel(table_ref, part_hbm, raw_ref, gain_ref, grad_ref, by_core_ref, *scratch):
    acc, part_ref, sems = scratch
    head_dim = gain_ref.shape[1]
    tokens = part_ref.shape[1]
    steps = sems.shape[0]
    count = part_ref.shape[0] // steps
    copies = []
    for step in range(steps):
        here = pl.ds(step * count, count)
        copies.append(
            pltpu.make_async_copy(part_hbm.at[here], part_ref.at[here], sems.at[step])
        )
    for copy in copies:
        copy.start()
    acc[...] = jnp.zeros_like(acc)

    def add(d, carry):
        @pl.when(table_ref[POS, d] >= 0)
        def _():
            acc[table_ref[POS, d]] += part_ref[d].astype(F32)

        return carry

    for step in range(steps):
        copies[step].wait()
        lax.fori_loop(step * count, (step + 1) * count, add, 0)
    gain = gain_ref[...]
    for i in range(acc.shape[0]):
        here = slice(i * tokens, (i + 1) * tokens)
        raw = raw_ref[here]
        scale = lax.rsqrt(jnp.mean(raw * raw, axis=-1, keepdims=True) + EPS)
        scaled = acc[i, :, :head_dim] * gain
        pull = jnp.mean(raw * scaled, axis=-1, keepdims=True)
        grad = scale * scaled - raw * (scale * scale * scale * pull)
        grad_ref[here, :head_dim] = grad.astype(BF16)
        grad_ref[here, head_dim:] = acc[i, :, head_dim:].astype(BF16)
    for i in range(acc.shape[0]):
        at = pl.multiple_of(lax.rem(table_ref[PLACE, 3] + i, 2) * tokens, tokens)
        by_core_ref[i * tokens : (i + 1) * tokens, :] = grad_ref[pl.ds(at, tokens), :]


def owner_grads(table, parts, raw, gain, images):
    tokens, cols = parts.shape[1:]
    grads = jax.ShapeDtypeStruct((images * tokens, cols), BF16)
    return pl.pallas_call(
        owner_kernel,
        grid_spec=pltpu.PrefetchScalarGridSpec(
            num_scalar_prefetch=1,
            grid=(),
            in_specs=[in_hbm()] + [in_vmem()] * 2,
            out_specs=[in_vmem()] * 2,
            scratch_shapes=[
                pltpu.VMEM((images, tokens, cols), F32),
                pltpu.VMEM(parts.shape, BF16),
                pltpu.SemaphoreType.DMA((4,)),
            ],
        ),
        out_shape=[grads, grads],
        compiler_params=limit(6),
        cost_estimate=cost(0, 3),
        name="owner_grads",
    )(table, *hold(parts, raw), gain)


def transpose_kernel(*refs):
    pieces, out_ref = refs[:-1], refs[-1]
    tokens = pieces[0].shape[0]
    for i, ref in enumerate(pieces):
        out_ref[:, i * tokens : (i + 1) * tokens] = ref[...].T


def transpose_pieces(pieces):
    tokens, width = pieces[0].shape
    return pl.pallas_call(
        transpose_kernel,
        in_specs=[in_vmem()] * len(pieces),
        out_specs=in_vmem(),
        out_shape=jax.ShapeDtypeStruct((width, tokens * len(pieces)), BF16),
        compiler_params=limit(7),
        cost_estimate=cost(0, 4),
        name="transpose_pieces",
    )(*hold(*pieces))


def weight_kernel(own_ref, other_ref, *refs):
    lines, out_ref = refs[:-1], refs[-1]
    half = lines[0].shape[0] // 2
    first = jnp.concatenate([ref[:half, :] for ref in lines], axis=0)
    second = jnp.concatenate([ref[half:, :] for ref in lines], axis=0)
    block = out_ref.shape[1]
    for i in range(out_ref.shape[0]):
        here = slice(i * block, (i + 1) * block)
        total = jnp.dot(own_ref[here, :], first, preferred_element_type=F32)
        total = total + jnp.dot(other_ref[here, :], second, preferred_element_type=F32)
        out_ref[i] = total.astype(BF16)


def weight_terms(own_cols, other_cols, lines):
    width, cols = own_cols.shape[0], lines[0].shape[1]
    return pl.pallas_call(
        weight_kernel,
        in_specs=[in_vmem()] * (2 + len(lines)),
        out_specs=in_vmem(),
        out_shape=pltpu.HBM((NZ, width // NZ, cols), BF16),
        compiler_params=limit(9),
        cost_estimate=cost(4 * own_cols.size * cols, 6),
        name="weight_terms",
    )(own_cols, other_cols, *lines)


def assemble_kernel(table_ref, *refs, zones):
    w_refs, out_refs = refs[:-2], refs[-2:]
    for here, spot, _, _ in weight_blocks(table_ref, w_refs, zones):
        for out_ref, (ref, rows) in zip(out_refs, spot):
            out_ref[here, :] = ref[rows, :]


def assemble(table, pieces, zones, width, head_dim):
    return pl.pallas_call(
        functools.partial(assemble_kernel, zones=zones),
        grid_spec=pltpu.PrefetchScalarGridSpec(
            num_scalar_prefetch=1,
            grid=(),
            in_specs=[in_vmem()] * len(pieces),
            out_specs=[in_vmem()] * 2,
        ),
        out_shape=[pltpu.HBM((width, head_dim), BF16)] * 2,
        compiler_params=limit(10),
        cost_estimate=cost(0, 1),
        name="assemble",
    )(table, *pieces)


def feature_kernel(table_ref, own_ref, other_ref, *refs, targets):
    w_refs, out_refs, (lhs, held, sems) = refs[:4], refs[4:-3], refs[-3:]
    chips = len(out_refs)
    tokens, head_dim = own_ref.shape[0] // 2, own_ref.shape[1] // 2
    share = tokens // targets
    steps, block = held.shape[1:3]
    copies = [
        [
            pltpu.make_async_copy(
                w_ref.at[pl.ds(step * block, block), :], held.at[n, step], sems.at[n, step]
            )
            for n, w_ref in enumerate(w_refs)
        ]
        for step in range(steps)
    ]
    for step in range(steps):
        for copy in copies[step]:
            copy.start()
    for core, ref in enumerate((own_ref, other_ref)):
        for chip in range(chips):
            target = lax.rem(table_ref[PLACE, 2] + chip, chips) * 2 + table_ref[PLACE, 3]
            for i in range(2):
                at = pl.multiple_of(i * tokens + target * share, share)
                to = (chip * 2 + i) * share
                for n in range(2):
                    lhs[core, n, to : to + share, :] = ref[
                        pl.ds(at, share), n * head_dim : (n + 1) * head_dim
                    ]
    for step in range(steps):
        part = 0.0
        for core in range(2):
            for n in range(2):
                copies[step][2 * core + n].wait()
            left = jnp.concatenate([lhs[core, 0], lhs[core, 1]], axis=1)
            right = jnp.concatenate([held[2 * core, step], held[2 * core + 1, step]], axis=1)
            part = part + dot_dims(left, right, 1, 1)
        for chip, ref in enumerate(out_refs):
            ref[:, step * block : (step + 1) * block] = part[
                chip * 2 * share : (chip + 1) * 2 * share
            ].astype(BF16)


def feature_terms(table, own, other, weights, targets):
    width, head_dim = weights[0].shape
    chips, steps = targets // 2, 8
    rows = own.shape[0] // targets
    return pl.pallas_call(
        functools.partial(feature_kernel, targets=targets),
        grid_spec=pltpu.PrefetchScalarGridSpec(
            num_scalar_prefetch=1,
            grid=(),
            in_specs=[in_vmem()] * 2 + [in_hbm()] * 4,
            out_specs=[in_vmem()] * chips,
            scratch_shapes=[
                pltpu.VMEM((2, 2, own.shape[0] // 2, head_dim), BF16),
                pltpu.VMEM((4, steps, width // steps, head_dim), BF16),
                pltpu.SemaphoreType.DMA((4, steps)),
            ],
        ),
        out_shape=[jax.ShapeDtypeStruct((rows, width), BF16)] * chips,
        compiler_params=limit(14),
        cost_estimate=cost(4 * own.size * width, 10),
        name="feature_terms",
    )(table, own, other, *hold(*weights))


def finish_kernel(share_ref, *refs):
    terms, (features_ref, key_ref, value_ref) = refs[:-3], refs[-3:]
    head_dim = key_ref.shape[1]
    total = share_ref[0].astype(F32)
    for i in range(1, share_ref.shape[0]):
        total = total + share_ref[i].astype(F32)
    key_ref[...] = total[:, :head_dim]
    value_ref[...] = total[:, head_dim:]
    block = features_ref.shape[1] // NZ
    for i in range(NZ):
        here = slice(i * block, (i + 1) * block)
        total = terms[0][:, here].astype(F32)
        for term in terms[1:]:
            total = total + term[:, here].astype(F32)
        features_ref[:, here] = total.astype(BF16)


def finish(shares, terms):
    rows, cols = shares.shape[1:]
    weights = pltpu.HBM((rows, cols // 2), F32)
    return pl.pallas_call(
        finish_kernel,
        in_specs=[in_vmem()] * (1 + len(terms)),
        out_specs=[in_vmem()] * 3,
        out_shape=[pltpu.HBM(terms[0].shape, BF16), weights, weights],
        compiler_params=limit(6),
        cost_estimate=cost(0, 3),
        name="finish",
    )(shares, *terms)


def shift_y(x, by):
    if by == 0:
        return x
    pairs = [(y * NZ + z, (y + by) % NY * NZ + z) for y in range(NY) for z in range(NZ)]
    return lax.ppermute(x, "dp", pairs)


def shift_z(x, by):
    pairs = [(y * NZ + z, y * NZ + (z + by) % NZ) for y in range(NY) for z in range(NZ)]
    return lax.ppermute(x, "dp", pairs)


def swap_cores(x, count):
    return lax.ppermute(x, "tensor", [(t, t ^ 1) for t in range(count)])


def local(
    queries, features, k_weight, v_weight, k_gain, block_image, image_slot, image_tiles, cotangent
):
    dp_count = lax.axis_size("dp")
    tensor_count = lax.axis_size("tensor")
    me = lax.axis_index("dp")
    images, tokens, width = features.shape
    head_dim = k_gain.shape[0]
    rows = features.reshape(images * tokens, width)
    gain = k_gain.reshape(1, head_dim)
    my_y, my_z = me // NZ, lax.rem(me, NZ)
    tensor = lax.axis_index("tensor")
    core = lax.rem(tensor, 2)

    image_ids = lax.broadcasted_iota(jnp.int32, (1, image_slot.shape[0]), 1)
    id_match = block_image[:, None] == image_ids
    slots = jnp.sum(jnp.where(id_match, image_slot[None, :], 0), axis=1).reshape(dp_count, -1)
    tiles = jnp.sum(jnp.where(id_match, image_tiles[None, :], 0), axis=1).reshape(dp_count, -1)
    my_slots = lax.dynamic_index_in_dim(slots, me, 0, keepdims=False)
    my_tiles = lax.dynamic_index_in_dim(tiles, me, 0, keepdims=False)
    first = jnp.concatenate(
        [jnp.ones((1,), jnp.int32), (my_slots[1:] != my_slots[:-1]).astype(jnp.int32)]
    )
    pos = jnp.max(jnp.where(slots // images == me, slots % images, -1), axis=1)
    place = jnp.stack([my_y, my_z, tensor // 2, core])
    place = jnp.pad(place, (0, pos.shape[0] - place.shape[0]))
    table = jnp.stack([pos, my_slots // images, my_tiles * (tokens // TILES), first, place])

    v_line = jnp.concatenate([shift_y(v_weight, (NY - i) % NY) for i in range(NY)])
    k_ring, v_ring = [k_weight], [v_line]
    for hop in range(1, NZ // 2):
        k_ring += [shift_z(k_ring[max(-2, -len(k_ring))], 1), shift_z(k_ring[-1], -1)]
        if hop == 1:
            v_ring += [shift_z(v_line, 1), shift_z(v_line, -1)]
        if hop == 2:
            k_ring[-2], k_ring[-1], v_ring[-2], v_ring[-1] = lax.optimization_barrier(
                (k_ring[-2], k_ring[-1], v_ring[-2], v_ring[-1])
            )
    for hop in range(2, NZ // 2):
        v_ring += [shift_z(v_ring[-2], 1), shift_z(v_ring[-1], -1)]
    k_ring += [shift_z(k_ring[-2], 1)]
    v_ring += [shift_z(v_ring[-2], 1)]
    offsets = [0] + [z for hop in range(1, NZ // 2) for z in (NZ - hop, hop)] + [NZ // 2]
    v_zones = [[(y, z) for y in range(NY)] for z in offsets]
    k_pieces, k_zones = [], []
    for part in (slice(0, NZ // 2), slice(NZ // 2, NZ)):
        k_line = jnp.concatenate(k_ring[part])
        after, before = shift_y(k_line, -1), shift_y(k_line, 1)
        far = shift_y(before, 1) if part.start else shift_y(after, -1)
        k_pieces += [k_line, after, before, far]
        k_zones += [[(y, z) for z in offsets[part]] for y in (0, 1, NY - 1, NY // 2)]
    pieces, zones = k_pieces + v_ring, k_zones + v_zones

    send, raw = project(
        table, rows, pieces, zones, gain, dp_count, images, tokens
    )
    kv = lax.all_to_all(send, "dp", 0, 0, tiled=True)

    rows_later, _ = lax.optimization_barrier((features, raw))
    span = width // NY
    col_pieces = [
        shift_y(
            lax.dynamic_slice(
                rows_later, (core, 0, (my_y + s) % NY * span), (1, tokens, span)
            )[0],
            s,
        )
        for s in range(NY)
    ]

    parts, probs, d_scores = attend(table, queries, cotangent, kv)
    parts, col_pieces, pieces = lax.optimization_barrier((parts, col_pieces, pieces))
    parts = lax.all_to_all(parts, "dp", 0, 0, tiled=True)
    own_cols = transpose_pieces(col_pieces)
    other_cols = swap_cores(own_cols, tensor_count)
    weights = list(assemble(table, pieces, zones, width, head_dim))
    weights += [swap_cores(w, tensor_count) for w in weights]
    attended, grad_queries = apply(table, kv, probs, d_scores, queries.shape)
    parts, other_cols, attended, grad_queries, weights = lax.optimization_barrier(
        (parts, other_cols, attended, grad_queries, weights)
    )
    grads, by_core = owner_grads(table, parts, raw, gain, images)

    lines = [shift_y(by_core, s) for s in range(NY)]
    shares = weight_terms(own_cols, other_cols, lines)
    other_grads = swap_cores(grads, tensor_count)
    shares, grads, other_grads = lax.optimization_barrier((shares, grads, other_grads))
    shares = lax.all_to_all(shares, "dp", 0, 0, tiled=True, axis_index_groups=Z_GROUPS)

    terms = list(feature_terms(table, grads, other_grads, weights, tensor_count))
    for s in range(1, tensor_count // 2):
        pairs = [(t, (t + 2 * s) % tensor_count) for t in range(tensor_count)]
        terms[s] = lax.ppermute(terms[s], "tensor", pairs)
    grad_features, grad_k, grad_v = finish(shares, terms)
    grad_features = grad_features.reshape(images, tokens // tensor_count, width)
    return attended, grad_queries, grad_features, grad_k, grad_v


def solution(mesh):
    in_specs = (
        P("dp", "tensor"),
        P("dp", None, None),
        P("dp", "tensor"),
        P("dp", "tensor"),
        P(),
        P(),
        P(),
        P(),
        P("dp", "tensor"),
    )
    out_specs = (
        P("dp", "tensor"),
        P("dp", "tensor"),
        P("dp", "tensor", None),
        P("dp", "tensor"),
        P("dp", "tensor"),
    )
    return jax.shard_map(local, mesh=mesh, in_specs=in_specs, out_specs=out_specs, check_vma=False)
```
